128 devices in a mesh: section: 8 (over x_hi, z), dp: 16 (over y, x_lo, core).
Axes of the slice: x: 4 (x_hi: 2, x_lo: 2; x = x_hi * 2 + x_lo), y: 4, z: 4, core: 2. Of those that a mesh axis runs over, the one named last changes fastest.
Arguments:
- hidden_states: bfloat16 [8, 2, 2048, 8192], P('section', None, 'dp'), may hold values from -12 to 12
- key_rows: bfloat16 [8, 2, 2048, 4096], P('section', None, 'dp'), may hold values from -27 to 27
- value_rows: bfloat16 [8, 2, 2048, 4096], P('section', None, 'dp'), may hold values from -6 to 6
- latents: bfloat16 [2, 2048, 768], P(None, 'dp'), may hold values from -6 to 6
- next_latents: bfloat16 [2048, 768], P('dp'), may hold values from -6 to 6
- media_index: int32 [2, 2048], P(None, 'dp'), may hold values from 0 to 1
- cotangent: bfloat16 [2, 2048, 8192], P(None, 'dp'), may hold values from -6 to 6
- gate_alpha: float32 [8], P('section'), may hold values from 0.3 to 1.2
- weights: float32 [8, 2, 768, 4096], P('section', None, None, 'dp'), may hold values from -0.21875 to 0.21875
- moment_first: float32 [8, 2, 768, 4096], P('section', None, None, 'dp'), may hold values from -4 to 4
- moment_second: float32 [8, 2, 768, 4096], P('section', None, None, 'dp'), may hold values from 0.1 to 10
Outputs:
- input_grads: bfloat16 [8, 2, 2048, 8192], P('section', None, 'dp')
- new_weights: float32 [8, 2, 768, 4096], P('section', None, None, 'dp')
- next_keyvals: bfloat16 [8, 2, 2048, 4096], P('section', None, 'dp')
The draws below stay inside these ranges and needn't reach their ends.
Inputs may be any that keep to these rules, and one draw needn't show every extreme that they name: `media_index`: each token attends to one of the 2 media items held with its own block of 128 tokens.
All inputs are finite; a program needn't handle non-finite values.
Results may differ from the reference program's by a relative error of at most 0.0085.
Values may be sent and summed in bfloat16 or wider, within the bound.
A program may use at most 192 MiB of HBM per device.

```python
import math
import jax
import jax.numpy as jnp
from jax import lax

D = 8192
HEADS = 32
HEAD_DIM = 128
LATENTS = 64
LAT_D = 768
MICRO = 2
TOK_DEV = 128
MEDIA_DEV = 2
QK_WIDTH = 4096
LAT_ROWS = 128
TOKENS = 2048
MEDIA_ROWS = 2048
SECTIONS = 8


def draw_hidden_states(key, part):
    key = jax.random.fold_in(key, 11)
    base_key, scale_key = jax.random.split(key)
    shape = (SECTIONS, MICRO, TOKENS, D)
    row_scale = jnp.exp(jax.random.uniform(scale_key, (SECTIONS, MICRO, TOKENS, 1), jnp.float32, math.log(0.2), math.log(2.0)))
    result = jnp.clip(jax.random.normal(base_key, shape, jnp.float32), -6.0, 6.0) * row_scale
    return result.astype(jnp.bfloat16)


def draw_key_rows(key, part):
    key = jax.random.fold_in(key, 23)
    shape = (SECTIONS, MICRO, MEDIA_ROWS, QK_WIDTH)
    result = jnp.clip(jax.random.normal(key, shape, jnp.float32), -6.0, 6.0)
    return result.astype(jnp.bfloat16)


def with_ends(entries, own_key, low, largest):
    shape = entries.shape
    spot = [jax.random.randint(jax.random.fold_in(own_key, axis), (), 0, shape[axis]) for axis in range(len(shape))]
    entries = entries.at[tuple(spot)].set(low)
    longest = shape.index(max(shape))
    spot[longest] = (spot[longest] + 1) % shape[longest]
    return entries.at[tuple(spot)].set(largest)


def shard_levels(stream_key, shape, cuts, least, top_value):
    gain, own = 1.0, jax.random.fold_in(stream_key, 6)
    for axis_at, blocks in cuts:
        heights = jnp.exp(jax.random.uniform(jax.random.fold_in(own, axis_at), (blocks,), jnp.float32, least / len(cuts), top_value / len(cuts)))
        gain = gain * jnp.repeat(heights, shape[axis_at] // blocks).reshape([-1 if axis == axis_at else 1 for axis in range(len(shape))])
    return gain


def normal_values(key, dims, deviation, bound, cuts=(), dtype=jnp.bfloat16):
    values = jax.random.normal(key, dims, jnp.float32) * deviation
    if len(cuts) > 0:
        values = shard_levels(key, dims, cuts, -0.22, 0.18) * values
    return jnp.clip(values, min=-bound, max=bound).astype(dtype)


def setup_inputs(seed: int = 0) -> dict:
    key_list = jax.random.split(jax.random.key(seed), 12)
    hidden_states = draw_hidden_states(jax.random.fold_in(key_list[11], 71), 0)
    key_rows = draw_key_rows(jax.random.fold_in(key_list[11], 71), 0)
    value_rows = normal_values(key_list[2], (SECTIONS, MICRO, MEDIA_ROWS, QK_WIDTH), 1.0, 6.0, ((0, 8), (2, 16)))
    latents = normal_values(key_list[3], (MICRO, MEDIA_ROWS, LAT_D), 1.0, 6.0, ((1, 16),))
    next_latents = normal_values(key_list[4], (MEDIA_ROWS, LAT_D), 1.0, 6.0, ((0, 16),))
    media_index = with_ends(jax.random.randint(key_list[5], (MICRO, TOKENS), 0, MEDIA_DEV), jax.random.fold_in(key_list[5], 1), 0, MEDIA_DEV - 1).astype(jnp.int32)
    cotangent = normal_values(key_list[6], (MICRO, TOKENS, D), 1.0, 6.0, ((1, 16),))
    gate_alpha = jnp.clip(0.3 + 0.90000004 * jax.random.uniform(key_list[7], (SECTIONS,), jnp.float32) ** shard_levels(key_list[7], (SECTIONS,), ((0, 8),), -0.2, 0.2), 0.3, 1.2)
    weights = normal_values(key_list[8], (SECTIONS, 2, LAT_D, QK_WIDTH), LAT_D ** -0.5, 0.21875, ((0, 8), (3, 16)), jnp.float32)
    moment_first = normal_values(key_list[9], (SECTIONS, 2, LAT_D, QK_WIDTH), 0.3, 4.0, ((0, 8), (3, 16)), jnp.float32)
    moment_second = jnp.clip(jnp.exp(math.log(10.0) - 4.6051702 * jax.random.uniform(key_list[10], (SECTIONS, 2, LAT_D, QK_WIDTH), jnp.float32) ** shard_levels(key_list[10], (SECTIONS, 2, LAT_D, QK_WIDTH), ((0, 8), (3, 16)), -0.2, 0.2)), 0.1, 10.0)
    return dict(hidden_states=hidden_states, key_rows=key_rows, value_rows=value_rows, latents=latents, next_latents=next_latents, media_index=media_index, cotangent=cotangent, gate_alpha=gate_alpha, weights=weights, moment_first=moment_first, moment_second=moment_second)


def attend_back(states, media_ids, upstream, key_block, value_block, gate_tanh):
    count = states.shape[0]
    rows_here = key_block.shape[0]
    span = key_block.shape[1]
    width = states.shape[1]
    scale = 1.0 / math.sqrt(HEAD_DIM)
    floats = states.astype(jnp.float32)
    root_mean = jnp.sqrt(lax.optimization_barrier(jnp.mean(floats * floats, axis=1, keepdims=True)) + 1e-06)
    normed = floats / root_mean
    query = normed[:, :span].astype(jnp.bfloat16).reshape(count, HEADS, HEAD_DIM).astype(jnp.float32)
    key_heads = key_block.reshape(rows_here, HEADS, HEAD_DIM).astype(jnp.float32)
    value_heads = value_block.reshape(rows_here, HEADS, HEAD_DIM).astype(jnp.float32)
    scores = jnp.einsum('thd,rhd->htr', query, key_heads) * scale
    allowed = (jnp.arange(rows_here) // LATENTS)[None, :] == media_ids[:, None]
    scores = jnp.where(allowed[None], scores, -1e+30)
    peak = lax.optimization_barrier(jnp.max(scores, axis=2, keepdims=True))
    raised = jnp.exp(scores - peak)
    probs = raised / lax.optimization_barrier(jnp.sum(raised, axis=2, keepdims=True))
    probs_low = probs.astype(jnp.bfloat16).astype(jnp.float32)
    grad_out = (gate_tanh * upstream[:, :span].astype(jnp.float32)).astype(jnp.bfloat16)
    grad_out = grad_out.reshape(count, HEADS, HEAD_DIM).astype(jnp.float32)
    grad_probs = jnp.einsum('thd,rhd->htr', grad_out, value_heads)
    weighted = lax.optimization_barrier(jnp.sum(probs * grad_probs, axis=2, keepdims=True))
    grad_scores = (probs * (grad_probs - weighted)).astype(jnp.bfloat16).astype(jnp.float32)
    grad_query = jnp.einsum('htr,rhd->thd', grad_scores, key_heads) * scale
    grad_keys = (jnp.einsum('htr,thd->rhd', grad_scores, query) * scale).astype(jnp.bfloat16)
    grad_values = jnp.einsum('htr,thd->rhd', probs_low, grad_out).astype(jnp.bfloat16)
    grad_normed = jnp.pad(grad_query.reshape(count, span), ((0, 0), (0, width - span)))
    inner = lax.optimization_barrier(jnp.mean(grad_normed * normed, axis=1, keepdims=True))
    grad_input = upstream.astype(jnp.float32) + (grad_normed - normed * inner) / root_mean
    return (grad_input.astype(jnp.bfloat16), grad_keys.reshape(rows_here, span), grad_values.reshape(rows_here, span))

def block_term(total, pieces):
    lat_block, key_block, value_block = pieces
    lat_float = lat_block.astype(jnp.float32)
    term_keys = jnp.einsum('mrl,mrc->lc', lat_float, key_block.astype(jnp.float32))
    term_values = jnp.einsum('mrl,mrc->lc', lat_float, value_block.astype(jnp.float32))
    rounded = lax.optimization_barrier(jnp.stack([term_keys, term_values]).astype(jnp.bfloat16))
    return (total + rounded.astype(jnp.float32), None)

def reference(hidden_states, key_rows, value_rows, latents, next_latents, media_index, cotangent, gate_alpha, weights, moment_first, moment_second):
    blocks = TOKENS // TOK_DEV
    upstream = [cotangent[index] for index in range(MICRO)]
    grads_out = [None] * SECTIONS
    weights_out = [None] * SECTIONS
    keyvals_out = [None] * SECTIONS
    lat_blocks = latents.reshape(MICRO, blocks, LAT_ROWS, LAT_D).transpose(1, 0, 2, 3)
    for section in range(SECTIONS - 1, -1, -1):
        gate_tanh = jnp.tanh(gate_alpha[section])
        produced = []
        key_grads = []
        value_grads = []
        for index in range(MICRO):
            pieces = (hidden_states[section, index].reshape(blocks, TOK_DEV, D), media_index[index].reshape(blocks, TOK_DEV), upstream[index].reshape(blocks, TOK_DEV, D), key_rows[section, index].reshape(blocks, LAT_ROWS, QK_WIDTH), value_rows[section, index].reshape(blocks, LAT_ROWS, QK_WIDTH))
            grad_x, grad_k, grad_v = lax.map(lambda item: attend_back(item[0], item[1], item[2], item[3], item[4], gate_tanh), pieces)
            produced.append(grad_x.reshape(TOKENS, D))
            key_grads.append(grad_k)
            value_grads.append(grad_v)
        upstream = produced
        grads_out[section] = jnp.stack(produced)
        key_stack = jnp.stack(key_grads, axis=1)
        value_stack = jnp.stack(value_grads, axis=1)
        grads, unused = lax.scan(block_term, jnp.zeros((2, LAT_D, QK_WIDTH), jnp.float32), (lat_blocks, key_stack, value_stack))
        first = 0.9 * moment_first[section] + 0.1 * grads
        second = 0.95 * moment_second[section] + 0.05 * grads * grads
        updated = weights[section] - 0.02 * (first / (jnp.sqrt(second) + 1e-08) + 0.1 * weights[section])
        weights_out[section] = updated
        weights_low = updated.astype(jnp.bfloat16)
        keyvals_out[section] = jnp.stack([jnp.dot(next_latents, weights_low[pick], preferred_element_type=jnp.float32).astype(jnp.bfloat16) for pick in range(2)])
    return (jnp.stack(grads_out), jnp.stack(weights_out), jnp.stack(keyvals_out))
```

```python
import functools
import math

import jax
import jax.numpy as jnp
from jax import lax
from jax.experimental import pallas as pl
from jax.experimental.pallas import tpu as pltpu
from jax.sharding import PartitionSpec as P

HEAD_DIM = 128
LATENTS = 64
CHUNK = 16
CHUNK2 = 32
NORM_ROWS = 16
ADAM_ROWS = 64
F32 = jnp.float32
BF16 = jnp.bfloat16
MESH = pl.DeviceIdType.MESH


def dot_nt(a, b):
    return lax.dot_general(a, b, (((1,), (1,)), ((), ())), preferred_element_type=F32)


def dot_tn(a, b):
    return lax.dot_general(a, b, (((0,), (0,)), ((), ())), preferred_element_type=F32)


def dot_nn(a, b):
    return jnp.dot(a, b, preferred_element_type=F32)


def kernel(
    n_sec, n_dp,
    hid_hbm, key_hbm, val_hbm, lat_hbm, nl_hbm, media_ref, cot_hbm, gate_ref, w_hbm, mf_hbm, ms_hbm,
    ig_hbm, nw_hbm, kv_hbm,
    hid, keys, vals, lat, inc, inc2, q, p, go, gs, gbuf, rinv, coef, maskf,
    lt_all, nl_all, snd, rcv, wts, mf, ms, grads, wlow, kvs,
    in_sem, out_sem, r1_send, r1_recv, r2_send, r2_recv,
    gat_send, gat_recv, a2a_send, a2a_recv, kv_send, kv_recv, loc_sem,
):
    sec, me = lax.axis_index("section"), lax.axis_index("dp")
    micro, block, width = hid_hbm.shape
    span = key_hbm.shape[2]
    rows_m = key_hbm.shape[1]
    lat_w = lat_hbm.shape[2]
    cols_d = w_hbm.shape[2]
    heads = span // HEAD_DIM
    heads_d = cols_d // HEAD_DIM
    tokens = micro * block
    n_chunks = tokens // CHUNK
    per_micro = n_chunks // micro
    n_chunks2 = tokens // CHUNK2
    n_y = n_dp // 4
    scale = 1.0 / math.sqrt(HEAD_DIM)
    core = lax.rem(me, 2)
    x_lo = lax.rem(me // 2, 2)
    y_at = me // 4
    top = sec == n_sec - 1
    early = sec < n_sec // 2

    def dp_dev(j):
        return (sec, j)

    barrier = pltpu.get_barrier_semaphore()

    @pl.loop(1, n_dp)
    def _(k):
        pl.semaphore_signal(barrier, inc=1, device_id=dp_dev(lax.rem(me + k, n_dp)), device_id_type=MESH)

    @pl.when(sec > 0)
    def _():
        pl.semaphore_signal(barrier, inc=1, device_id=(sec - 1, me), device_id_type=MESH)

    @pl.when(sec < n_sec - 1)
    def _():
        pl.semaphore_signal(barrier, inc=1, device_id=(sec + 1, me), device_id_type=MESH)

    def load(i, src, dst):
        return pltpu.make_async_copy(src, dst, in_sem.at[i])

    hid_loads = [load(m, hid_hbm.at[m], hid.at[pl.ds(m * block, block), :]) for m in range(micro)]
    key_loads = [load(2 + m, key_hbm.at[m], keys.at[m]) for m in range(micro)]
    val_loads = [load(4 + m, val_hbm.at[m], vals.at[m]) for m in range(micro)]
    lat_load = load(6, lat_hbm, lat)
    nl_load = load(7, nl_hbm, nl_all.at[pl.ds(me * block, block), :])
    w_load, mf_load, ms_load = load(8, w_hbm, wts), load(9, mf_hbm, mf), load(10, ms_hbm, ms)
    cot_loads = [load(11 + m, cot_hbm.at[m, :, pl.ds(0, span)], inc.at[pl.ds(m * block, block), :]) for m in range(micro)]
    cot2_loads = [
        load(13 + m, cot_hbm.at[m, :, pl.ds(span, width - span)], inc2.at[pl.ds(m * block, block), :])
        for m in range(micro)
    ]
    lat_load.start()
    nl_load.start()
    hid_loads[0].start()
    key_loads[0].start()

    @pl.when(top)
    def _():
        for c in cot_loads:
            c.start()

    val_loads[0].start()
    for c in (hid_loads[1], key_loads[1], val_loads[1], w_load, mf_load, ms_load):
        c.start()

    @pl.when(top)
    def _():
        for c in cot2_loads:
            c.start()

    for m in range(micro):
        row = media_ref[pl.ds(m, 1), :].astype(F32)
        maskf[m] = jnp.transpose(jnp.broadcast_to(row, (block, block)))
    lat_load.wait()
    nl_load.wait()
    my_rows = pl.ds(pl.multiple_of(me * rows_m, rows_m), rows_m)
    for m in range(micro):
        lt_all[m, :, my_rows] = jnp.transpose(lat[m].astype(F32)).astype(BF16)

    others = jnp.where(sec > 0, 1, 0) + jnp.where(sec < n_sec - 1, 1, 0) + n_dp - 1
    pl.semaphore_wait(barrier, others)

    def gather_copy(slot, owner, target):
        at = pl.ds(pl.multiple_of(owner * rows_m, rows_m), rows_m)
        ref_l = lt_all.at[:, :, at]
        ref_n = nl_all.at[at, :]
        return [
            pltpu.make_async_remote_copy(
                src_ref=ref, dst_ref=ref, send_sem=gat_send.at[i, slot], recv_sem=gat_recv.at[i, owner],
                device_id=dp_dev(target), device_id_type=MESH,
            )
            for i, ref in enumerate((ref_l, ref_n))
        ]

    def gather_start(slot, owner, target):
        for c in gather_copy(slot, owner, target):
            c.start()

    def gather_wait_recv(owner):
        for c in gather_copy(0, owner, me):
            c.wait_recv()

    def gather_wait_send(slot):
        for c in gather_copy(slot, me, me):
            c.wait_send()

    x_peer = me + 2 - 4 * x_lo
    core_peer = me + 1 - 2 * core

    def y_peer(dy):
        return lax.rem(y_at + dy, n_y) * 4 + x_lo * 2 + core

    gather_start(0, me, x_peer)
    for dy in range(1, n_y):
        gather_start(dy, me, y_peer(dy))

    def gather_second():
        gather_wait_recv(x_peer)
        for dy in range(1, n_y):
            gather_start(n_y - 1 + dy, x_peer, y_peer(dy))

    def gather_third():
        for dy in range(1, n_y):
            gather_wait_recv(y_peer(dy))
            gather_wait_recv(y_peer(dy) + 2 - 4 * x_lo)

        @pl.loop(0, n_dp // 2)
        def _(k):
            gather_start(2 * n_y - 1 + k, 2 * k + core, core_peer)

    def prepare(m):
        base = m * block

        @pl.loop(0, block // NORM_ROWS)
        def _(t):
            rows = pl.ds(pl.multiple_of(base + t * NORM_ROWS, NORM_ROWS), NORM_ROWS)
            total = jnp.zeros((NORM_ROWS, 128), F32)
            for c in range(width // 128):
                h = hid[rows, pl.ds(c * 128, 128)].astype(F32)
                total = total + h * h
            mean = jnp.sum(total, axis=1, keepdims=True) * (1.0 / width)
            r = jnp.broadcast_to(1.0 / jnp.sqrt(mean + 1e-06), (NORM_ROWS, 128))
            rinv[rows, :] = r
            for c in range(heads):
                cols = pl.ds(c * 128, 128)
                q[rows, cols] = (hid[rows, cols].astype(F32) * r).astype(BF16)

        rows = pl.ds(pl.multiple_of(base, block), block)
        half = lax.broadcasted_iota(jnp.int32, (block, rows_m), 1) // LATENTS
        allowed = half.astype(F32) == maskf[m]
        group = 4

        @pl.loop(0, heads // group)
        def _(hg):
            for j in range(group):
                cols = pl.ds(pl.multiple_of((hg * group + j) * 128, 128), 128)
                s = dot_nt(q[rows, cols], keys[m, :, cols]) * scale
                s = jnp.where(allowed, s, -1e30)
                e = jnp.exp(s - jnp.max(s, axis=1, keepdims=True))
                p[rows, cols] = e / jnp.sum(e, axis=1, keepdims=True)

    def relay1(c):
        rows = pl.ds(pl.multiple_of(c * CHUNK, CHUNK), CHUNK)
        return pltpu.make_async_remote_copy(
            src_ref=inc.at[rows, :], dst_ref=inc.at[rows, :], send_sem=r1_send.at[c], recv_sem=r1_recv.at[c],
            device_id=(jnp.maximum(sec - 1, 0), me), device_id_type=MESH,
        )

    def relay2(c):
        rows = pl.ds(pl.multiple_of(c * CHUNK2, CHUNK2), CHUNK2)
        return pltpu.make_async_remote_copy(
            src_ref=inc2.at[rows, :], dst_ref=inc2.at[rows, :], send_sem=r2_send.at[c], recv_sem=r2_recv.at[c],
            device_id=(jnp.maximum(sec - 1, 0), me), device_id_type=MESH,
        )

    gate_tanh = jnp.tanh(jnp.broadcast_to(gate_ref[...], (CHUNK, 128)))

    def chain_step(c):
        m = c // per_micro
        rows = pl.ds(pl.multiple_of(c * CHUNK, CHUNK), CHUNK)
        acc = jnp.zeros((CHUNK, 128), F32)
        for h in range(heads):
            cols = pl.ds(h * 128, 128)
            g = (gate_tanh * inc[rows, cols].astype(F32)).astype(BF16)
            go[rows, cols] = g
            gp = dot_nt(g, vals[m, :, cols])
            pr = p[rows, cols]
            weighted = jnp.sum(pr * gp, axis=1, keepdims=True)
            gsc = (pr * (gp - weighted)).astype(BF16)
            gs[rows, cols] = gsc
            gk = dot_nn(gsc, keys[m, :, cols])
            gbuf[:, cols] = gk
            acc = acc + gk * hid[rows, cols].astype(F32)
        r = rinv[rows, :]
        dots = jnp.sum(acc, axis=1, keepdims=True)
        a = r * scale
        b = r * r * r * (dots * (scale / width))
        coef[rows, :] = b
        for h in range(heads):
            cols = pl.ds(h * 128, 128)
            new = inc[rows, cols].astype(F32) + (a * gbuf[:, cols] - b * hid[rows, cols].astype(F32))
            inc[rows, cols] = new.astype(BF16)

    def second_step(c):
        @pl.when(jnp.logical_not(top))
        def _():
            relay2(c).wait_recv()

        for t in range(CHUNK2 // 16):
            rows = pl.ds(pl.multiple_of(c * CHUNK2 + t * 16, 16), 16)
            b = coef[rows, :]
            for h in range((width - span) // 128):
                cols, hcols = pl.ds(h * 128, 128), pl.ds(span + h * 128, 128)
                inc2[rows, cols] = (inc2[rows, cols].astype(F32) - b * hid[rows, hcols].astype(F32)).astype(BF16)

        @pl.when(sec > 0)
        def _():
            relay2(c).start()

    def a2a_copy(m, j, target):
        return pltpu.make_async_remote_copy(
            src_ref=snd.at[m, j], dst_ref=rcv.at[m, my_rows, :], send_sem=a2a_send.at[m, j],
            recv_sem=a2a_recv.at[m, me], device_id=dp_dev(target), device_id_type=MESH,
        )

    def a2a_own(m):
        return pltpu.make_async_copy(snd.at[m, me], rcv.at[m, my_rows, :], loc_sem.at[m])

    def project(m, k):
        j = lax.rem(me + k, n_dp)
        rows = pl.ds(pl.multiple_of(m * block, block), block)
        for i in range(heads_d):
            cols = pl.ds(pl.multiple_of(j * cols_d + i * 128, 128), 128)
            gk = dot_tn(gs[rows, cols], q[rows, cols]) * scale
            gv = dot_tn(p[rows, cols].astype(BF16), go[rows, cols])
            snd[m, j, :, pl.ds(i * 128, 128)] = gk.astype(BF16)
            snd[m, j, :, pl.ds(cols_d + i * 128, 128)] = gv.astype(BF16)

        @pl.when(k > 0)
        def _():
            a2a_copy(m, j, j).start()

        @pl.when(k == 0)
        def _():
            a2a_own(m).start()

    def a2a_wait(m):
        a2a_own(m).wait()

        @pl.loop(1, n_dp)
        def _(k):
            j = lax.rem(me + k, n_dp)
            at = pl.ds(pl.multiple_of(j * rows_m, rows_m), rows_m)
            pltpu.make_async_remote_copy(
                src_ref=snd.at[m, j], dst_ref=rcv.at[m, at, :], send_sem=a2a_send.at[m, j],
                recv_sem=a2a_recv.at[m, j], device_id=dp_dev(j), device_id_type=MESH,
            ).wait_recv()

    def weight_grad(m):
        tile = 128

        @pl.loop(0, lat_w // tile)
        def _(t):
            at = pl.ds(pl.multiple_of(t * tile, tile), tile)
            part = dot_nn(lt_all[m, at, :], rcv[m])
            if m == 0:
                grads[at, :] = part
            else:
                grads[at, :] += part

    for c in (hid_loads[0], key_loads[0]):
        c.wait()
    prepare(0)
    for c in (hid_loads[1], key_loads[1], val_loads[0], val_loads[1]):
        c.wait()

    @pl.when(jnp.logical_not(top))
    def _():
        prepare(1)

    @pl.when(top)
    def _():
        for c in cot_loads:
            c.wait()

    @pl.when(early)
    def _():
        gather_second()

    @pl.loop(0, n_chunks)
    def _(c):
        @pl.when(jnp.logical_and(c == per_micro, top))
        def _():
            prepare(1)

        @pl.when(jnp.logical_and(c == per_micro, jnp.logical_not(early)))
        def _():
            gather_second()

        @pl.when(jnp.logical_and(c == per_micro + per_micro // 2, early))
        def _():
            gather_third()

        @pl.when(jnp.logical_not(top))
        def _():
            relay1(c).wait_recv()

        chain_step(c)

        @pl.when(sec > 0)
        def _():
            relay1(c).start()

        share = n_dp // per_micro

        @pl.when(c >= per_micro)
        def _():
            for i in range(share):
                project(0, (c - per_micro) * share + i)

    out_first = [
        pltpu.make_async_copy(inc.at[pl.ds(m * block, block), :], ig_hbm.at[m, :, pl.ds(0, span)], out_sem.at[m])
        for m in range(micro)
    ]
    for c in out_first:
        c.start()

    @pl.loop(0, n_dp)
    def _(k):
        project(1, k)

    @pl.when(jnp.logical_not(early))
    def _():
        gather_third()

    @pl.when(top)
    def _():
        for c in cot2_loads:
            c.wait()

    @pl.loop(0, n_chunks2 // 2)
    def _(c):
        second_step(c)

    @pl.loop(0, n_dp // 2)
    def _(k):
        gather_wait_recv(2 * k + 1 - core)

    a2a_wait(0)
    weight_grad(0)
    for c in (w_load, mf_load, ms_load):
        c.wait()
    a2a_wait(1)
    weight_grad(1)

    @pl.loop(0, lat_w // ADAM_ROWS)
    def _(t):
        at = pl.ds(pl.multiple_of(t * ADAM_ROWS, ADAM_ROWS), ADAM_ROWS)
        for i in range(2):
            cols = pl.ds(i * cols_d, cols_d)
            g = grads[at, cols]
            cur = wts[i, at, :]
            first = 0.9 * mf[i, at, :] + 0.1 * g
            second = 0.95 * ms[i, at, :] + 0.05 * g * g
            new = cur - 0.02 * (first / (jnp.sqrt(second) + 1e-08) + 0.1 * cur)
            wts[i, at, :] = new
            wlow[at, cols] = new.astype(BF16)

    out_w = pltpu.make_async_copy(wts, nw_hbm, out_sem.at[2])
    out_w.start()

    my_cols = pl.ds(pl.multiple_of(me * cols_d, cols_d), cols_d)

    def kv_copy(j, source):
        cols = pl.ds(pl.multiple_of(source * cols_d, cols_d), cols_d)
        return pltpu.make_async_remote_copy(
            src_ref=kvs.at[j], dst_ref=kv_hbm.at[:, :, cols], send_sem=kv_send.at[j],
            recv_sem=kv_recv.at[source], device_id=dp_dev(j), device_id_type=MESH,
        )

    kv_own = pltpu.make_async_copy(kvs.at[me], kv_hbm.at[:, :, my_cols], loc_sem.at[2])

    @pl.loop(0, n_dp // 2)
    def _(k):
        pair = lax.rem(me // 2 + 1 + k, n_dp // 2)
        at = pl.ds(pl.multiple_of(pair * 2 * block, 2 * block), 2 * block)
        out = dot_nn(nl_all[at, :], wlow[...]).astype(BF16)
        for i in range(2):
            for kind in range(2):
                kvs[2 * pair + i, kind] = out[i * block : (i + 1) * block, kind * cols_d : (kind + 1) * cols_d]

        @pl.when(k < n_dp // 2 - 1)
        def _():
            for i in range(2):
                kv_copy(2 * pair + i, me).start()

        @pl.when(k == n_dp // 2 - 1)
        def _():
            kv_copy(core_peer, me).start()
            kv_own.start()

    @pl.loop(n_chunks2 // 2, n_chunks2)
    def _(c):
        second_step(c)

    out_second = [
        pltpu.make_async_copy(inc2.at[pl.ds(m * block, block), :], ig_hbm.at[m, :, pl.ds(span, width - span)], out_sem.at[3 + m])
        for m in range(micro)
    ]
    for c in out_second:
        c.start()

    @pl.when(sec > 0)
    def _():
        @pl.loop(0, n_chunks)
        def _(c):
            relay1(c).wait_send()

        @pl.loop(0, n_chunks2)
        def _(c):
            relay2(c).wait_send()

    @pl.loop(0, 2 * n_y - 1 + n_dp // 2)
    def _(k):
        gather_wait_send(k)

    for m in range(micro):
        @pl.loop(1, n_dp)
        def _(k):
            j = lax.rem(me + k, n_dp)
            a2a_copy(m, j, j).wait_send()

    @pl.loop(1, n_dp)
    def _(k):
        j = lax.rem(me + k, n_dp)
        kv_copy(j, me).wait_send()
        kv_copy(j, j).wait_recv()

    kv_own.wait()
    out_w.wait()
    for c in out_first + out_second:
        c.wait()


def body(
    hidden_states, key_rows, value_rows, latents, next_latents, media_index, cotangent, gate_alpha,
    weights, moment_first, moment_second,
):
    n_sec, n_dp = lax.axis_size("section"), lax.axis_size("dp")
    _, micro, block, width = hidden_states.shape
    span, rows_m = key_rows.shape[3], key_rows.shape[2]
    lat_w, cols_d = weights.shape[2], weights.shape[3]
    tokens = micro * block
    n_y = n_dp // 4
    n_chunks, n_chunks2 = tokens // CHUNK, tokens // CHUNK2
    any_spec = pl.BlockSpec(memory_space=pl.ANY)
    vmem_spec = pl.BlockSpec(memory_space=pltpu.VMEM)
    dma = pltpu.SemaphoreType.DMA
    vmem = pltpu.VMEM
    grad_in, new_w, kv = pl.pallas_call(
        functools.partial(kernel, n_sec, n_dp),
        out_shape=(
            jax.ShapeDtypeStruct((micro, block, width), BF16),
            jax.ShapeDtypeStruct((2, lat_w, cols_d), F32),
            jax.ShapeDtypeStruct((2, rows_m, span), BF16),
        ),
        in_specs=[any_spec] * 5 + [vmem_spec, any_spec, vmem_spec] + [any_spec] * 3,
        out_specs=(any_spec, any_spec, any_spec),
        scratch_shapes=[
            vmem((tokens, width), BF16),
            vmem((micro, rows_m, span), BF16),
            vmem((micro, rows_m, span), BF16),
            vmem((micro, rows_m, lat_w), BF16),
            vmem((tokens, span), BF16),
            vmem((tokens, width - span), BF16),
            vmem((tokens, span), BF16),
            vmem((tokens, span), F32),
            vmem((tokens, span), BF16),
            vmem((tokens, span), BF16),
            vmem((CHUNK, span), F32),
            vmem((tokens, 128), F32),
            vmem((tokens, 128), F32),
            vmem((micro, block, rows_m), F32),
            vmem((micro, lat_w, n_dp * rows_m), BF16),
            vmem((n_dp * block, lat_w), BF16),
            vmem((micro, n_dp, rows_m, 2 * cols_d), BF16),
            vmem((micro, n_dp * rows_m, 2 * cols_d), BF16),
            vmem((2, lat_w, cols_d), F32),
            vmem((2, lat_w, cols_d), F32),
            vmem((2, lat_w, cols_d), F32),
            vmem((lat_w, 2 * cols_d), F32),
            vmem((lat_w, 2 * cols_d), BF16),
            vmem((n_dp, 2, block, cols_d), BF16),
            dma((15,)),
            dma((5,)),
            dma((n_chunks,)),
            dma((n_chunks,)),
            dma((n_chunks2,)),
            dma((n_chunks2,)),
            dma((2, 2 * n_y - 1 + n_dp // 2)),
            dma((2, n_dp)),
            dma((micro, n_dp)),
            dma((micro, n_dp)),
            dma((n_dp,)),
            dma((n_dp,)),
            dma((3,)),
        ],
        compiler_params=pltpu.CompilerParams(
            collective_id=0, has_side_effects=True, vmem_limit_bytes=62 * 1024 * 1024
        ),
    )(
        hidden_states[0], key_rows[0], value_rows[0], latents, next_latents, media_index, cotangent,
        gate_alpha.reshape(1, 1), weights[0], moment_first[0], moment_second[0],
    )
    return grad_in[None], new_w[None], kv[None]


def solution(mesh):
    in_specs = (
        P("section", None, "dp", None),
        P("section", None, "dp", None),
        P("section", None, "dp", None),
        P(None, "dp", None),
        P("dp", None),
        P(None, "dp"),
        P(None, "dp", None),
        P("section"),
        P("section", None, None, "dp"),
        P("section", None, None, "dp"),
        P("section", None, None, "dp"),
    )
    out_specs = (
        P("section", None, "dp", None),
        P("section", None, None, "dp"),
        P("section", None, "dp", None),
    )
    return jax.shard_map(body, mesh=mesh, in_specs=in_specs, out_specs=out_specs, check_vma=False)
```

```python
import functools
import math

import jax
import jax.numpy as jnp
from jax import lax
from jax.experimental import pallas as pl
from jax.experimental.pallas import tpu as pltpu
from jax.sharding import PartitionSpec as P

HEAD_DIM = 128
LATENTS = 64
CHUNK = 16
CHUNK2 = 32
NORM_ROWS = 16
ADAM_ROWS = 64
F32 = jnp.float32
BF16 = jnp.bfloat16
MESH = pl.DeviceIdType.MESH


def dot_nt(a, b):
    return lax.dot_general(a, b, (((1,), (1,)), ((), ())), preferred_element_type=F32)


def dot_tn(a, b):
    return lax.dot_general(a, b, (((0,), (0,)), ((), ())), preferred_element_type=F32)


def dot_nn(a, b):
    return jnp.dot(a, b, preferred_element_type=F32)


def kernel(
    n_sec, n_dp,
    hid_hbm, key_hbm, val_hbm, lat_hbm, nl_hbm, media_ref, cot_hbm, gate_ref, w_hbm, mf_hbm, ms_hbm,
    ig_hbm, nw_hbm, kv_hbm,
    hid, keys, vals, lat, inc, inc2, q, p, go, gs, gpbuf, gbuf, rinv, coef, maskf,
    lt_all, nl_all, snd, rcv, wts, mf, ms, grads, wlow, kvs,
    in_sem, out_sem, r1_send, r1_recv, r2_send, r2_recv,
    gat_send, gat_recv, a2a_send, a2a_recv, kv_send, kv_recv, loc_sem,
):
    sec, me = lax.axis_index("section"), lax.axis_index("dp")
    micro, block, width = hid_hbm.shape
    span = key_hbm.shape[2]
    rows_m = key_hbm.shape[1]
    lat_w = lat_hbm.shape[2]
    cols_d = w_hbm.shape[2]
    heads = span // HEAD_DIM
    heads_d = cols_d // HEAD_DIM
    tokens = micro * block
    n_chunks = tokens // CHUNK
    per_micro = n_chunks // micro
    n_chunks2 = tokens // CHUNK2
    n_y = n_dp // 4
    scale = 1.0 / math.sqrt(HEAD_DIM)
    core = lax.rem(me, 2)
    x_lo = lax.rem(me // 2, 2)
    y_at = me // 4
    top = sec == n_sec - 1
    early = sec < n_sec // 2

    def dp_dev(j):
        return (sec, j)

    barrier = pltpu.get_barrier_semaphore()

    @pl.loop(1, n_dp)
    def _(k):
        pl.semaphore_signal(barrier, inc=1, device_id=dp_dev(lax.rem(me + k, n_dp)), device_id_type=MESH)

    @pl.when(sec > 0)
    def _():
        pl.semaphore_signal(barrier, inc=1, device_id=(sec - 1, me), device_id_type=MESH)

    @pl.when(sec < n_sec - 1)
    def _():
        pl.semaphore_signal(barrier, inc=1, device_id=(sec + 1, me), device_id_type=MESH)

    def load(i, src, dst):
        return pltpu.make_async_copy(src, dst, in_sem.at[i])

    hid_loads = [load(m, hid_hbm.at[m], hid.at[pl.ds(m * block, block), :]) for m in range(micro)]
    key_loads = [load(2 + m, key_hbm.at[m], keys.at[m]) for m in range(micro)]
    val_loads = [load(4 + m, val_hbm.at[m], vals.at[m]) for m in range(micro)]
    lat_load = load(6, lat_hbm, lat)
    nl_load = load(7, nl_hbm, nl_all.at[pl.ds(me * block, block), :])
    w_load, mf_load, ms_load = load(8, w_hbm, wts), load(9, mf_hbm, mf), load(10, ms_hbm, ms)
    cot_loads = [load(11 + m, cot_hbm.at[m, :, pl.ds(0, span)], inc.at[pl.ds(m * block, block), :]) for m in range(micro)]
    cot2_loads = [
        load(13 + m, cot_hbm.at[m, :, pl.ds(span, width - span)], inc2.at[pl.ds(m * block, block), :])
        for m in range(micro)
    ]
    lat_load.start()
    nl_load.start()
    hid_loads[0].start()
    key_loads[0].start()

    @pl.when(top)
    def _():
        for c in cot_loads:
            c.start()

    val_loads[0].start()
    for c in (hid_loads[1], key_loads[1], val_loads[1], w_load, mf_load, ms_load):
        c.start()

    @pl.when(top)
    def _():
        for c in cot2_loads:
            c.start()

    for m in range(micro):
        row = media_ref[pl.ds(m, 1), :].astype(F32)
        maskf[m] = jnp.transpose(jnp.broadcast_to(row, (block, block)))
    lat_load.wait()
    nl_load.wait()
    my_rows = pl.ds(pl.multiple_of(me * rows_m, rows_m), rows_m)
    for m in range(micro):
        lt_all[m, :, my_rows] = jnp.transpose(lat[m].astype(F32)).astype(BF16)

    others = jnp.where(sec > 0, 1, 0) + jnp.where(sec < n_sec - 1, 1, 0) + n_dp - 1
    pl.semaphore_wait(barrier, others)

    def gather_copy(slot, owner, target):
        at = pl.ds(pl.multiple_of(owner * rows_m, rows_m), rows_m)
        ref_l = lt_all.at[:, :, at]
        ref_n = nl_all.at[at, :]
        return [
            pltpu.make_async_remote_copy(
                src_ref=ref, dst_ref=ref, send_sem=gat_send.at[i, slot], recv_sem=gat_recv.at[i, owner],
                device_id=dp_dev(target), device_id_type=MESH,
            )
            for i, ref in enumerate((ref_l, ref_n))
        ]

    def gather_start(slot, owner, target):
        for c in gather_copy(slot, owner, target):
            c.start()

    def gather_wait_recv(owner):
        for c in gather_copy(0, owner, me):
            c.wait_recv()

    def gather_wait_send(slot):
        for c in gather_copy(slot, me, me):
            c.wait_send()

    x_peer = me + 2 - 4 * x_lo
    core_peer = me + 1 - 2 * core

    def y_peer(dy):
        return lax.rem(y_at + dy, n_y) * 4 + x_lo * 2 + core

    gather_start(0, me, x_peer)
    for dy in range(1, n_y):
        gather_start(dy, me, y_peer(dy))

    def gather_second():
        gather_wait_recv(x_peer)
        for dy in range(1, n_y):
            gather_start(n_y - 1 + dy, x_peer, y_peer(dy))

    def gather_third():
        for dy in range(1, n_y):
            gather_wait_recv(y_peer(dy))
            gather_wait_recv(y_peer(dy) + 2 - 4 * x_lo)

        @pl.loop(0, n_dp // 2)
        def _(k):
            gather_start(2 * n_y - 1 + k, 2 * k + core, core_peer)

    def prepare(m):
        base = m * block

        @pl.loop(0, block // NORM_ROWS)
        def _(t):
            rows = pl.ds(pl.multiple_of(base + t * NORM_ROWS, NORM_ROWS), NORM_ROWS)
            total = jnp.zeros((NORM_ROWS, 128), F32)
            for c in range(width // 128):
                h = hid[rows, pl.ds(c * 128, 128)].astype(F32)
                total = total + h * h
            mean = jnp.sum(total, axis=1, keepdims=True) * (1.0 / width)
            r = jnp.broadcast_to(1.0 / jnp.sqrt(mean + 1e-06), (NORM_ROWS, 128))
            rinv[rows, :] = r
            for c in range(heads):
                cols = pl.ds(c * 128, 128)
                q[rows, cols] = (hid[rows, cols].astype(F32) * r).astype(BF16)

        rows = pl.ds(pl.multiple_of(base, block), block)
        half = lax.broadcasted_iota(jnp.int32, (block, rows_m), 1) // LATENTS
        allowed = half.astype(F32) == maskf[m]
        group = 4

        @pl.loop(0, heads // group)
        def _(hg):
            for j in range(group):
                cols = pl.ds(pl.multiple_of((hg * group + j) * 128, 128), 128)
                s = dot_nt(q[rows, cols], keys[m, :, cols]) * scale
                s = jnp.where(allowed, s, -1e30)
                e = jnp.exp(s - jnp.max(s, axis=1, keepdims=True))
                p[rows, cols] = e / jnp.sum(e, axis=1, keepdims=True)

    def transpose_values(m):
        @pl.loop(0, heads // 4)
        def _(hg):
            for j in range(4):
                cols = pl.ds(pl.multiple_of((hg * 4 + j) * 128, 128), 128)
                vals[m, :, cols] = jnp.transpose(vals[m, :, cols])

    def relay1(c):
        rows = pl.ds(pl.multiple_of(c * CHUNK, CHUNK), CHUNK)
        return pltpu.make_async_remote_copy(
            src_ref=inc.at[rows, :], dst_ref=inc.at[rows, :], send_sem=r1_send.at[c], recv_sem=r1_recv.at[c],
            device_id=(jnp.maximum(sec - 1, 0), me), device_id_type=MESH,
        )

    def relay2(c):
        rows = pl.ds(pl.multiple_of(c * CHUNK2, CHUNK2), CHUNK2)
        return pltpu.make_async_remote_copy(
            src_ref=inc2.at[rows, :], dst_ref=inc2.at[rows, :], send_sem=r2_send.at[c], recv_sem=r2_recv.at[c],
            device_id=(jnp.maximum(sec - 1, 0), me), device_id_type=MESH,
        )

    gate_tanh = jnp.tanh(jnp.broadcast_to(gate_ref[...], (CHUNK, 128)))

    def chain_step(c):
        m = c // per_micro
        rows = pl.ds(pl.multiple_of(c * CHUNK, CHUNK), CHUNK)
        for h in range(heads):
            cols = pl.ds(h * 128, 128)
            g = (gate_tanh * inc[rows, cols].astype(F32)).astype(BF16)
            go[rows, cols] = g
            gpbuf[:, cols] = dot_nn(g, vals[m, :, cols])
        for h in range(heads):
            cols = pl.ds(h * 128, 128)
            pr, gp = p[rows, cols], gpbuf[:, cols]
            weighted = jnp.sum(pr * gp, axis=1, keepdims=True)
            gs[rows, cols] = (pr * (gp - weighted)).astype(BF16)
        acc = jnp.zeros((CHUNK, 128), F32)
        for h in range(heads):
            cols = pl.ds(h * 128, 128)
            gk = dot_nn(gs[rows, cols], keys[m, :, cols])
            gbuf[:, cols] = gk
            acc = acc + gk * hid[rows, cols].astype(F32)
        r = rinv[rows, :]
        dots = jnp.sum(acc, axis=1, keepdims=True)
        a = r * scale
        b = r * r * r * (dots * (scale / width))
        coef[rows, :] = b
        for h in range(heads):
            cols = pl.ds(h * 128, 128)
            new = inc[rows, cols].astype(F32) + (a * gbuf[:, cols] - b * hid[rows, cols].astype(F32))
            inc[rows, cols] = new.astype(BF16)

    def second_step(c):
        @pl.when(jnp.logical_not(top))
        def _():
            relay2(c).wait_recv()

        for t in range(CHUNK2 // 16):
            rows = pl.ds(pl.multiple_of(c * CHUNK2 + t * 16, 16), 16)
            b = coef[rows, :]
            for h in range((width - span) // 128):
                cols, hcols = pl.ds(h * 128, 128), pl.ds(span + h * 128, 128)
                inc2[rows, cols] = (inc2[rows, cols].astype(F32) - b * hid[rows, hcols].astype(F32)).astype(BF16)

        @pl.when(sec > 0)
        def _():
            relay2(c).start()

    def a2a_copy(m, j, target):
        return pltpu.make_async_remote_copy(
            src_ref=snd.at[m, j], dst_ref=rcv.at[m, my_rows, :], send_sem=a2a_send.at[m, j],
            recv_sem=a2a_recv.at[m, me], device_id=dp_dev(target), device_id_type=MESH,
        )

    def a2a_own(m):
        return pltpu.make_async_copy(snd.at[m, me], rcv.at[m, my_rows, :], loc_sem.at[m])

    def project(m, k):
        j = lax.rem(me + k, n_dp)
        project_compute(m, j)

        @pl.when(k > 0)
        def _():
            a2a_copy(m, j, j).start()

        @pl.when(k == 0)
        def _():
            a2a_own(m).start()

    def project_compute(m, j):
        rows = pl.ds(pl.multiple_of(m * block, block), block)
        for i in range(heads_d):
            cols = pl.ds(pl.multiple_of(j * cols_d + i * 128, 128), 128)
            gk = dot_tn(gs[rows, cols], q[rows, cols]) * scale
            gv = dot_tn(p[rows, cols].astype(BF16), go[rows, cols])
            snd[m, j, :, pl.ds(i * 128, 128)] = gk.astype(BF16)
            snd[m, j, :, pl.ds(cols_d + i * 128, 128)] = gv.astype(BF16)

    def a2a_wait(m):
        a2a_own(m).wait()

        @pl.loop(1, n_dp)
        def _(k):
            j = lax.rem(me + k, n_dp)
            at = pl.ds(pl.multiple_of(j * rows_m, rows_m), rows_m)
            pltpu.make_async_remote_copy(
                src_ref=snd.at[m, j], dst_ref=rcv.at[m, at, :], send_sem=a2a_send.at[m, j],
                recv_sem=a2a_recv.at[m, j], device_id=dp_dev(j), device_id_type=MESH,
            ).wait_recv()

    def weight_grad(m):
        tile = 128

        @pl.loop(0, lat_w // tile)
        def _(t):
            at = pl.ds(pl.multiple_of(t * tile, tile), tile)
            part = dot_nn(lt_all[m, at, :], rcv[m])
            if m == 0:
                grads[at, :] = part
            else:
                grads[at, :] += part

    for c in (hid_loads[0], key_loads[0]):
        c.wait()
    prepare(0)
    val_loads[0].wait()
    transpose_values(0)
    for c in (hid_loads[1], key_loads[1], val_loads[1]):
        c.wait()

    @pl.when(jnp.logical_not(top))
    def _():
        prepare(1)
        transpose_values(1)

    @pl.when(top)
    def _():
        for c in cot_loads:
            c.wait()

    @pl.when(early)
    def _():
        gather_second()

    @pl.loop(0, n_chunks)
    def _(c):
        @pl.when(jnp.logical_and(c == per_micro, top))
        def _():
            prepare(1)
            transpose_values(1)

        @pl.when(jnp.logical_and(c == per_micro, jnp.logical_not(early)))
        def _():
            gather_second()

        @pl.when(jnp.logical_and(c == per_micro + per_micro // 2, early))
        def _():
            gather_third()

        @pl.when(jnp.logical_not(top))
        def _():
            relay1(c).wait_recv()

        chain_step(c)

        @pl.when(sec > 0)
        def _():
            relay1(c).start()

        share = n_dp // per_micro

        @pl.when(c >= per_micro)
        def _():
            for i in range(share):
                project(0, (c - per_micro) * share + i)

    out_first = [
        pltpu.make_async_copy(inc.at[pl.ds(m * block, block), :], ig_hbm.at[m, :, pl.ds(0, span)], out_sem.at[m])
        for m in range(micro)
    ]
    for c in out_first:
        c.start()

    @pl.loop(0, n_dp)
    def _(k):
        project(1, k)

    @pl.when(jnp.logical_not(early))
    def _():
        gather_third()

    @pl.when(top)
    def _():
        for c in cot2_loads:
            c.wait()

    @pl.loop(0, n_chunks2 // 2)
    def _(c):
        second_step(c)

    @pl.loop(0, n_dp // 2)
    def _(k):
        gather_wait_recv(2 * k + 1 - core)

    a2a_wait(0)
    weight_grad(0)
    for c in (w_load, mf_load, ms_load):
        c.wait()
    a2a_wait(1)
    weight_grad(1)

    @pl.loop(0, lat_w // ADAM_ROWS)
    def _(t):
        at = pl.ds(pl.multiple_of(t * ADAM_ROWS, ADAM_ROWS), ADAM_ROWS)
        for i in range(2):
            cols = pl.ds(i * cols_d, cols_d)
            g = grads[at, cols]
            cur = wts[i, at, :]
            first = 0.9 * mf[i, at, :] + 0.1 * g
            second = 0.95 * ms[i, at, :] + 0.05 * g * g
            new = cur - 0.02 * (first / (jnp.sqrt(second) + 1e-08) + 0.1 * cur)
            wts[i, at, :] = new
            wlow[at, cols] = new.astype(BF16)

    out_w = pltpu.make_async_copy(wts, nw_hbm, out_sem.at[2])
    out_w.start()

    my_cols = pl.ds(pl.multiple_of(me * cols_d, cols_d), cols_d)

    def kv_copy(j, source):
        cols = pl.ds(pl.multiple_of(source * cols_d, cols_d), cols_d)
        return pltpu.make_async_remote_copy(
            src_ref=kvs.at[j], dst_ref=kv_hbm.at[:, :, cols], send_sem=kv_send.at[j],
            recv_sem=kv_recv.at[source], device_id=dp_dev(j), device_id_type=MESH,
        )

    kv_own = pltpu.make_async_copy(kvs.at[me], kv_hbm.at[:, :, my_cols], loc_sem.at[2])

    @pl.loop(0, n_dp // 2)
    def _(k):
        pair = lax.rem(me // 2 + 1 + k, n_dp // 2)
        at = pl.ds(pl.multiple_of(pair * 2 * block, 2 * block), 2 * block)
        out = dot_nn(nl_all[at, :], wlow[...]).astype(BF16)
        for i in range(2):
            for kind in range(2):
                kvs[2 * pair + i, kind] = out[i * block : (i + 1) * block, kind * cols_d : (kind + 1) * cols_d]

        @pl.when(k < n_dp // 2 - 1)
        def _():
            for i in range(2):
                kv_copy(2 * pair + i, me).start()

        @pl.when(k == n_dp // 2 - 1)
        def _():
            kv_copy(core_peer, me).start()
            kv_own.start()

    @pl.loop(n_chunks2 // 2, n_chunks2)
    def _(c):
        second_step(c)

    out_second = [
        pltpu.make_async_copy(inc2.at[pl.ds(m * block, block), :], ig_hbm.at[m, :, pl.ds(span, width - span)], out_sem.at[3 + m])
        for m in range(micro)
    ]
    for c in out_second:
        c.start()

    @pl.when(sec > 0)
    def _():
        @pl.loop(0, n_chunks)
        def _(c):
            relay1(c).wait_send()

        @pl.loop(0, n_chunks2)
        def _(c):
            relay2(c).wait_send()

    @pl.loop(0, 2 * n_y - 1 + n_dp // 2)
    def _(k):
        gather_wait_send(k)

    for m in range(micro):
        @pl.loop(1, n_dp)
        def _(k):
            j = lax.rem(me + k, n_dp)
            a2a_copy(m, j, j).wait_send()

    @pl.loop(1, n_dp)
    def _(k):
        j = lax.rem(me + k, n_dp)
        kv_copy(j, me).wait_send()
        kv_copy(j, j).wait_recv()

    kv_own.wait()
    out_w.wait()
    for c in out_first + out_second:
        c.wait()


def body(
    hidden_states, key_rows, value_rows, latents, next_latents, media_index, cotangent, gate_alpha,
    weights, moment_first, moment_second,
):
    n_sec, n_dp = lax.axis_size("section"), lax.axis_size("dp")
    _, micro, block, width = hidden_states.shape
    span, rows_m = key_rows.shape[3], key_rows.shape[2]
    lat_w, cols_d = weights.shape[2], weights.shape[3]
    tokens = micro * block
    n_y = n_dp // 4
    n_chunks, n_chunks2 = tokens // CHUNK, tokens // CHUNK2
    any_spec = pl.BlockSpec(memory_space=pl.ANY)
    vmem_spec = pl.BlockSpec(memory_space=pltpu.VMEM)
    dma = pltpu.SemaphoreType.DMA
    vmem = pltpu.VMEM
    grad_in, new_w, kv = pl.pallas_call(
        functools.partial(kernel, n_sec, n_dp),
        out_shape=(
            jax.ShapeDtypeStruct((micro, block, width), BF16),
            jax.ShapeDtypeStruct((2, lat_w, cols_d), F32),
            jax.ShapeDtypeStruct((2, rows_m, span), BF16),
        ),
        in_specs=[any_spec] * 5 + [vmem_spec, any_spec, vmem_spec] + [any_spec] * 3,
        out_specs=(any_spec, any_spec, any_spec),
        scratch_shapes=[
            vmem((tokens, width), BF16),
            vmem((micro, rows_m, span), BF16),
            vmem((micro, rows_m, span), BF16),
            vmem((micro, rows_m, lat_w), BF16),
            vmem((tokens, span), BF16),
            vmem((tokens, width - span), BF16),
            vmem((tokens, span), BF16),
            vmem((tokens, span), F32),
            vmem((tokens, span), BF16),
            vmem((tokens, span), BF16),
            vmem((CHUNK, span), F32),
            vmem((CHUNK, span), F32),
            vmem((tokens, 128), F32),
            vmem((tokens, 128), F32),
            vmem((micro, block, rows_m), F32),
            vmem((micro, lat_w, n_dp * rows_m), BF16),
            vmem((n_dp * block, lat_w), BF16),
            vmem((micro, n_dp, rows_m, 2 * cols_d), BF16),
            vmem((micro, n_dp * rows_m, 2 * cols_d), BF16),
            vmem((2, lat_w, cols_d), F32),
            vmem((2, lat_w, cols_d), F32),
            vmem((2, lat_w, cols_d), F32),
            vmem((lat_w, 2 * cols_d), F32),
            vmem((lat_w, 2 * cols_d), BF16),
            vmem((n_dp, 2, block, cols_d), BF16),
            dma((15,)),
            dma((5,)),
            dma((n_chunks,)),
            dma((n_chunks,)),
            dma((n_chunks2,)),
            dma((n_chunks2,)),
            dma((2, 2 * n_y - 1 + n_dp // 2)),
            dma((2, n_dp)),
            dma((micro, n_dp)),
            dma((micro, n_dp)),
            dma((n_dp,)),
            dma((n_dp,)),
            dma((3,)),
        ],
        compiler_params=pltpu.CompilerParams(
            collective_id=0, has_side_effects=True, vmem_limit_bytes=62 * 1024 * 1024
        ),
    )(
        hidden_states[0], key_rows[0], value_rows[0], latents, next_latents, media_index, cotangent,
        gate_alpha.reshape(1, 1), weights[0], moment_first[0], moment_second[0],
    )
    return grad_in[None], new_w[None], kv[None]


def solution(mesh):
    in_specs = (
        P("section", None, "dp", None),
        P("section", None, "dp", None),
        P("section", None, "dp", None),
        P(None, "dp", None),
        P("dp", None),
        P(None, "dp"),
        P(None, "dp", None),
        P("section"),
        P("section", None, None, "dp"),
        P("section", None, None, "dp"),
        P("section", None, None, "dp"),
    )
    out_specs = (
        P("section", None, "dp", None),
        P("section", None, None, "dp"),
        P("section", None, "dp", None),
    )
    return jax.shard_map(body, mesh=mesh, in_specs=in_specs, out_specs=out_specs, check_vma=False)
```

```python
import functools
import math

import jax
import jax.numpy as jnp
from jax import lax
from jax.experimental import pallas as pl
from jax.experimental.pallas import tpu as pltpu
from jax.sharding import PartitionSpec as P

HEAD_DIM = 128
LATENTS = 64
CHUNK = 16
CHUNK2 = 16
NORM_ROWS = 16
TOP_ROWS = 32
OWNERS = 4
GROUP = 8
ADAM_ROWS = 64
WG_ROWS = 256
F32 = jnp.float32
BF16 = jnp.bfloat16
MESH = pl.DeviceIdType.MESH


def dot_nt(a, b):
    return lax.dot_general(a, b, (((1,), (1,)), ((), ())), preferred_element_type=F32)


def dot_tn(a, b):
    return lax.dot_general(a, b, (((0,), (0,)), ((), ())), preferred_element_type=F32)


def dot_nn(a, b):
    return jnp.dot(a, b, preferred_element_type=F32)


def kernel(
    n_sec, n_dp,
    hid_hbm, key_hbm, val_hbm, lat_hbm, nl_hbm, media_ref, cot_hbm, gate_ref, w_hbm, mf_hbm, ms_hbm,
    ig_hbm, nw_hbm, kv_hbm,
    hid, keys, vals, lat, inc, inc2, q, p, go, gs, sbuf, gpbuf, gbuf, rinv, coef, maskf,
    lt_all, nl_all, snd, rcv, wts, mf, ms, grads, wlow, kvs, fwd,
    in_sem, out_sem, r1_send, r1_recv, r2_send, r2_recv,
    f_send, gat_send, gat_recv, a2a_send, a2a_recv, kv_send, kv_recv, loc_sem,
):
    sec, me = lax.axis_index("section"), lax.axis_index("dp")
    micro, block, width = hid_hbm.shape
    span = key_hbm.shape[2]
    rows_m = key_hbm.shape[1]
    lat_w = lat_hbm.shape[2]
    cols_d = w_hbm.shape[2]
    heads = span // HEAD_DIM
    heads_d = cols_d // HEAD_DIM
    tokens = micro * block
    n_chunks = tokens // CHUNK
    per_micro = n_chunks // micro
    n_chunks2 = tokens // CHUNK2
    n_y = n_dp // 4
    scale = 1.0 / math.sqrt(HEAD_DIM)
    core = lax.rem(me, 2)
    x_lo = lax.rem(me // 2, 2)
    y_at = me // 4
    top = sec == n_sec - 1
    mid_at = n_sec // 2
    early = sec < mid_at
    detour = mid_at < n_sec - 1
    mid = jnp.logical_and(sec == mid_at, detour)

    def dp_dev(j):
        return (sec, j)

    barrier = pltpu.get_barrier_semaphore()

    @pl.loop(1, n_dp)
    def _(k):
        pl.semaphore_signal(barrier, inc=1, device_id=dp_dev(lax.rem(me + k, n_dp)), device_id_type=MESH)

    @pl.when(sec > 0)
    def _():
        pl.semaphore_signal(barrier, inc=1, device_id=(sec - 1, me), device_id_type=MESH)

    @pl.when(sec < n_sec - 1)
    def _():
        pl.semaphore_signal(barrier, inc=1, device_id=(sec + 1, me), device_id_type=MESH)

    def ring_pairs(do):
        if detour:
            for one, two in ((mid_at, n_sec - 1), (n_sec - 1, mid_at - 1)):
                if one - two != 1 and two - one != 1:
                    for a, b in ((one, two), (two, one)):
                        do(a, b)

    def greet(a, b):
        @pl.when(sec == a)
        def _():
            pl.semaphore_signal(barrier, inc=1, device_id=(b, me), device_id_type=MESH)

    ring_pairs(greet)

    def load(i, src, dst):
        return pltpu.make_async_copy(src, dst, in_sem.at[i])

    hid_loads = [load(m, hid_hbm.at[m], hid.at[pl.ds(m * block, block), :]) for m in range(micro)]
    key_loads = [load(2 + m, key_hbm.at[m], keys.at[m]) for m in range(micro)]
    val_loads = [load(4 + m, val_hbm.at[m], vals.at[m]) for m in range(micro)]
    lat_load = load(6, lat_hbm, lat)
    nl_load = load(7, nl_hbm, nl_all.at[pl.ds(me * block, block), :])
    w_load, mf_load, ms_load = load(8, w_hbm, wts), load(9, mf_hbm, mf), load(10, ms_hbm, ms)
    cot_loads = [load(11 + m, cot_hbm.at[m, :, pl.ds(0, span)], inc.at[pl.ds(m * block, block), :]) for m in range(micro)]
    cot2_loads = [
        load(13 + m, cot_hbm.at[m, :, pl.ds(span, width - span)], inc2.at[pl.ds(m * block, block), :])
        for m in range(micro)
    ]
    lat_load.start()
    nl_load.start()
    hid_loads[0].start()
    key_loads[0].start()

    @pl.when(top)
    def _():
        for c in cot_loads:
            c.start()

    val_loads[0].start()
    for c in (hid_loads[1], key_loads[1], val_loads[1], w_load, mf_load, ms_load):
        c.start()

    @pl.when(top)
    def _():
        for c in cot2_loads:
            c.start()

    for m in range(micro):
        row = media_ref[pl.ds(m, 1), :].astype(F32)
        maskf[m] = jnp.transpose(jnp.broadcast_to(row, (block, block)))
    lat_load.wait()
    nl_load.wait()
    my_rows = pl.ds(pl.multiple_of(me * rows_m, rows_m), rows_m)
    for m in range(micro):
        lt_all[m, :, my_rows] = jnp.transpose(lat[m].astype(F32)).astype(BF16)

    others = jnp.where(sec > 0, 1, 0) + jnp.where(sec < n_sec - 1, 1, 0) + n_dp - 1
    extra = [others]

    def expect(a, b):
        extra[0] = extra[0] + jnp.where(sec == a, 1, 0)

    ring_pairs(expect)
    pl.semaphore_wait(barrier, extra[0])

    def gather_copy(slot, owner, target):
        at = pl.ds(pl.multiple_of(owner * rows_m, rows_m), rows_m)
        ref_l = lt_all.at[:, :, at]
        ref_n = nl_all.at[at, :]
        return [
            pltpu.make_async_remote_copy(
                src_ref=ref, dst_ref=ref, send_sem=gat_send.at[i, slot], recv_sem=gat_recv.at[i, owner],
                device_id=dp_dev(target), device_id_type=MESH,
            )
            for i, ref in enumerate((ref_l, ref_n))
        ]

    def gather_start(slot, owner, target):
        for c in gather_copy(slot, owner, target):
            c.start()

    def gather_wait_recv(owner):
        for c in gather_copy(0, owner, me):
            c.wait_recv()

    def gather_wait_send(slot):
        for c in gather_copy(slot, me, me):
            c.wait_send()

    x_peer = me + 2 - 4 * x_lo
    core_peer = me + 1 - 2 * core

    def y_peer(dy):
        return lax.rem(y_at + dy, n_y) * 4 + x_lo * 2 + core

    gather_start(0, me, x_peer)
    for dy in range(1, n_y):
        gather_start(dy, me, y_peer(dy))

    def gather_second():
        gather_wait_recv(x_peer)
        for dy in range(1, n_y):
            gather_start(n_y - 1 + dy, x_peer, y_peer(dy))

    def gather_third():
        for dy in range(1, n_y):
            gather_wait_recv(y_peer(dy))
            gather_wait_recv(y_peer(dy) + 2 - 4 * x_lo)

        @pl.loop(0, n_dp // 2)
        def _(k):
            gather_start(2 * n_y - 1 + k, 2 * k + core, core_peer)

    def prepare(m, start, count):
        @pl.loop(0, count // NORM_ROWS)
        def _(t):
            rows = pl.ds(pl.multiple_of(m * block + start + t * NORM_ROWS, NORM_ROWS), NORM_ROWS)
            total = jnp.zeros((NORM_ROWS, 128), F32)
            for c in range(width // 128):
                h = hid[rows, pl.ds(c * 128, 128)].astype(F32)
                total = total + h * h
            mean = jnp.sum(total, axis=1, keepdims=True) * (1.0 / width)
            r = jnp.broadcast_to(1.0 / jnp.sqrt(mean + 1e-06), (NORM_ROWS, 128))
            rinv[rows, :] = r
            for c in range(heads):
                cols = pl.ds(c * 128, 128)
                q[rows, cols] = (hid[rows, cols].astype(F32) * r).astype(BF16)

        rows = pl.ds(pl.multiple_of(m * block + start, count), count)
        half = lax.broadcasted_iota(jnp.int32, (count, rows_m), 1) // LATENTS
        allowed = half.astype(F32) == maskf[m, pl.ds(pl.multiple_of(start, count), count), :]

        @pl.loop(0, heads // GROUP)
        def _(hg):
            for j in range(GROUP):
                cols = pl.ds(pl.multiple_of((hg * GROUP + j) * 128, 128), 128)
                sbuf[pl.ds(0, count), pl.ds(j * 128, 128)] = dot_nt(q[rows, cols], keys[m, :, cols])
            for j in range(GROUP):
                cols = pl.ds(pl.multiple_of((hg * GROUP + j) * 128, 128), 128)
                s = jnp.where(allowed, sbuf[pl.ds(0, count), pl.ds(j * 128, 128)] * scale, -1e30)
                e = jnp.exp(s - jnp.max(s, axis=1, keepdims=True))
                p[rows, cols] = e / jnp.sum(e, axis=1, keepdims=True)

    def transpose_values(m):
        @pl.loop(0, heads // 4)
        def _(hg):
            for j in range(4):
                cols = pl.ds(pl.multiple_of((hg * 4 + j) * 128, 128), 128)
                vals[m, :, cols] = jnp.transpose(vals[m, :, cols])

    def relay1(c):
        rows = pl.ds(pl.multiple_of(c * CHUNK, CHUNK), CHUNK)
        return pltpu.make_async_remote_copy(
            src_ref=inc.at[rows, :], dst_ref=inc.at[rows, :], send_sem=r1_send.at[c], recv_sem=r1_recv.at[c],
            device_id=(jnp.maximum(sec - 1, 0), me), device_id_type=MESH,
        )

    def relay2(c, dst=inc2, to=None):
        rows = pl.ds(pl.multiple_of(c * CHUNK2, CHUNK2), CHUNK2)
        return pltpu.make_async_remote_copy(
            src_ref=inc2.at[rows, :], dst_ref=dst.at[rows, :], send_sem=r2_send.at[c], recv_sem=r2_recv.at[c],
            device_id=(jnp.maximum(sec - 1, 0) if to is None else to, me), device_id_type=MESH,
        )

    def forward2(c):
        rows = pl.ds(pl.multiple_of(c * CHUNK2, CHUNK2), CHUNK2)
        return pltpu.make_async_remote_copy(
            src_ref=fwd.at[rows, :], dst_ref=inc2.at[rows, :], send_sem=f_send.at[c], recv_sem=r2_recv.at[c],
            device_id=(mid_at - 1, me), device_id_type=MESH,
        )

    gate_tanh = jnp.tanh(jnp.broadcast_to(gate_ref[...], (CHUNK, 128)))

    def chain_step(c, dot_values):
        m = c // per_micro
        rows = pl.ds(pl.multiple_of(c * CHUNK, CHUNK), CHUNK)
        for h in range(heads):
            cols = pl.ds(h * 128, 128)
            g = (gate_tanh * inc[rows, cols].astype(F32)).astype(BF16)
            go[rows, cols] = g
            gpbuf[:, cols] = dot_values(g, vals[m, :, cols])
        for h in range(heads):
            cols = pl.ds(h * 128, 128)
            pr, gp = p[rows, cols], gpbuf[:, cols]
            weighted = jnp.sum(pr * gp, axis=1, keepdims=True)
            gs[rows, cols] = (pr * (gp - weighted)).astype(BF16)
        acc = jnp.zeros((CHUNK, 128), F32)
        for h in range(heads):
            cols = pl.ds(h * 128, 128)
            gk = dot_nn(gs[rows, cols], keys[m, :, cols])
            gbuf[:, cols] = gk
            acc = acc + gk * hid[rows, cols].astype(F32)
        r = rinv[rows, :]
        dots = jnp.sum(acc, axis=1, keepdims=True)
        a = r * scale
        b = r * r * r * (dots * (scale / width))
        coef[rows, :] = b
        for h in range(heads):
            cols = pl.ds(h * 128, 128)
            new = inc[rows, cols].astype(F32) + (a * gbuf[:, cols] - b * hid[rows, cols].astype(F32))
            inc[rows, cols] = new.astype(BF16)

    def second_step(c):
        @pl.when(jnp.logical_not(top))
        def _():
            relay2(c).wait_recv()

        for t in range(CHUNK2 // 16):
            rows = pl.ds(pl.multiple_of(c * CHUNK2 + t * 16, 16), 16)
            b = coef[rows, :]
            for h in range((width - span) // 128):
                cols, hcols = pl.ds(h * 128, 128), pl.ds(span + h * 128, 128)
                inc2[rows, cols] = (inc2[rows, cols].astype(F32) - b * hid[rows, hcols].astype(F32)).astype(BF16)

        @pl.when(jnp.logical_and(sec > 0, jnp.logical_not(mid)))
        def _():
            relay2(c).start()

        if detour:
            @pl.when(mid)
            def _():
                relay2(c, fwd, n_sec - 1).start()

    def a2a_copy(m, kind, j):
        return pltpu.make_async_remote_copy(
            src_ref=snd.at[m, j, kind], dst_ref=rcv.at[m, kind, my_rows, :], send_sem=a2a_send.at[m, kind, j],
            recv_sem=a2a_recv.at[m, kind, me], device_id=dp_dev(j), device_id_type=MESH,
        )

    def a2a_in(m, kind, j):
        at = pl.ds(pl.multiple_of(j * rows_m, rows_m), rows_m)
        return pltpu.make_async_remote_copy(
            src_ref=snd.at[m, j, kind], dst_ref=rcv.at[m, kind, at, :], send_sem=a2a_send.at[m, kind, j],
            recv_sem=a2a_recv.at[m, kind, j], device_id=dp_dev(j), device_id_type=MESH,
        )

    def a2a_own(m, kind):
        return pltpu.make_async_copy(snd.at[m, me, kind], rcv.at[m, kind, my_rows, :], loc_sem.at[m, kind])

    def project(m, kinds, k, count):
        owners = [lax.rem(me + k + i, n_dp) for i in range(count)]
        for kind in kinds:
            project_compute(m, kind, owners)
        for i, j in enumerate(owners):
            for kind in kinds:
                @pl.when(k + i > 0)
                def _():
                    a2a_copy(m, kind, j).start()

                @pl.when(k + i == 0)
                def _():
                    a2a_own(m, kind).start()

    def project_compute(m, kind, owners):
        rows = pl.ds(pl.multiple_of(m * block, block), block)
        outs = []
        for j in owners:
            for i in range(heads_d):
                cols = pl.ds(pl.multiple_of(j * cols_d + i * 128, 128), 128)
                if kind == 0:
                    out = dot_tn(gs[rows, cols], q[rows, cols]) * scale
                else:
                    out = dot_tn(p[rows, cols].astype(BF16), go[rows, cols])
                outs.append((j, i, out.astype(BF16)))
        for j, i, out in outs:
            snd[m, j, kind, :, pl.ds(i * 128, 128)] = out

    def a2a_wait(m, kind):
        a2a_own(m, kind).wait()

        @pl.loop(1, n_dp)
        def _(k):
            a2a_in(m, kind, lax.rem(me + k, n_dp)).wait_recv()

    def weight_grad(m, kind):
        tile = WG_ROWS

        @pl.loop(0, lat_w // tile)
        def _(t):
            at = pl.ds(pl.multiple_of(t * tile, tile), tile)
            part = dot_nn(lt_all[m, at, :], rcv[m, kind])
            if m == 0:
                grads[kind, at, :] = part
            else:
                grads[kind, at, :] += part

    def adam(i):
        @pl.loop(0, lat_w // ADAM_ROWS)
        def _(t):
            at = pl.ds(pl.multiple_of(t * ADAM_ROWS, ADAM_ROWS), ADAM_ROWS)
            g = grads[i, at, :]
            cur = wts[i, at, :]
            first = 0.9 * mf[i, at, :] + 0.1 * g
            second = 0.95 * ms[i, at, :] + 0.05 * g * g
            new = cur - 0.02 * (first / (jnp.sqrt(second) + 1e-08) + 0.1 * cur)
            wts[i, at, :] = new
            wlow[i, at, :] = new.astype(BF16)

    my_cols = pl.ds(pl.multiple_of(me * cols_d, cols_d), cols_d)

    def kv_copy(kind, j, source):
        cols = pl.ds(pl.multiple_of(source * cols_d, cols_d), cols_d)
        return pltpu.make_async_remote_copy(
            src_ref=kvs.at[kind, j], dst_ref=kv_hbm.at[kind, :, cols], send_sem=kv_send.at[kind, j],
            recv_sem=kv_recv.at[kind, source], device_id=dp_dev(j), device_id_type=MESH,
        )

    def kv_own(kind):
        return pltpu.make_async_copy(kvs.at[kind, me], kv_hbm.at[kind, :, my_cols], loc_sem.at[2, kind])

    def next_rows(kind):
        @pl.loop(0, n_dp // 2)
        def _(k):
            pair = lax.rem(me // 2 + 1 + k, n_dp // 2)
            at = pl.ds(pl.multiple_of(pair * 2 * block, 2 * block), 2 * block)
            out = dot_nn(nl_all[at, :], wlow[kind]).astype(BF16)
            for i in range(2):
                kvs[kind, 2 * pair + i] = out[i * block : (i + 1) * block, :]

            @pl.when(k < n_dp // 2 - 1)
            def _():
                for i in range(2):
                    kv_copy(kind, 2 * pair + i, me).start()

            @pl.when(k == n_dp // 2 - 1)
            def _():
                kv_copy(kind, core_peer, me).start()
                kv_own(kind).start()

    def out_weights(kind):
        return pltpu.make_async_copy(wts.at[kind], nw_hbm.at[kind], out_sem.at[2 * micro + kind])

    def finish_kind(kind):
        a2a_wait(1, kind)
        weight_grad(1, kind)
        adam(kind)
        out_weights(kind).start()
        next_rows(kind)

    for c in (hid_loads[0], key_loads[0]):
        c.wait()

    @pl.when(jnp.logical_not(top))
    def _():
        prepare(0, 0, block)

    val_loads[0].wait()

    def wait_rest():
        for c in (hid_loads[1:], key_loads[1:], val_loads[1:]):
            for d in c:
                d.wait()

    @pl.when(jnp.logical_not(top))
    def _():
        wait_rest()
        prepare(1, 0, block)
        for m in range(micro):
            transpose_values(m)

    @pl.when(top)
    def _():
        cot_loads[0].wait()

    @pl.when(early)
    def _():
        gather_second()

    share = n_dp // per_micro
    together = TOP_ROWS // CHUNK

    @pl.loop(0, n_chunks)
    def _(c):
        @pl.when(jnp.logical_and(c == per_micro, jnp.logical_not(early)))
        def _():
            gather_second()

        @pl.when(jnp.logical_and(c == per_micro + per_micro // 2, early))
        def _():
            gather_third()

        @pl.when(top)
        def _():
            @pl.when(c == per_micro)
            def _():
                wait_rest()
                for d in cot_loads[1:]:
                    d.wait()

            @pl.when(lax.rem(c, together) == 0)
            def _():
                prepare(c // per_micro, lax.rem(c, per_micro) * CHUNK, TOP_ROWS)

            chain_step(c, dot_nt)

        @pl.when(jnp.logical_not(top))
        def _():
            relay1(c).wait_recv()
            chain_step(c, dot_nn)

        @pl.when(sec > 0)
        def _():
            relay1(c).start()

        @pl.when(jnp.logical_and(c >= per_micro, jnp.logical_not(mid)))
        def _():
            project(0, (1, 0), (c - per_micro) * share, share)

    out_first = [
        pltpu.make_async_copy(inc.at[pl.ds(m * block, block), :], ig_hbm.at[m, :, pl.ds(0, span)], out_sem.at[m])
        for m in range(micro)
    ]
    for c in out_first:
        c.start()

    @pl.when(mid)
    def _():
        @pl.loop(0, n_dp // OWNERS)
        def _(k):
            project(0, (1, 0), k * OWNERS, OWNERS)

    for kind in (1, 0):
        @pl.loop(0, n_dp // OWNERS)
        def _(k):
            project(1, (kind,), k * OWNERS, OWNERS)

    @pl.when(top)
    def _():
        for c in cot2_loads:
            c.wait()

    def second_steps(first, last):
        @pl.loop(first, last)
        def _(c):
            second_step(c)

    def forward_steps(first, last):
        if detour:
            @pl.when(top)
            def _():
                @pl.loop(first, last)
                def _(c):
                    relay2(c, fwd, mid_at).wait_recv()
                    forward2(c).start()

    def upto(top_at, mid_at, late_at, at):
        bound = jnp.where(top, top_at, jnp.where(mid, mid_at, jnp.where(early, at, late_at)))
        return bound * n_chunks2 // 16

    stop0, stop1, stop2 = upto(16, 9, 7, 4), upto(16, 16, 13, 6), upto(16, 16, 16, 10)
    second_steps(0, stop0)

    @pl.when(jnp.logical_not(early))
    def _():
        gather_third()

    @pl.loop(0, n_dp // 2)
    def _(k):
        gather_wait_recv(2 * k + 1 - core)

    for c in (w_load, mf_load, ms_load):
        c.wait()
    for kind in (1, 0):
        a2a_wait(0, kind)
        weight_grad(0, kind)
    second_steps(stop0, stop1)
    forward_steps(0, n_chunks2)
    finish_kind(1)
    second_steps(stop1, stop2)
    finish_kind(0)

    second_steps(stop2, n_chunks2)

    out_second = [
        pltpu.make_async_copy(inc2.at[pl.ds(m * block, block), :], ig_hbm.at[m, :, pl.ds(span, width - span)], out_sem.at[micro + m])
        for m in range(micro)
    ]
    for c in out_second:
        c.start()

    @pl.when(sec > 0)
    def _():
        @pl.loop(0, n_chunks)
        def _(c):
            relay1(c).wait_send()

        @pl.loop(0, n_chunks2)
        def _(c):
            relay2(c).wait_send()

    @pl.loop(0, 2 * n_y - 1 + n_dp // 2)
    def _(k):
        gather_wait_send(k)

    if detour:
        @pl.when(top)
        def _():
            @pl.loop(0, n_chunks2)
            def _(c):
                forward2(c).wait_send()

    @pl.loop(1, n_dp)
    def _(k):
        j = lax.rem(me + k, n_dp)
        for kind in range(2):
            for m in range(micro):
                a2a_copy(m, kind, j).wait_send()
            kv_copy(kind, j, me).wait_send()
            kv_copy(kind, j, j).wait_recv()

    for kind in range(2):
        kv_own(kind).wait()
        out_weights(kind).wait()
    for c in out_first + out_second:
        c.wait()


def body(
    hidden_states, key_rows, value_rows, latents, next_latents, media_index, cotangent, gate_alpha,
    weights, moment_first, moment_second,
):
    n_sec, n_dp = lax.axis_size("section"), lax.axis_size("dp")
    _, micro, block, width = hidden_states.shape
    span, rows_m = key_rows.shape[3], key_rows.shape[2]
    lat_w, cols_d = weights.shape[2], weights.shape[3]
    tokens = micro * block
    n_y = n_dp // 4
    n_chunks, n_chunks2 = tokens // CHUNK, tokens // CHUNK2
    any_spec = pl.BlockSpec(memory_space=pl.ANY)
    vmem_spec = pl.BlockSpec(memory_space=pltpu.VMEM)
    dma = pltpu.SemaphoreType.DMA
    vmem = pltpu.VMEM
    grad_in, new_w, kv = pl.pallas_call(
        functools.partial(kernel, n_sec, n_dp),
        out_shape=(
            jax.ShapeDtypeStruct((micro, block, width), BF16),
            jax.ShapeDtypeStruct((2, lat_w, cols_d), F32),
            jax.ShapeDtypeStruct((2, rows_m, span), BF16),
        ),
        in_specs=[any_spec] * 5 + [vmem_spec, any_spec, vmem_spec] + [any_spec] * 3,
        out_specs=(any_spec, any_spec, any_spec),
        scratch_shapes=[
            vmem((tokens, width), BF16),
            vmem((micro, rows_m, span), BF16),
            vmem((micro, rows_m, span), BF16),
            vmem((micro, rows_m, lat_w), BF16),
            vmem((tokens, span), BF16),
            vmem((tokens, width - span), BF16),
            vmem((tokens, span), BF16),
            vmem((tokens, span), F32),
            vmem((tokens, span), BF16),
            vmem((tokens, span), BF16),
            vmem((block, GROUP * 128), F32),
            vmem((CHUNK, span), F32),
            vmem((CHUNK, span), F32),
            vmem((tokens, 128), F32),
            vmem((tokens, 128), F32),
            vmem((micro, block, rows_m), F32),
            vmem((micro, lat_w, n_dp * rows_m), BF16),
            vmem((n_dp * block, lat_w), BF16),
            vmem((micro, n_dp, 2, rows_m, cols_d), BF16),
            vmem((micro, 2, n_dp * rows_m, cols_d), BF16),
            vmem((2, lat_w, cols_d), F32),
            vmem((2, lat_w, cols_d), F32),
            vmem((2, lat_w, cols_d), F32),
            vmem((2, lat_w, cols_d), F32),
            vmem((2, lat_w, cols_d), BF16),
            vmem((2, n_dp, block, cols_d), BF16),
            vmem((tokens, width - span), BF16),
            dma((15,)),
            dma((2 * micro + 2,)),
            dma((n_chunks,)),
            dma((n_chunks,)),
            dma((n_chunks2,)),
            dma((n_chunks2,)),
            dma((n_chunks2,)),
            dma((2, 2 * n_y - 1 + n_dp // 2)),
            dma((2, n_dp)),
            dma((micro, 2, n_dp)),
            dma((micro, 2, n_dp)),
            dma((2, n_dp)),
            dma((2, n_dp)),
            dma((3, 2)),
        ],
        compiler_params=pltpu.CompilerParams(
            collective_id=0, has_side_effects=True, vmem_limit_bytes=62 * 1024 * 1024
        ),
    )(
        hidden_states[0], key_rows[0], value_rows[0], latents, next_latents, media_index, cotangent,
        gate_alpha.reshape(1, 1), weights[0], moment_first[0], moment_second[0],
    )
    return grad_in[None], new_w[None], kv[None]


def solution(mesh):
    in_specs = (
        P("section", None, "dp", None),
        P("section", None, "dp", None),
        P("section", None, "dp", None),
        P(None, "dp", None),
        P("dp", None),
        P(None, "dp"),
        P(None, "dp", None),
        P("section"),
        P("section", None, None, "dp"),
        P("section", None, None, "dp"),
        P("section", None, None, "dp"),
    )
    out_specs = (
        P("section", None, "dp", None),
        P("section", None, None, "dp"),
        P("section", None, "dp", None),
    )
    return jax.shard_map(body, mesh=mesh, in_specs=in_specs, out_specs=out_specs, check_vma=False)
```

```python
import functools
import math

import jax
import jax.numpy as jnp
from jax import lax
from jax.experimental import pallas as pl
from jax.experimental.pallas import tpu as pltpu
from jax.sharding import PartitionSpec as P

HEAD_DIM = 128
LATENTS = 64
CHUNK = 16
CHUNK2 = 16
NORM_ROWS = 16
TOP_ROWS = 32
OWNERS = 4
GROUP = 8
ADAM_ROWS = 64
WG_ROWS = 256
F32 = jnp.float32
BF16 = jnp.bfloat16
MESH = pl.DeviceIdType.MESH


def dot_nt(a, b):
    return lax.dot_general(a, b, (((1,), (1,)), ((), ())), preferred_element_type=F32)


def dot_tn(a, b):
    return lax.dot_general(a, b, (((0,), (0,)), ((), ())), preferred_element_type=F32)


def dot_nn(a, b):
    return jnp.dot(a, b, preferred_element_type=F32)


def kernel(
    n_sec, n_dp,
    hid_hbm, key_hbm, val_hbm, lat_hbm, nl_hbm, media_ref, cot_hbm, gate_ref, w_hbm, mf_hbm, ms_hbm,
    ig_hbm, nw_hbm, kv_hbm,
    hid, keys, vals, lat, inc, inc2, q, p, go, gs, sbuf, gpbuf, gbuf, rinv, coef, maskf,
    lt_all, nl_all, snd, rcv, wts, mf, ms, grads, wlow, kvs, fwd,
    in_sem, out_sem, r1_send, r1_recv, r2_send, r2_recv,
    f_send, gat_send, gat_recv, a2a_send, a2a_recv, kv_send, kv_recv, loc_sem,
):
    sec, me = lax.axis_index("section"), lax.axis_index("dp")
    micro, block, width = hid_hbm.shape
    span = key_hbm.shape[2]
    rows_m = key_hbm.shape[1]
    lat_w = lat_hbm.shape[2]
    cols_d = w_hbm.shape[2]
    heads = span // HEAD_DIM
    heads_d = cols_d // HEAD_DIM
    tokens = micro * block
    n_chunks = tokens // CHUNK
    per_micro = n_chunks // micro
    n_chunks2 = tokens // CHUNK2
    n_y = n_dp // 4
    scale = 1.0 / math.sqrt(HEAD_DIM)
    core = lax.rem(me, 2)
    x_lo = lax.rem(me // 2, 2)
    y_at = me // 4
    top = sec == n_sec - 1
    mid_at = n_sec // 2
    early = sec < mid_at
    detour = mid_at < n_sec - 1
    mid = jnp.logical_and(sec == mid_at, detour)

    def dp_dev(j):
        return (sec, j)

    barrier = pltpu.get_barrier_semaphore()

    @pl.loop(1, n_dp)
    def _(k):
        pl.semaphore_signal(barrier, inc=1, device_id=dp_dev(lax.rem(me + k, n_dp)), device_id_type=MESH)

    @pl.when(sec > 0)
    def _():
        pl.semaphore_signal(barrier, inc=1, device_id=(sec - 1, me), device_id_type=MESH)

    @pl.when(sec < n_sec - 1)
    def _():
        pl.semaphore_signal(barrier, inc=1, device_id=(sec + 1, me), device_id_type=MESH)

    def ring_pairs(do):
        if detour:
            for one, two in ((mid_at, n_sec - 1), (n_sec - 1, mid_at - 1)):
                if one - two != 1 and two - one != 1:
                    for a, b in ((one, two), (two, one)):
                        do(a, b)

    def greet(a, b):
        @pl.when(sec == a)
        def _():
            pl.semaphore_signal(barrier, inc=1, device_id=(b, me), device_id_type=MESH)

    ring_pairs(greet)

    def load(i, src, dst):
        return pltpu.make_async_copy(src, dst, in_sem.at[i])

    hid_loads = [load(m, hid_hbm.at[m], hid.at[pl.ds(m * block, block), :]) for m in range(micro)]
    key_loads = [load(2 + m, key_hbm.at[m], keys.at[m]) for m in range(micro)]
    val_loads = [load(4 + m, val_hbm.at[m], vals.at[m]) for m in range(micro)]
    lat_load = load(6, lat_hbm, lat)
    nl_load = load(7, nl_hbm, nl_all.at[pl.ds(me * block, block), :])
    w_load, mf_load, ms_load = load(8, w_hbm, wts), load(9, mf_hbm, mf), load(10, ms_hbm, ms)
    cot_loads = [load(11 + m, cot_hbm.at[m, :, pl.ds(0, span)], inc.at[pl.ds(m * block, block), :]) for m in range(micro)]
    cot2_loads = [
        load(13 + m, cot_hbm.at[m, :, pl.ds(span, width - span)], inc2.at[pl.ds(m * block, block), :])
        for m in range(micro)
    ]
    lat_load.start()
    nl_load.start()
    hid_loads[0].start()
    key_loads[0].start()

    @pl.when(top)
    def _():
        for c in cot_loads:
            c.start()

    val_loads[0].start()
    for c in (hid_loads[1], key_loads[1], val_loads[1], w_load, mf_load, ms_load):
        c.start()

    @pl.when(top)
    def _():
        for c in cot2_loads:
            c.start()

    for m in range(micro):
        row = media_ref[pl.ds(m, 1), :].astype(F32)
        maskf[m] = jnp.transpose(jnp.broadcast_to(row, (block, block)))
    lat_load.wait()
    nl_load.wait()
    my_rows = pl.ds(pl.multiple_of(me * rows_m, rows_m), rows_m)
    for m in range(micro):
        lt_all[m, :, my_rows] = jnp.transpose(lat[m].astype(F32)).astype(BF16)

    def prepare(m, start, count):
        @pl.loop(0, count // NORM_ROWS)
        def _(t):
            rows = pl.ds(pl.multiple_of(m * block + start + t * NORM_ROWS, NORM_ROWS), NORM_ROWS)
            total = jnp.zeros((NORM_ROWS, 128), F32)
            for c in range(width // 128):
                h = hid[rows, pl.ds(c * 128, 128)].astype(F32)
                total = total + h * h
            mean = jnp.sum(total, axis=1, keepdims=True) * (1.0 / width)
            r = jnp.broadcast_to(1.0 / jnp.sqrt(mean + 1e-06), (NORM_ROWS, 128))
            rinv[rows, :] = r
            for c in range(heads):
                cols = pl.ds(c * 128, 128)
                q[rows, cols] = (hid[rows, cols].astype(F32) * r).astype(BF16)

        rows = pl.ds(pl.multiple_of(m * block + start, count), count)
        half = lax.broadcasted_iota(jnp.int32, (count, rows_m), 1) // LATENTS
        allowed = half.astype(F32) == maskf[m, pl.ds(pl.multiple_of(start, count), count), :]

        @pl.loop(0, heads // GROUP)
        def _(hg):
            for j in range(GROUP):
                cols = pl.ds(pl.multiple_of((hg * GROUP + j) * 128, 128), 128)
                sbuf[pl.ds(0, count), pl.ds(j * 128, 128)] = dot_nt(q[rows, cols], keys[m, :, cols])
            for j in range(GROUP):
                cols = pl.ds(pl.multiple_of((hg * GROUP + j) * 128, 128), 128)
                s = jnp.where(allowed, sbuf[pl.ds(0, count), pl.ds(j * 128, 128)] * scale, -1e30)
                e = jnp.exp(s - jnp.max(s, axis=1, keepdims=True))
                p[rows, cols] = e / jnp.sum(e, axis=1, keepdims=True)

    @pl.when(top)
    def _():
        hid_loads[0].wait()
        key_loads[0].wait()
        prepare(0, 0, TOP_ROWS)

    others = jnp.where(sec > 0, 1, 0) + jnp.where(sec < n_sec - 1, 1, 0) + n_dp - 1
    extra = [others]

    def expect(a, b):
        extra[0] = extra[0] + jnp.where(sec == a, 1, 0)

    ring_pairs(expect)
    pl.semaphore_wait(barrier, extra[0])

    def gather_copy(slot, owner, target):
        at = pl.ds(pl.multiple_of(owner * rows_m, rows_m), rows_m)
        ref_l = lt_all.at[:, :, at]
        ref_n = nl_all.at[at, :]
        return [
            pltpu.make_async_remote_copy(
                src_ref=ref, dst_ref=ref, send_sem=gat_send.at[i, slot], recv_sem=gat_recv.at[i, owner],
                device_id=dp_dev(target), device_id_type=MESH,
            )
            for i, ref in enumerate((ref_l, ref_n))
        ]

    def gather_start(slot, owner, target):
        for c in gather_copy(slot, owner, target):
            c.start()

    def gather_wait_recv(owner):
        for c in gather_copy(0, owner, me):
            c.wait_recv()

    def gather_wait_send(slot):
        for c in gather_copy(slot, me, me):
            c.wait_send()

    x_peer = me + 2 - 4 * x_lo
    core_peer = me + 1 - 2 * core

    def y_peer(dy):
        return lax.rem(y_at + dy, n_y) * 4 + x_lo * 2 + core

    def beside(j):
        return j + 2 - 4 * x_lo

    near = sorted({1, n_y - 1} - {0})
    far = [2] if n_y == 4 else []

    gather_start(0, me, x_peer)
    for dy in near:
        gather_start(dy, me, y_peer(dy))

    def gather_second():
        gather_wait_recv(x_peer)
        for dy in near:
            gather_start(n_y - 1 + dy, x_peer, y_peer(dy))

    def gather_core(owner):
        gather_start(2 * n_y - 1 + owner // 2, owner, core_peer)

    def gather_third():
        for dy in near:
            gather_wait_recv(y_peer(dy))
            gather_wait_recv(beside(y_peer(dy)))
        for dy in far:
            gather_start(dy, y_peer(n_y - 1), y_peer(1))
            gather_start(n_y - 1 + dy, beside(y_peer(1)), y_peer(n_y - 1))
        for owner in [me, x_peer] + [y_peer(dy) for dy in near] + [beside(y_peer(dy)) for dy in near]:
            gather_core(owner)

    def gather_fourth():
        for dy in far:
            for owner in (y_peer(dy), beside(y_peer(dy))):
                gather_wait_recv(owner)
                gather_core(owner)

    def transpose_values(m):
        @pl.loop(0, heads // 4)
        def _(hg):
            for j in range(4):
                cols = pl.ds(pl.multiple_of((hg * 4 + j) * 128, 128), 128)
                vals[m, :, cols] = jnp.transpose(vals[m, :, cols])

    def relay1(c):
        rows = pl.ds(pl.multiple_of(c * CHUNK, CHUNK), CHUNK)
        return pltpu.make_async_remote_copy(
            src_ref=inc.at[rows, :], dst_ref=inc.at[rows, :], send_sem=r1_send.at[c], recv_sem=r1_recv.at[c],
            device_id=(jnp.maximum(sec - 1, 0), me), device_id_type=MESH,
        )

    def relay2(c, dst=inc2, to=None):
        rows = pl.ds(pl.multiple_of(c * CHUNK2, CHUNK2), CHUNK2)
        return pltpu.make_async_remote_copy(
            src_ref=inc2.at[rows, :], dst_ref=dst.at[rows, :], send_sem=r2_send.at[c], recv_sem=r2_recv.at[c],
            device_id=(jnp.maximum(sec - 1, 0) if to is None else to, me), device_id_type=MESH,
        )

    def forward2(c):
        rows = pl.ds(pl.multiple_of(c * CHUNK2, CHUNK2), CHUNK2)
        return pltpu.make_async_remote_copy(
            src_ref=fwd.at[rows, :], dst_ref=inc2.at[rows, :], send_sem=f_send.at[c], recv_sem=r2_recv.at[c],
            device_id=(mid_at - 1, me), device_id_type=MESH,
        )

    gate_tanh = jnp.tanh(jnp.broadcast_to(gate_ref[...], (CHUNK, 128)))

    def chain_step(c, dot_values):
        m = c // per_micro
        rows = pl.ds(pl.multiple_of(c * CHUNK, CHUNK), CHUNK)
        for h in range(heads):
            cols = pl.ds(h * 128, 128)
            g = (gate_tanh * inc[rows, cols].astype(F32)).astype(BF16)
            go[rows, cols] = g
            gpbuf[:, cols] = dot_values(g, vals[m, :, cols])
        for h in range(heads):
            cols = pl.ds(h * 128, 128)
            pr, gp = p[rows, cols], gpbuf[:, cols]
            weighted = jnp.sum(pr * gp, axis=1, keepdims=True)
            gs[rows, cols] = (pr * (gp - weighted)).astype(BF16)
        acc = jnp.zeros((CHUNK, 128), F32)
        for h in range(heads):
            cols = pl.ds(h * 128, 128)
            gk = dot_nn(gs[rows, cols], keys[m, :, cols])
            gbuf[:, cols] = gk
            acc = acc + gk * hid[rows, cols].astype(F32)
        r = rinv[rows, :]
        dots = jnp.sum(acc, axis=1, keepdims=True)
        a = r * scale
        b = r * r * r * (dots * (scale / width))
        coef[rows, :] = b
        for h in range(heads):
            cols = pl.ds(h * 128, 128)
            new = inc[rows, cols].astype(F32) + (a * gbuf[:, cols] - b * hid[rows, cols].astype(F32))
            inc[rows, cols] = new.astype(BF16)

    def second_step(c):
        @pl.when(jnp.logical_not(top))
        def _():
            relay2(c).wait_recv()

        for t in range(CHUNK2 // 16):
            rows = pl.ds(pl.multiple_of(c * CHUNK2 + t * 16, 16), 16)
            b = coef[rows, :]
            for h in range((width - span) // 128):
                cols, hcols = pl.ds(h * 128, 128), pl.ds(span + h * 128, 128)
                inc2[rows, cols] = (inc2[rows, cols].astype(F32) - b * hid[rows, hcols].astype(F32)).astype(BF16)

        @pl.when(jnp.logical_and(sec > 0, jnp.logical_not(mid)))
        def _():
            relay2(c).start()

        if detour:
            @pl.when(mid)
            def _():
                relay2(c, fwd, n_sec - 1).start()

    def a2a_copy(m, kind, j):
        return pltpu.make_async_remote_copy(
            src_ref=snd.at[m, j, kind], dst_ref=rcv.at[m, kind, my_rows, :], send_sem=a2a_send.at[m, kind, j],
            recv_sem=a2a_recv.at[m, kind, me], device_id=dp_dev(j), device_id_type=MESH,
        )

    def a2a_in(m, kind, j):
        at = pl.ds(pl.multiple_of(j * rows_m, rows_m), rows_m)
        return pltpu.make_async_remote_copy(
            src_ref=snd.at[m, j, kind], dst_ref=rcv.at[m, kind, at, :], send_sem=a2a_send.at[m, kind, j],
            recv_sem=a2a_recv.at[m, kind, j], device_id=dp_dev(j), device_id_type=MESH,
        )

    def a2a_own(m, kind):
        return pltpu.make_async_copy(snd.at[m, me, kind], rcv.at[m, kind, my_rows, :], loc_sem.at[m, kind])

    def owner_at(g, i):
        if n_y == 4 and OWNERS == 4:
            odd, high = lax.rem(g, 2), g // 2
            dy = (2 * g + 1, 15 - 2 * g, 2, 0)[i]
            dx = (0, 1, 1 - odd, 1 - high)[i]
            dc = (high, 1 - high, lax.rem(odd + high, 2), 1 - odd)[i]
            return lax.rem(y_at + dy, 4) * 4 + lax.rem(x_lo + dx, 2) * 2 + lax.rem(core + dc, 2)
        return lax.rem(me + 1 + OWNERS * g + i, n_dp)

    def project(m, kinds, g):
        owners = [owner_at(g, i) for i in range(OWNERS)]
        for kind in kinds:
            project_compute(m, kind, owners)
        for i, j in enumerate(owners):
            for kind in kinds:
                own = OWNERS * g + i == n_dp - 1

                @pl.when(jnp.logical_not(own))
                def _():
                    a2a_copy(m, kind, j).start()

                @pl.when(own)
                def _():
                    a2a_own(m, kind).start()

    def project_compute(m, kind, owners):
        rows = pl.ds(pl.multiple_of(m * block, block), block)
        outs = []
        for j in owners:
            for i in range(heads_d):
                cols = pl.ds(pl.multiple_of(j * cols_d + i * 128, 128), 128)
                if kind == 0:
                    out = dot_tn(gs[rows, cols], q[rows, cols]) * scale
                else:
                    out = dot_tn(p[rows, cols].astype(BF16), go[rows, cols])
                outs.append((j, i, out.astype(BF16)))
        for j, i, out in outs:
            snd[m, j, kind, :, pl.ds(i * 128, 128)] = out

    def a2a_wait(m, kind):
        a2a_own(m, kind).wait()

        @pl.loop(1, n_dp)
        def _(k):
            a2a_in(m, kind, lax.rem(me + k, n_dp)).wait_recv()

    def weight_grad(m, kind):
        tile = WG_ROWS

        @pl.loop(0, lat_w // tile)
        def _(t):
            at = pl.ds(pl.multiple_of(t * tile, tile), tile)
            part = dot_nn(lt_all[m, at, :], rcv[m, kind])
            if m == 0:
                grads[kind, at, :] = part
            else:
                grads[kind, at, :] += part

    def adam(i):
        @pl.loop(0, lat_w // ADAM_ROWS)
        def _(t):
            at = pl.ds(pl.multiple_of(t * ADAM_ROWS, ADAM_ROWS), ADAM_ROWS)
            g = grads[i, at, :]
            cur = wts[i, at, :]
            first = 0.9 * mf[i, at, :] + 0.1 * g
            second = 0.95 * ms[i, at, :] + 0.05 * g * g
            new = cur - 0.02 * (first / (jnp.sqrt(second) + 1e-08) + 0.1 * cur)
            wts[i, at, :] = new
            wlow[i, at, :] = new.astype(BF16)

    my_cols = pl.ds(pl.multiple_of(me * cols_d, cols_d), cols_d)

    def kv_copy(kind, j, source):
        cols = pl.ds(pl.multiple_of(source * cols_d, cols_d), cols_d)
        return pltpu.make_async_remote_copy(
            src_ref=kvs.at[kind, j], dst_ref=kv_hbm.at[kind, :, cols], send_sem=kv_send.at[kind, j],
            recv_sem=kv_recv.at[kind, source], device_id=dp_dev(j), device_id_type=MESH,
        )

    def kv_own(kind):
        return pltpu.make_async_copy(kvs.at[kind, me], kv_hbm.at[kind, :, my_cols], loc_sem.at[2, kind])

    def next_rows(kind, send):
        @pl.loop(0, n_dp // 2)
        def _(k):
            pair = lax.rem(me // 2 + 1 + k, n_dp // 2)
            at = pl.ds(pl.multiple_of(pair * 2 * block, 2 * block), 2 * block)
            out = dot_nn(nl_all[at, :], wlow[kind]).astype(BF16)
            for i in range(2):
                kvs[kind, 2 * pair + i] = out[i * block : (i + 1) * block, :]
            if send:
                send_rows(kind, k)

    def send_rows(kind, k):
        pair = lax.rem(me // 2 + 1 + k, n_dp // 2)

        @pl.when(k < n_dp // 2 - 1)
        def _():
            for i in range(2):
                kv_copy(kind, 2 * pair + i, me).start()

        @pl.when(k == n_dp // 2 - 1)
        def _():
            kv_copy(kind, core_peer, me).start()
            kv_own(kind).start()

    def out_weights(kind):
        return pltpu.make_async_copy(wts.at[kind], nw_hbm.at[kind], out_sem.at[2 * micro + kind])

    def update_kind(kind):
        a2a_wait(1, kind)
        weight_grad(1, kind)
        adam(kind)
        out_weights(kind).start()

    def finish_kind(kind):
        update_kind(kind)
        next_rows(kind, True)

    @pl.when(jnp.logical_not(top))
    def _():
        hid_loads[0].wait()
        key_loads[0].wait()
        prepare(0, 0, block)

    val_loads[0].wait()

    def wait_rest():
        for c in (hid_loads[1:], key_loads[1:], val_loads[1:]):
            for d in c:
                d.wait()

    @pl.when(jnp.logical_not(top))
    def _():
        wait_rest()
        prepare(1, 0, block)
        for m in range(micro):
            transpose_values(m)

    @pl.when(top)
    def _():
        cot_loads[0].wait()

    soon = sec < n_sec - 2

    @pl.when(soon)
    def _():
        gather_second()

    together = TOP_ROWS // CHUNK

    @pl.loop(0, n_chunks)
    def _(c):
        @pl.when(jnp.logical_and(c == per_micro // 2, jnp.logical_not(soon)))
        def _():
            gather_second()

        third_at = jnp.where(early, per_micro // 2, per_micro + per_micro // 2)

        @pl.when(jnp.logical_and(c == third_at, jnp.logical_not(top)))
        def _():
            gather_third()

        @pl.when(jnp.logical_and(c == per_micro + per_micro // 2, early))
        def _():
            gather_fourth()

        @pl.when(top)
        def _():
            @pl.when(c == per_micro)
            def _():
                wait_rest()
                for d in cot_loads[1:]:
                    d.wait()

            @pl.when(jnp.logical_and(lax.rem(c, together) == 0, c > 0))
            def _():
                prepare(c // per_micro, lax.rem(c, per_micro) * CHUNK, TOP_ROWS)

            chain_step(c, dot_nt)

        @pl.when(jnp.logical_not(top))
        def _():
            relay1(c).wait_recv()
            chain_step(c, dot_nn)

        @pl.when(sec > 0)
        def _():
            relay1(c).start()

        project_now = jnp.logical_and(c >= per_micro, c < per_micro + n_dp // OWNERS)

        @pl.when(jnp.logical_and(project_now, jnp.logical_not(mid)))
        def _():
            project(0, (1, 0), c - per_micro)

    out_first = [
        pltpu.make_async_copy(inc.at[pl.ds(m * block, block), :], ig_hbm.at[m, :, pl.ds(0, span)], out_sem.at[m])
        for m in range(micro)
    ]
    for c in out_first:
        c.start()

    @pl.when(mid)
    def _():
        @pl.loop(0, n_dp // OWNERS)
        def _(k):
            project(0, (1, 0), k)

    for kind in (1, 0):
        @pl.loop(0, n_dp // OWNERS)
        def _(k):
            project(1, (kind,), k)

    @pl.when(top)
    def _():
        for c in cot2_loads:
            c.wait()

    def second_steps(first, last):
        @pl.loop(first, last)
        def _(c):
            second_step(c)

    def forward_steps(first, last):
        if detour:
            @pl.when(top)
            def _():
                @pl.loop(first, last)
                def _(c):
                    relay2(c, fwd, mid_at).wait_recv()
                    forward2(c).start()

    def upto(late_at, early_at):
        return jnp.where(top, n_chunks2, jnp.where(early, early_at, late_at) * n_chunks2 // 16)

    stops = [0, upto(7, 0), upto(13, 1), upto(16, 3), upto(16, 7), n_chunks2]
    second_steps(stops[0], stops[1])

    @pl.when(top)
    def _():
        gather_third()

    forward_steps(0, n_chunks2 // 4)

    @pl.when(jnp.logical_not(early))
    def _():
        gather_fourth()

    second_steps(stops[1], stops[2])
    half = n_chunks2 // 2
    forward_steps(n_chunks2 // 4, half)

    @pl.loop(0, n_dp // 2)
    def _(k):
        gather_wait_recv(2 * k + 1 - core)

    for c in (w_load, mf_load, ms_load):
        c.wait()

    def part_grads(kind):
        a2a_wait(0, kind)
        weight_grad(0, kind)

    @pl.when(top)
    def _():
        pieces = [
            lambda: part_grads(1),
            lambda: part_grads(0),
            lambda: update_kind(1),
            lambda: next_rows(1, False),
            lambda: update_kind(0),
            lambda: next_rows(0, False),
        ]
        left = n_chunks2 - half
        for i, piece in enumerate(pieces):
            forward_steps(half + i * left // len(pieces), half + (i + 1) * left // len(pieces))
            piece()
        for kind in (1, 0):
            @pl.loop(0, n_dp // 2)
            def _(k):
                send_rows(kind, k)

    @pl.when(jnp.logical_not(top))
    def _():
        part_grads(1)
        part_grads(0)
        second_steps(stops[2], stops[3])
        finish_kind(1)
        second_steps(stops[3], stops[4])
        finish_kind(0)
        second_steps(stops[4], stops[5])

    out_second = [
        pltpu.make_async_copy(inc2.at[pl.ds(m * block, block), :], ig_hbm.at[m, :, pl.ds(span, width - span)], out_sem.at[micro + m])
        for m in range(micro)
    ]
    for c in out_second:
        c.start()

    @pl.when(sec > 0)
    def _():
        @pl.loop(0, n_chunks)
        def _(c):
            relay1(c).wait_send()

        @pl.loop(0, n_chunks2)
        def _(c):
            relay2(c).wait_send()

    @pl.loop(0, 2 * n_y - 1 + n_dp // 2)
    def _(k):
        gather_wait_send(k)

    if detour:
        @pl.when(top)
        def _():
            @pl.loop(0, n_chunks2)
            def _(c):
                forward2(c).wait_send()

    @pl.loop(1, n_dp)
    def _(k):
        j = lax.rem(me + k, n_dp)
        for kind in range(2):
            for m in range(micro):
                a2a_copy(m, kind, j).wait_send()
            kv_copy(kind, j, me).wait_send()
            kv_copy(kind, j, j).wait_recv()

    for kind in range(2):
        kv_own(kind).wait()
        out_weights(kind).wait()
    for c in out_first + out_second:
        c.wait()


def body(
    hidden_states, key_rows, value_rows, latents, next_latents, media_index, cotangent, gate_alpha,
    weights, moment_first, moment_second,
):
    n_sec, n_dp = lax.axis_size("section"), lax.axis_size("dp")
    _, micro, block, width = hidden_states.shape
    span, rows_m = key_rows.shape[3], key_rows.shape[2]
    lat_w, cols_d = weights.shape[2], weights.shape[3]
    tokens = micro * block
    n_y = n_dp // 4
    n_chunks, n_chunks2 = tokens // CHUNK, tokens // CHUNK2
    any_spec = pl.BlockSpec(memory_space=pl.ANY)
    vmem_spec = pl.BlockSpec(memory_space=pltpu.VMEM)
    dma = pltpu.SemaphoreType.DMA
    vmem = pltpu.VMEM
    grad_in, new_w, kv = pl.pallas_call(
        functools.partial(kernel, n_sec, n_dp),
        out_shape=(
            jax.ShapeDtypeStruct((micro, block, width), BF16),
            jax.ShapeDtypeStruct((2, lat_w, cols_d), F32),
            jax.ShapeDtypeStruct((2, rows_m, span), BF16),
        ),
        in_specs=[any_spec] * 5 + [vmem_spec, any_spec, vmem_spec] + [any_spec] * 3,
        out_specs=(any_spec, any_spec, any_spec),
        scratch_shapes=[
            vmem((tokens, width), BF16),
            vmem((micro, rows_m, span), BF16),
            vmem((micro, rows_m, span), BF16),
            vmem((micro, rows_m, lat_w), BF16),
            vmem((tokens, span), BF16),
            vmem((tokens, width - span), BF16),
            vmem((tokens, span), BF16),
            vmem((tokens, span), F32),
            vmem((tokens, span), BF16),
            vmem((tokens, span), BF16),
            vmem((block, GROUP * 128), F32),
            vmem((CHUNK, span), F32),
            vmem((CHUNK, span), F32),
            vmem((tokens, 128), F32),
            vmem((tokens, 128), F32),
            vmem((micro, block, rows_m), F32),
            vmem((micro, lat_w, n_dp * rows_m), BF16),
            vmem((n_dp * block, lat_w), BF16),
            vmem((micro, n_dp, 2, rows_m, cols_d), BF16),
            vmem((micro, 2, n_dp * rows_m, cols_d), BF16),
            vmem((2, lat_w, cols_d), F32),
            vmem((2, lat_w, cols_d), F32),
            vmem((2, lat_w, cols_d), F32),
            vmem((2, lat_w, cols_d), F32),
            vmem((2, lat_w, cols_d), BF16),
            vmem((2, n_dp, block, cols_d), BF16),
            vmem((tokens, width - span), BF16),
            dma((15,)),
            dma((2 * micro + 2,)),
            dma((n_chunks,)),
            dma((n_chunks,)),
            dma((n_chunks2,)),
            dma((n_chunks2,)),
            dma((n_chunks2,)),
            dma((2, 2 * n_y - 1 + n_dp // 2)),
            dma((2, n_dp)),
            dma((micro, 2, n_dp)),
            dma((micro, 2, n_dp)),
            dma((2, n_dp)),
            dma((2, n_dp)),
            dma((3, 2)),
        ],
        compiler_params=pltpu.CompilerParams(
            collective_id=0, has_side_effects=True, vmem_limit_bytes=62 * 1024 * 1024
        ),
    )(
        hidden_states[0], key_rows[0], value_rows[0], latents, next_latents, media_index, cotangent,
        gate_alpha.reshape(1, 1), weights[0], moment_first[0], moment_second[0],
    )
    return grad_in[None], new_w[None], kv[None]


def solution(mesh):
    in_specs = (
        P("section", None, "dp", None),
        P("section", None, "dp", None),
        P("section", None, "dp", None),
        P(None, "dp", None),
        P("dp", None),
        P(None, "dp"),
        P(None, "dp", None),
        P("section"),
        P("section", None, None, "dp"),
        P("section", None, None, "dp"),
        P("section", None, None, "dp"),
    )
    out_specs = (
        P("section", None, "dp", None),
        P("section", None, None, "dp"),
        P("section", None, "dp", None),
    )
    return jax.shard_map(body, mesh=mesh, in_specs=in_specs, out_specs=out_specs, check_vma=False)
```

```python
import functools
import math

import jax
import jax.numpy as jnp
from jax import lax
from jax.experimental import pallas as pl
from jax.experimental.pallas import tpu as pltpu
from jax.sharding import PartitionSpec as P

HEAD_DIM = 128
LATENTS = 64
CHUNK = 16
CHUNK2 = 16
NORM_ROWS = 16
TOP_ROWS = 32
OWNERS = 4
GROUP = 8
ADAM_ROWS = 64
WG_ROWS = 256
LIMIT = 54 * 1024 * 1024
F32 = jnp.float32
BF16 = jnp.bfloat16
MESH = pl.DeviceIdType.MESH


def dot_nt(a, b):
    return lax.dot_general(a, b, (((1,), (1,)), ((), ())), preferred_element_type=F32)


def dot_tn(a, b):
    return lax.dot_general(a, b, (((0,), (0,)), ((), ())), preferred_element_type=F32)


def dot_nn(a, b):
    return jnp.dot(a, b, preferred_element_type=F32)


def kernel(
    n_sec, n_dp,
    hid_hbm, key_hbm, val_hbm, lat_hbm, nl_hbm, media_ref, cot_hbm, gate_ref, w_hbm, mf_hbm, ms_hbm,
    inc, inc2, wts, kv,
    hid, keys, vals, lat, q, p, go, gs, sbuf, gpbuf, gbuf, rinv, coef, maskf,
    lt_all, nl_all, snd, rcv, mf, ms, grads, wlow, kvs, fwd,
    in_sem, r1_send, r1_recv, r2_send, r2_recv,
    f_send, gat_send, gat_recv, a2a_send, a2a_recv, kv_send, kv_recv, loc_sem,
):
    sec, me = lax.axis_index("section"), lax.axis_index("dp")
    micro, block, width = hid_hbm.shape
    span = key_hbm.shape[2]
    rows_m = key_hbm.shape[1]
    lat_w = lat_hbm.shape[2]
    cols_d = w_hbm.shape[2]
    heads = span // HEAD_DIM
    heads_d = cols_d // HEAD_DIM
    tokens = micro * block
    n_chunks = tokens // CHUNK
    per_micro = n_chunks // micro
    n_chunks2 = tokens // CHUNK2
    n_y = n_dp // 4
    scale = 1.0 / math.sqrt(HEAD_DIM)
    core = lax.rem(me, 2)
    x_lo = lax.rem(me // 2, 2)
    y_at = me // 4
    top = sec == n_sec - 1
    mid_at = n_sec // 2
    early = sec < mid_at
    detour = mid_at < n_sec - 1
    mid = jnp.logical_and(sec == mid_at, detour)

    def dp_dev(j):
        return (sec, j)

    barrier = pltpu.get_barrier_semaphore()

    @pl.loop(1, n_dp)
    def _(k):
        pl.semaphore_signal(barrier, inc=1, device_id=dp_dev(lax.rem(me + k, n_dp)), device_id_type=MESH)

    @pl.when(sec > 0)
    def _():
        pl.semaphore_signal(barrier, inc=1, device_id=(sec - 1, me), device_id_type=MESH)

    @pl.when(sec < n_sec - 1)
    def _():
        pl.semaphore_signal(barrier, inc=1, device_id=(sec + 1, me), device_id_type=MESH)

    def ring_pairs(do):
        if detour:
            for one, two in ((mid_at, n_sec - 1), (n_sec - 1, mid_at - 1)):
                if one - two != 1 and two - one != 1:
                    for a, b in ((one, two), (two, one)):
                        do(a, b)

    def greet(a, b):
        @pl.when(sec == a)
        def _():
            pl.semaphore_signal(barrier, inc=1, device_id=(b, me), device_id_type=MESH)

    ring_pairs(greet)

    def load(i, src, dst):
        return pltpu.make_async_copy(src, dst, in_sem.at[i])

    hid_loads = [load(m, hid_hbm.at[m], hid.at[pl.ds(m * block, block), :]) for m in range(micro)]
    key_loads = [load(2 + m, key_hbm.at[m], keys.at[m]) for m in range(micro)]
    val_loads = [load(4 + m, val_hbm.at[m], vals.at[m]) for m in range(micro)]
    lat_load = load(6, lat_hbm, lat)
    nl_load = load(7, nl_hbm, nl_all.at[pl.ds(me * block, block), :])
    w_load, mf_load, ms_load = load(8, w_hbm, wts), load(9, mf_hbm, mf), load(10, ms_hbm, ms)
    cot_loads = [load(11 + m, cot_hbm.at[m, :, pl.ds(0, span)], inc.at[pl.ds(m * block, block), :]) for m in range(micro)]
    cot2_loads = [
        load(13 + m, cot_hbm.at[m, :, pl.ds(span, width - span)], inc2.at[pl.ds(m * block, block), :])
        for m in range(micro)
    ]
    lat_load.start()
    nl_load.start()
    hid_loads[0].start()
    key_loads[0].start()

    @pl.when(top)
    def _():
        for c in cot_loads:
            c.start()

    val_loads[0].start()
    for c in (hid_loads[1], key_loads[1], val_loads[1], w_load, mf_load, ms_load):
        c.start()

    @pl.when(top)
    def _():
        for c in cot2_loads:
            c.start()

    for m in range(micro):
        row = media_ref[pl.ds(m, 1), :].astype(F32)
        maskf[m] = jnp.transpose(jnp.broadcast_to(row, (block, block)))
    lat_load.wait()
    nl_load.wait()
    my_rows = pl.ds(pl.multiple_of(me * rows_m, rows_m), rows_m)
    for m in range(micro):
        lt_all[m, :, my_rows] = jnp.transpose(lat[m].astype(F32)).astype(BF16)

    def prepare(m, start, count):
        @pl.loop(0, count // NORM_ROWS)
        def _(t):
            rows = pl.ds(pl.multiple_of(m * block + start + t * NORM_ROWS, NORM_ROWS), NORM_ROWS)
            total = jnp.zeros((NORM_ROWS, 128), F32)
            for c in range(width // 128):
                h = hid[rows, pl.ds(c * 128, 128)].astype(F32)
                total = total + h * h
            mean = jnp.sum(total, axis=1, keepdims=True) * (1.0 / width)
            r = jnp.broadcast_to(1.0 / jnp.sqrt(mean + 1e-06), (NORM_ROWS, 128))
            rinv[rows, :] = r
            for c in range(heads):
                cols = pl.ds(c * 128, 128)
                q[rows, cols] = (hid[rows, cols].astype(F32) * r).astype(BF16)

        rows = pl.ds(pl.multiple_of(m * block + start, count), count)
        half = lax.broadcasted_iota(jnp.int32, (count, rows_m), 1) // LATENTS
        allowed = half.astype(F32) == maskf[m, pl.ds(pl.multiple_of(start, count), count), :]

        @pl.loop(0, heads // GROUP)
        def _(hg):
            for j in range(GROUP):
                cols = pl.ds(pl.multiple_of((hg * GROUP + j) * 128, 128), 128)
                sbuf[pl.ds(0, count), pl.ds(j * 128, 128)] = dot_nt(q[rows, cols], keys[m, :, cols])
            for j in range(GROUP):
                cols = pl.ds(pl.multiple_of((hg * GROUP + j) * 128, 128), 128)
                s = jnp.where(allowed, sbuf[pl.ds(0, count), pl.ds(j * 128, 128)] * scale, -1e30)
                e = jnp.exp(s - jnp.max(s, axis=1, keepdims=True))
                p[rows, cols] = e / jnp.sum(e, axis=1, keepdims=True)

    @pl.when(top)
    def _():
        hid_loads[0].wait()
        key_loads[0].wait()
        prepare(0, 0, TOP_ROWS)

    others = jnp.where(sec > 0, 1, 0) + jnp.where(sec < n_sec - 1, 1, 0) + n_dp - 1
    extra = [others]

    def expect(a, b):
        extra[0] = extra[0] + jnp.where(sec == a, 1, 0)

    ring_pairs(expect)
    pl.semaphore_wait(barrier, extra[0])

    def gather_copy(slot, owner, target):
        at = pl.ds(pl.multiple_of(owner * rows_m, rows_m), rows_m)
        ref_l = lt_all.at[:, :, at]
        ref_n = nl_all.at[at, :]
        return [
            pltpu.make_async_remote_copy(
                src_ref=ref, dst_ref=ref, send_sem=gat_send.at[i, slot], recv_sem=gat_recv.at[i, owner],
                device_id=dp_dev(target), device_id_type=MESH,
            )
            for i, ref in enumerate((ref_l, ref_n))
        ]

    def gather_start(slot, owner, target):
        for c in gather_copy(slot, owner, target):
            c.start()

    def gather_wait_recv(owner):
        for c in gather_copy(0, owner, me):
            c.wait_recv()

    def gather_wait_send(slot):
        for c in gather_copy(slot, me, me):
            c.wait_send()

    x_peer = me + 2 - 4 * x_lo
    core_peer = me + 1 - 2 * core

    def y_peer(dy):
        return lax.rem(y_at + dy, n_y) * 4 + x_lo * 2 + core

    def beside(j):
        return j + 2 - 4 * x_lo

    near = sorted({1, n_y - 1} - {0})
    far = [2] if n_y == 4 else []

    gather_start(0, me, x_peer)
    for dy in near:
        gather_start(dy, me, y_peer(dy))

    def gather_second():
        gather_wait_recv(x_peer)
        for dy in near:
            gather_start(n_y - 1 + dy, x_peer, y_peer(dy))

    def gather_core(owner):
        gather_start(2 * n_y - 1 + owner // 2, owner, core_peer)

    def gather_third():
        for dy in near:
            gather_wait_recv(y_peer(dy))
            gather_wait_recv(beside(y_peer(dy)))
        for dy in far:
            gather_start(dy, y_peer(n_y - 1), y_peer(1))
            gather_start(n_y - 1 + dy, beside(y_peer(1)), y_peer(n_y - 1))
        for owner in [me, x_peer] + [y_peer(dy) for dy in near] + [beside(y_peer(dy)) for dy in near]:
            gather_core(owner)

    def gather_fourth():
        for dy in far:
            for owner in (y_peer(dy), beside(y_peer(dy))):
                gather_wait_recv(owner)
                gather_core(owner)

    def transpose_values(m):
        @pl.loop(0, heads // 4)
        def _(hg):
            for j in range(4):
                cols = pl.ds(pl.multiple_of((hg * 4 + j) * 128, 128), 128)
                vals[m, :, cols] = jnp.transpose(vals[m, :, cols])

    def relay1(c):
        rows = pl.ds(pl.multiple_of(c * CHUNK, CHUNK), CHUNK)
        return pltpu.make_async_remote_copy(
            src_ref=inc.at[rows, :], dst_ref=inc.at[rows, :], send_sem=r1_send.at[c], recv_sem=r1_recv.at[c],
            device_id=(jnp.maximum(sec - 1, 0), me), device_id_type=MESH,
        )

    def relay2(c, dst=inc2, to=None):
        rows = pl.ds(pl.multiple_of(c * CHUNK2, CHUNK2), CHUNK2)
        return pltpu.make_async_remote_copy(
            src_ref=inc2.at[rows, :], dst_ref=dst.at[rows, :], send_sem=r2_send.at[c], recv_sem=r2_recv.at[c],
            device_id=(jnp.maximum(sec - 1, 0) if to is None else to, me), device_id_type=MESH,
        )

    def forward2(c):
        rows = pl.ds(pl.multiple_of(c * CHUNK2, CHUNK2), CHUNK2)
        return pltpu.make_async_remote_copy(
            src_ref=fwd.at[rows, :], dst_ref=inc2.at[rows, :], send_sem=f_send.at[c], recv_sem=r2_recv.at[c],
            device_id=(mid_at - 1, me), device_id_type=MESH,
        )

    gate_tanh = jnp.tanh(jnp.broadcast_to(gate_ref[...], (CHUNK, 128)))

    def chain_step(c, dot_values):
        m = c // per_micro
        rows = pl.ds(pl.multiple_of(c * CHUNK, CHUNK), CHUNK)
        for h in range(heads):
            cols = pl.ds(h * 128, 128)
            g = (gate_tanh * inc[rows, cols].astype(F32)).astype(BF16)
            go[rows, cols] = g
            gpbuf[:, cols] = dot_values(g, vals[m, :, cols])
        for h in range(heads):
            cols = pl.ds(h * 128, 128)
            pr, gp = p[rows, cols], gpbuf[:, cols]
            weighted = jnp.sum(pr * gp, axis=1, keepdims=True)
            gs[rows, cols] = (pr * (gp - weighted)).astype(BF16)
        acc = jnp.zeros((CHUNK, 128), F32)
        for h in range(heads):
            cols = pl.ds(h * 128, 128)
            gk = dot_nn(gs[rows, cols], keys[m, :, cols])
            gbuf[:, cols] = gk
            acc = acc + gk * hid[rows, cols].astype(F32)
        r = rinv[rows, :]
        dots = jnp.sum(acc, axis=1, keepdims=True)
        a = r * scale
        b = r * r * r * (dots * (scale / width))
        coef[rows, :] = b
        for h in range(heads):
            cols = pl.ds(h * 128, 128)
            new = inc[rows, cols].astype(F32) + (a * gbuf[:, cols] - b * hid[rows, cols].astype(F32))
            inc[rows, cols] = new.astype(BF16)

    def second_step(c):
        @pl.when(jnp.logical_not(top))
        def _():
            relay2(c).wait_recv()

        for t in range(CHUNK2 // 16):
            rows = pl.ds(pl.multiple_of(c * CHUNK2 + t * 16, 16), 16)
            b = coef[rows, :]
            for h in range((width - span) // 128):
                cols, hcols = pl.ds(h * 128, 128), pl.ds(span + h * 128, 128)
                inc2[rows, cols] = (inc2[rows, cols].astype(F32) - b * hid[rows, hcols].astype(F32)).astype(BF16)

        @pl.when(jnp.logical_and(sec > 0, jnp.logical_not(mid)))
        def _():
            relay2(c).start()

        if detour:
            @pl.when(mid)
            def _():
                relay2(c, fwd, n_sec - 1).start()

    def a2a_copy(m, kind, j):
        return pltpu.make_async_remote_copy(
            src_ref=snd.at[m, j, kind], dst_ref=rcv.at[m, kind, my_rows, :], send_sem=a2a_send.at[m, kind, j],
            recv_sem=a2a_recv.at[m, kind, me], device_id=dp_dev(j), device_id_type=MESH,
        )

    def a2a_in(m, kind, j):
        at = pl.ds(pl.multiple_of(j * rows_m, rows_m), rows_m)
        return pltpu.make_async_remote_copy(
            src_ref=snd.at[m, j, kind], dst_ref=rcv.at[m, kind, at, :], send_sem=a2a_send.at[m, kind, j],
            recv_sem=a2a_recv.at[m, kind, j], device_id=dp_dev(j), device_id_type=MESH,
        )

    def a2a_own(m, kind):
        return pltpu.make_async_copy(snd.at[m, me, kind], rcv.at[m, kind, my_rows, :], loc_sem.at[m, kind])

    def owner_at(g, i):
        if n_y == 4 and OWNERS == 4:
            odd, high = lax.rem(g, 2), g // 2
            dy = (2 * g + 1, 15 - 2 * g, 2, 0)[i]
            dx = (0, 1, 1 - odd, 1 - high)[i]
            dc = (high, 1 - high, lax.rem(odd + high, 2), 1 - odd)[i]
            return lax.rem(y_at + dy, 4) * 4 + lax.rem(x_lo + dx, 2) * 2 + lax.rem(core + dc, 2)
        return lax.rem(me + 1 + OWNERS * g + i, n_dp)

    def project(m, kinds, g):
        owners = [owner_at(g, i) for i in range(OWNERS)]
        for kind in kinds:
            project_compute(m, kind, owners)
        for i, j in enumerate(owners):
            for kind in kinds:
                own = OWNERS * g + i == n_dp - 1

                @pl.when(jnp.logical_not(own))
                def _():
                    a2a_copy(m, kind, j).start()

                @pl.when(own)
                def _():
                    a2a_own(m, kind).start()

    def project_compute(m, kind, owners):
        rows = pl.ds(pl.multiple_of(m * block, block), block)
        outs = []
        for j in owners:
            for i in range(heads_d):
                cols = pl.ds(pl.multiple_of(j * cols_d + i * 128, 128), 128)
                if kind == 0:
                    out = dot_tn(gs[rows, cols], q[rows, cols]) * scale
                else:
                    out = dot_tn(p[rows, cols].astype(BF16), go[rows, cols])
                outs.append((j, i, out.astype(BF16)))
        for j, i, out in outs:
            snd[m, j, kind, :, pl.ds(i * 128, 128)] = out

    def a2a_wait(m, kind):
        a2a_own(m, kind).wait()

        @pl.loop(1, n_dp)
        def _(k):
            a2a_in(m, kind, lax.rem(me + k, n_dp)).wait_recv()

    def weight_grad(m, kind):
        tile = WG_ROWS

        @pl.loop(0, lat_w // tile)
        def _(t):
            at = pl.ds(pl.multiple_of(t * tile, tile), tile)
            part = dot_nn(lt_all[m, at, :], rcv[m, kind])
            if m == 0:
                grads[kind, at, :] = part
            else:
                grads[kind, at, :] += part

    def adam(i):
        @pl.loop(0, lat_w // ADAM_ROWS)
        def _(t):
            at = pl.ds(pl.multiple_of(t * ADAM_ROWS, ADAM_ROWS), ADAM_ROWS)
            g = grads[i, at, :]
            cur = wts[i, at, :]
            first = 0.9 * mf[i, at, :] + 0.1 * g
            second = 0.95 * ms[i, at, :] + 0.05 * g * g
            new = cur - 0.02 * (first / (jnp.sqrt(second) + 1e-08) + 0.1 * cur)
            wts[i, at, :] = new
            wlow[i, at, :] = new.astype(BF16)

    my_cols = pl.ds(pl.multiple_of(me * cols_d, cols_d), cols_d)

    def kv_copy(kind, j, source):
        cols = pl.ds(pl.multiple_of(source * cols_d, cols_d), cols_d)
        return pltpu.make_async_remote_copy(
            src_ref=kvs.at[kind, j], dst_ref=kv.at[kind, :, cols], send_sem=kv_send.at[kind, j],
            recv_sem=kv_recv.at[kind, source], device_id=dp_dev(j), device_id_type=MESH,
        )

    def kv_own(kind):
        return pltpu.make_async_copy(kvs.at[kind, me], kv.at[kind, :, my_cols], loc_sem.at[2, kind])

    def next_rows(kind, send):
        @pl.loop(0, n_dp // 2)
        def _(k):
            pair = lax.rem(me // 2 + 1 + k, n_dp // 2)
            at = pl.ds(pl.multiple_of(pair * 2 * block, 2 * block), 2 * block)
            out = dot_nn(nl_all[at, :], wlow[kind]).astype(BF16)
            for i in range(2):
                kvs[kind, 2 * pair + i] = out[i * block : (i + 1) * block, :]
            if send:
                send_rows(kind, k)

    def send_rows(kind, k):
        pair = lax.rem(me // 2 + 1 + k, n_dp // 2)

        @pl.when(k < n_dp // 2 - 1)
        def _():
            for i in range(2):
                kv_copy(kind, 2 * pair + i, me).start()

        @pl.when(k == n_dp // 2 - 1)
        def _():
            kv_copy(kind, core_peer, me).start()
            kv_own(kind).start()

    def update_kind(kind):
        a2a_wait(1, kind)
        weight_grad(1, kind)
        adam(kind)

    def finish_kind(kind):
        update_kind(kind)
        next_rows(kind, True)

    @pl.when(jnp.logical_not(top))
    def _():
        hid_loads[0].wait()
        key_loads[0].wait()
        prepare(0, 0, block)

    val_loads[0].wait()

    def wait_rest():
        for c in (hid_loads[1:], key_loads[1:], val_loads[1:]):
            for d in c:
                d.wait()

    @pl.when(jnp.logical_not(top))
    def _():
        wait_rest()
        prepare(1, 0, block)
        for m in range(micro):
            transpose_values(m)

    @pl.when(top)
    def _():
        cot_loads[0].wait()

    soon = sec < n_sec - 2

    @pl.when(soon)
    def _():
        gather_second()

    together = TOP_ROWS // CHUNK

    @pl.loop(0, n_chunks)
    def _(c):
        @pl.when(jnp.logical_and(c == per_micro // 2, jnp.logical_not(soon)))
        def _():
            gather_second()

        third_at = jnp.where(early, per_micro // 2, per_micro + per_micro // 2)

        @pl.when(jnp.logical_and(c == third_at, jnp.logical_not(top)))
        def _():
            gather_third()

        @pl.when(jnp.logical_and(c == per_micro + per_micro // 2, early))
        def _():
            gather_fourth()

        @pl.when(top)
        def _():
            @pl.when(c == per_micro)
            def _():
                wait_rest()
                for d in cot_loads[1:]:
                    d.wait()

            @pl.when(jnp.logical_and(lax.rem(c, together) == 0, c > 0))
            def _():
                prepare(c // per_micro, lax.rem(c, per_micro) * CHUNK, TOP_ROWS)

            chain_step(c, dot_nt)

        @pl.when(jnp.logical_not(top))
        def _():
            relay1(c).wait_recv()
            chain_step(c, dot_nn)

        @pl.when(sec > 0)
        def _():
            relay1(c).start()

        project_now = jnp.logical_and(c >= per_micro, c < per_micro + n_dp // OWNERS)

        @pl.when(jnp.logical_and(project_now, jnp.logical_not(mid)))
        def _():
            project(0, (1, 0), c - per_micro)

    @pl.when(mid)
    def _():
        @pl.loop(0, n_dp // OWNERS)
        def _(k):
            project(0, (1, 0), k)

    for kind in (1, 0):
        @pl.loop(0, n_dp // OWNERS)
        def _(k):
            project(1, (kind,), k)

    @pl.when(top)
    def _():
        for c in cot2_loads:
            c.wait()

    def second_steps(first, last):
        @pl.loop(first, last)
        def _(c):
            second_step(c)

    def forward_steps(first, last):
        if detour:
            @pl.when(top)
            def _():
                @pl.loop(first, last)
                def _(c):
                    relay2(c, fwd, mid_at).wait_recv()
                    forward2(c).start()

    def upto(late_at, early_at):
        return jnp.where(top, n_chunks2, jnp.where(early, early_at, late_at) * n_chunks2 // 16)

    stops = [0, upto(7, 0), upto(13, 1), upto(16, 3), upto(16, 7), n_chunks2]
    second_steps(stops[0], stops[1])

    @pl.when(top)
    def _():
        gather_third()

    forward_steps(0, n_chunks2 // 4)

    @pl.when(jnp.logical_not(early))
    def _():
        gather_fourth()

    second_steps(stops[1], stops[2])
    half = n_chunks2 // 2
    forward_steps(n_chunks2 // 4, half)

    @pl.loop(0, n_dp // 2)
    def _(k):
        gather_wait_recv(2 * k + 1 - core)

    for c in (w_load, mf_load, ms_load):
        c.wait()

    def part_grads(kind):
        a2a_wait(0, kind)
        weight_grad(0, kind)

    @pl.when(top)
    def _():
        pieces = [
            lambda: part_grads(1),
            lambda: part_grads(0),
            lambda: update_kind(1),
            lambda: next_rows(1, False),
            lambda: update_kind(0),
            lambda: next_rows(0, False),
        ]
        left = n_chunks2 - half
        for i, piece in enumerate(pieces):
            forward_steps(half + i * left // len(pieces), half + (i + 1) * left // len(pieces))
            piece()
        for kind in (1, 0):
            @pl.loop(0, n_dp // 2)
            def _(k):
                send_rows(kind, k)

    @pl.when(jnp.logical_not(top))
    def _():
        part_grads(1)
        part_grads(0)
        second_steps(stops[2], stops[3])
        finish_kind(1)
        second_steps(stops[3], stops[4])
        finish_kind(0)
        second_steps(stops[4], stops[5])

    @pl.when(sec > 0)
    def _():
        @pl.loop(0, n_chunks)
        def _(c):
            relay1(c).wait_send()

        @pl.loop(0, n_chunks2)
        def _(c):
            relay2(c).wait_send()

    @pl.loop(0, 2 * n_y - 1 + n_dp // 2)
    def _(k):
        gather_wait_send(k)

    if detour:
        @pl.when(top)
        def _():
            @pl.loop(0, n_chunks2)
            def _(c):
                forward2(c).wait_send()

    @pl.loop(1, n_dp)
    def _(k):
        j = lax.rem(me + k, n_dp)
        for kind in range(2):
            for m in range(micro):
                a2a_copy(m, kind, j).wait_send()
            kv_copy(kind, j, me).wait_send()
            kv_copy(kind, j, j).wait_recv()

    for kind in range(2):
        kv_own(kind).wait()


def store(inc, inc2, wts, kv, ig_hbm, nw_hbm, kv_hbm, sem):
    _, micro, block, width = ig_hbm.shape
    span = inc.shape[1]
    pairs = [(wts, nw_hbm.at[0]), (kv, kv_hbm.at[0])]
    for m in range(micro):
        rows = pl.ds(m * block, block)
        pairs.append((inc.at[rows, :], ig_hbm.at[0, m, :, pl.ds(0, span)]))
        pairs.append((inc2.at[rows, :], ig_hbm.at[0, m, :, pl.ds(span, width - span)]))
    copies = [pltpu.make_async_copy(src, dst, sem.at[i]) for i, (src, dst) in enumerate(pairs)]
    for c in copies:
        c.start()
    for c in copies:
        c.wait()


def body(
    hidden_states, key_rows, value_rows, latents, next_latents, media_index, cotangent, gate_alpha,
    weights, moment_first, moment_second,
):
    n_sec, n_dp = lax.axis_size("section"), lax.axis_size("dp")
    _, micro, block, width = hidden_states.shape
    span, rows_m = key_rows.shape[3], key_rows.shape[2]
    lat_w, cols_d = weights.shape[2], weights.shape[3]
    tokens = micro * block
    n_y = n_dp // 4
    n_chunks, n_chunks2 = tokens // CHUNK, tokens // CHUNK2
    any_spec = pl.BlockSpec(memory_space=pl.ANY)
    vmem_spec = pl.BlockSpec(memory_space=pltpu.VMEM)
    dma = pltpu.SemaphoreType.DMA
    vmem = pltpu.VMEM
    held = pl.pallas_call(
        functools.partial(kernel, n_sec, n_dp),
        out_shape=(
            vmem((tokens, span), BF16),
            vmem((tokens, width - span), BF16),
            vmem((2, lat_w, cols_d), F32),
            vmem((2, rows_m, span), BF16),
        ),
        in_specs=[any_spec] * 5 + [vmem_spec, any_spec, vmem_spec] + [any_spec] * 3,
        out_specs=(vmem_spec,) * 4,
        scratch_shapes=[
            vmem((tokens, width), BF16),
            vmem((micro, rows_m, span), BF16),
            vmem((micro, rows_m, span), BF16),
            vmem((micro, rows_m, lat_w), BF16),
            vmem((tokens, span), BF16),
            vmem((tokens, span), F32),
            vmem((tokens, span), BF16),
            vmem((tokens, span), BF16),
            vmem((block, GROUP * 128), F32),
            vmem((CHUNK, span), F32),
            vmem((CHUNK, span), F32),
            vmem((tokens, 128), F32),
            vmem((tokens, 128), F32),
            vmem((micro, block, rows_m), F32),
            vmem((micro, lat_w, n_dp * rows_m), BF16),
            vmem((n_dp * block, lat_w), BF16),
            vmem((micro, n_dp, 2, rows_m, cols_d), BF16),
            vmem((micro, 2, n_dp * rows_m, cols_d), BF16),
            vmem((2, lat_w, cols_d), F32),
            vmem((2, lat_w, cols_d), F32),
            vmem((2, lat_w, cols_d), F32),
            vmem((2, lat_w, cols_d), BF16),
            vmem((2, n_dp, block, cols_d), BF16),
            vmem((tokens, width - span), BF16),
            dma((15,)),
            dma((n_chunks,)),
            dma((n_chunks,)),
            dma((n_chunks2,)),
            dma((n_chunks2,)),
            dma((n_chunks2,)),
            dma((2, 2 * n_y - 1 + n_dp // 2)),
            dma((2, n_dp)),
            dma((micro, 2, n_dp)),
            dma((micro, 2, n_dp)),
            dma((2, n_dp)),
            dma((2, n_dp)),
            dma((3, 2)),
        ],
        compiler_params=pltpu.CompilerParams(
            collective_id=0, has_side_effects=True, vmem_limit_bytes=LIMIT
        ),
    )(
        hidden_states[0], key_rows[0], value_rows[0], latents, next_latents, media_index, cotangent,
        gate_alpha.reshape(1, 1), weights[0], moment_first[0], moment_second[0],
    )
    grad_in, new_w, kv = pl.pallas_call(
        store,
        out_shape=(
            jax.ShapeDtypeStruct((1, micro, block, width), BF16),
            jax.ShapeDtypeStruct((1, 2, lat_w, cols_d), F32),
            jax.ShapeDtypeStruct((1, 2, rows_m, span), BF16),
        ),
        in_specs=[vmem_spec] * 4,
        out_specs=(any_spec, any_spec, any_spec),
        scratch_shapes=[dma((2 + 2 * micro,))],
        compiler_params=pltpu.CompilerParams(vmem_limit_bytes=1024 * 1024),
    )(*held)
    return grad_in, new_w, kv


def solution(mesh):
    in_specs = (
        P("section", None, "dp", None),
        P("section", None, "dp", None),
        P("section", None, "dp", None),
        P(None, "dp", None),
        P("dp", None),
        P(None, "dp"),
        P(None, "dp", None),
        P("section"),
        P("section", None, None, "dp"),
        P("section", None, None, "dp"),
        P("section", None, None, "dp"),
    )
    out_specs = (
        P("section", None, "dp", None),
        P("section", None, None, "dp"),
        P("section", None, "dp", None),
    )
    return jax.shard_map(body, mesh=mesh, in_specs=in_specs, out_specs=out_specs, check_vma=False)
```

```python
import functools
import math

import jax
import jax.numpy as jnp
from jax import lax
from jax.experimental import pallas as pl
from jax.experimental.pallas import tpu as pltpu
from jax.sharding import PartitionSpec as P

HEAD_DIM = 128
LATENTS = 64
CHUNK = 16
SPLIT2 = 2
NORM_ROWS = 16
TOP_ROWS = 32
OWNERS = 4
GROUP = 8
ADAM_ROWS = 64
WG_ROWS = 256
LIMIT = 54 * 1024 * 1024
F32 = jnp.float32
BF16 = jnp.bfloat16
MESH = pl.DeviceIdType.MESH


def dot_nt(a, b):
    return lax.dot_general(a, b, (((1,), (1,)), ((), ())), preferred_element_type=F32)


def dot_tn(a, b):
    return lax.dot_general(a, b, (((0,), (0,)), ((), ())), preferred_element_type=F32)


def dot_nn(a, b):
    return jnp.dot(a, b, preferred_element_type=F32)


def kernel(
    n_sec, n_dp,
    hid_hbm, key_hbm, val_hbm, lat_hbm, nl_hbm, media_ref, cot_hbm, gate_ref, w_hbm, mf_hbm, ms_hbm,
    inc, inc2, wts, kv,
    hid, keys, vals, lat, q, p, go, gs, sbuf, gpbuf, gbuf, rinv, coef, maskf,
    lt_all, nl_all, snd, rcv, mf, ms, grads, wlow, kvs, fwd,
    in_sem, r1_send, r1_recv, r2_send, r2_recv,
    f_send, gat_send, gat_recv, a2a_send, a2a_recv, kv_send, kv_recv, loc_sem,
):
    sec, me = lax.axis_index("section"), lax.axis_index("dp")
    micro, block, width = hid_hbm.shape
    span = key_hbm.shape[2]
    rows_m = key_hbm.shape[1]
    lat_w = lat_hbm.shape[2]
    cols_d = w_hbm.shape[2]
    heads = span // HEAD_DIM
    heads_d = cols_d // HEAD_DIM
    tokens = micro * block
    n_chunks = tokens // CHUNK
    per_micro = n_chunks // micro
    n_chunks2 = n_chunks * SPLIT2
    n_y = n_dp // 4
    scale = 1.0 / math.sqrt(HEAD_DIM)
    core = lax.rem(me, 2)
    x_lo = lax.rem(me // 2, 2)
    y_at = me // 4
    top = sec == n_sec - 1
    mid_at = n_sec // 2
    early = sec < mid_at
    detour = mid_at < n_sec - 1
    mid = jnp.logical_and(sec == mid_at, detour)

    def dp_dev(j):
        return (sec, j)

    barrier = pltpu.get_barrier_semaphore()

    @pl.loop(1, n_dp)
    def _(k):
        pl.semaphore_signal(barrier, inc=1, device_id=dp_dev(lax.rem(me + k, n_dp)), device_id_type=MESH)

    @pl.when(sec > 0)
    def _():
        pl.semaphore_signal(barrier, inc=1, device_id=(sec - 1, me), device_id_type=MESH)

    @pl.when(sec < n_sec - 1)
    def _():
        pl.semaphore_signal(barrier, inc=1, device_id=(sec + 1, me), device_id_type=MESH)

    def ring_pairs(do):
        if detour:
            for one, two in ((mid_at, n_sec - 1), (n_sec - 1, mid_at - 1)):
                if one - two != 1 and two - one != 1:
                    for a, b in ((one, two), (two, one)):
                        do(a, b)

    def greet(a, b):
        @pl.when(sec == a)
        def _():
            pl.semaphore_signal(barrier, inc=1, device_id=(b, me), device_id_type=MESH)

    ring_pairs(greet)

    def load(i, src, dst):
        return pltpu.make_async_copy(src, dst, in_sem.at[i])

    hid_loads = [load(m, hid_hbm.at[m], hid.at[pl.ds(m * block, block), :]) for m in range(micro)]
    key_loads = [load(2 + m, key_hbm.at[m], keys.at[m]) for m in range(micro)]
    val_loads = [load(4 + m, val_hbm.at[m], vals.at[m]) for m in range(micro)]
    lat_load = load(6, lat_hbm, lat)
    nl_load = load(7, nl_hbm, nl_all.at[pl.ds(me * block, block), :])
    w_load, mf_load, ms_load = load(8, w_hbm, wts), load(9, mf_hbm, mf), load(10, ms_hbm, ms)
    cot_loads = [load(11 + m, cot_hbm.at[m, :, pl.ds(0, span)], inc.at[pl.ds(m * block, block), :]) for m in range(micro)]
    cot2_loads = [
        load(13 + m, cot_hbm.at[m, :, pl.ds(span, width - span)], inc2.at[pl.ds(m * block, block), :])
        for m in range(micro)
    ]
    lat_load.start()
    nl_load.start()
    hid_loads[0].start()
    key_loads[0].start()

    @pl.when(top)
    def _():
        for c in cot_loads:
            c.start()

    val_loads[0].start()
    for c in (hid_loads[1], key_loads[1], val_loads[1], w_load, mf_load, ms_load):
        c.start()

    @pl.when(top)
    def _():
        for c in cot2_loads:
            c.start()

    for m in range(micro):
        row = media_ref[pl.ds(m, 1), :].astype(F32)
        maskf[m] = jnp.transpose(jnp.broadcast_to(row, (block, block)))
    lat_load.wait()
    nl_load.wait()
    my_rows = pl.ds(pl.multiple_of(me * rows_m, rows_m), rows_m)
    for m in range(micro):
        lt_all[m, :, my_rows] = jnp.transpose(lat[m].astype(F32)).astype(BF16)

    def prepare(m, start, count):
        @pl.loop(0, count // NORM_ROWS)
        def _(t):
            rows = pl.ds(pl.multiple_of(m * block + start + t * NORM_ROWS, NORM_ROWS), NORM_ROWS)
            total = jnp.zeros((NORM_ROWS, 128), F32)
            for c in range(width // 128):
                h = hid[rows, pl.ds(c * 128, 128)].astype(F32)
                total = total + h * h
            mean = jnp.sum(total, axis=1, keepdims=True) * (1.0 / width)
            r = jnp.broadcast_to(1.0 / jnp.sqrt(mean + 1e-06), (NORM_ROWS, 128))
            rinv[rows, :] = r
            for c in range(heads):
                cols = pl.ds(c * 128, 128)
                q[rows, cols] = (hid[rows, cols].astype(F32) * r).astype(BF16)

        rows = pl.ds(m * block + start, count)
        half = lax.broadcasted_iota(jnp.int32, (count, rows_m), 1) // LATENTS
        allowed = half.astype(F32) == maskf[m, pl.ds(start, count), :]

        @pl.loop(0, heads // GROUP)
        def _(hg):
            for j in range(GROUP):
                cols = pl.ds(pl.multiple_of((hg * GROUP + j) * 128, 128), 128)
                sbuf[pl.ds(0, count), pl.ds(j * 128, 128)] = dot_nt(q[rows, cols], keys[m, :, cols])
            for j in range(GROUP):
                cols = pl.ds(pl.multiple_of((hg * GROUP + j) * 128, 128), 128)
                s = jnp.where(allowed, sbuf[pl.ds(0, count), pl.ds(j * 128, 128)] * scale, -1e30)
                e = jnp.exp(s - jnp.max(s, axis=1, keepdims=True))
                p[rows, cols] = e / jnp.sum(e, axis=1, keepdims=True)

    @pl.when(top)
    def _():
        hid_loads[0].wait()
        key_loads[0].wait()
        prepare(0, 0, TOP_ROWS)

    others = jnp.where(sec > 0, 1, 0) + jnp.where(sec < n_sec - 1, 1, 0) + n_dp - 1
    extra = [others]

    def expect(a, b):
        extra[0] = extra[0] + jnp.where(sec == a, 1, 0)

    ring_pairs(expect)
    pl.semaphore_wait(barrier, extra[0])

    def gather_copy(slot, owner, target):
        at = pl.ds(pl.multiple_of(owner * rows_m, rows_m), rows_m)
        ref_l = lt_all.at[:, :, at]
        ref_n = nl_all.at[at, :]
        return [
            pltpu.make_async_remote_copy(
                src_ref=ref, dst_ref=ref, send_sem=gat_send.at[i, slot], recv_sem=gat_recv.at[i, owner],
                device_id=dp_dev(target), device_id_type=MESH,
            )
            for i, ref in enumerate((ref_l, ref_n))
        ]

    def gather_start(slot, owner, target):
        for c in gather_copy(slot, owner, target):
            c.start()

    def gather_wait_recv(owner):
        for c in gather_copy(0, owner, me):
            c.wait_recv()

    def gather_wait_send(slot):
        for c in gather_copy(slot, me, me):
            c.wait_send()

    x_peer = me + 2 - 4 * x_lo
    core_peer = me + 1 - 2 * core

    def y_peer(dy):
        return lax.rem(y_at + dy, n_y) * 4 + x_lo * 2 + core

    def beside(j):
        return j + 2 - 4 * x_lo

    near = sorted({1, n_y - 1} - {0})
    far = [2] if n_y == 4 else []

    gather_start(0, me, x_peer)
    for dy in near:
        gather_start(dy, me, y_peer(dy))

    def gather_second():
        gather_wait_recv(x_peer)
        for dy in near:
            gather_start(n_y - 1 + dy, x_peer, y_peer(dy))

    def gather_core(owner):
        gather_start(2 * n_y - 1 + owner // 2, owner, core_peer)

    def gather_third():
        for dy in near:
            gather_wait_recv(y_peer(dy))
            gather_wait_recv(beside(y_peer(dy)))
        for dy in far:
            gather_start(dy, y_peer(n_y - 1), y_peer(1))
            gather_start(n_y - 1 + dy, beside(y_peer(1)), y_peer(n_y - 1))
        for owner in [me, x_peer] + [y_peer(dy) for dy in near] + [beside(y_peer(dy)) for dy in near]:
            gather_core(owner)

    def gather_fourth():
        for dy in far:
            for owner in (y_peer(dy), beside(y_peer(dy))):
                gather_wait_recv(owner)
                gather_core(owner)

    def transpose_values(m):
        @pl.loop(0, heads // 4)
        def _(hg):
            for j in range(4):
                cols = pl.ds(pl.multiple_of((hg * 4 + j) * 128, 128), 128)
                vals[m, :, cols] = jnp.transpose(vals[m, :, cols])

    def relay1(c):
        rows = pl.ds(pl.multiple_of(c * CHUNK, CHUNK), CHUNK)
        return pltpu.make_async_remote_copy(
            src_ref=inc.at[rows, :], dst_ref=inc.at[rows, :], send_sem=r1_send.at[c], recv_sem=r1_recv.at[c],
            device_id=(jnp.maximum(sec - 1, 0), me), device_id_type=MESH,
        )

    part2 = (width - span) // SPLIT2

    def at2(ref, c):
        return ref.at[
            pl.ds(pl.multiple_of(c // SPLIT2 * CHUNK, CHUNK), CHUNK),
            pl.ds(pl.multiple_of(lax.rem(c, SPLIT2) * part2, 128), part2),
        ]

    def relay2(c, dst=inc2, to=None):
        return pltpu.make_async_remote_copy(
            src_ref=at2(inc2, c), dst_ref=at2(dst, c), send_sem=r2_send.at[c], recv_sem=r2_recv.at[c],
            device_id=(jnp.maximum(sec - 1, 0) if to is None else to, me), device_id_type=MESH,
        )

    def forward2(c):
        return pltpu.make_async_remote_copy(
            src_ref=at2(fwd, c), dst_ref=at2(inc2, c), send_sem=f_send.at[c], recv_sem=r2_recv.at[c],
            device_id=(mid_at - 1, me), device_id_type=MESH,
        )

    gate_tanh = jnp.tanh(jnp.broadcast_to(gate_ref[...], (CHUNK, 128)))

    def chain_step(c, dot_values):
        m = c // per_micro
        rows = pl.ds(pl.multiple_of(c * CHUNK, CHUNK), CHUNK)
        for h in range(heads):
            cols = pl.ds(h * 128, 128)
            g = (gate_tanh * inc[rows, cols].astype(F32)).astype(BF16)
            go[rows, cols] = g
            gpbuf[:, cols] = dot_values(g, vals[m, :, cols])
        for h in range(heads):
            cols = pl.ds(h * 128, 128)
            pr, gp = p[rows, cols], gpbuf[:, cols]
            weighted = jnp.sum(pr * gp, axis=1, keepdims=True)
            gs[rows, cols] = (pr * (gp - weighted)).astype(BF16)
        acc = jnp.zeros((CHUNK, 128), F32)
        for h in range(heads):
            cols = pl.ds(h * 128, 128)
            gk = dot_nn(gs[rows, cols], keys[m, :, cols])
            gbuf[:, cols] = gk
            acc = acc + gk * hid[rows, cols].astype(F32)
        r = rinv[rows, :]
        dots = jnp.sum(acc, axis=1, keepdims=True)
        a = r * scale
        b = r * r * r * (dots * (scale / width))
        coef[rows, :] = b
        for h in range(heads):
            cols = pl.ds(h * 128, 128)
            new = inc[rows, cols].astype(F32) + (a * gbuf[:, cols] - b * hid[rows, cols].astype(F32))
            inc[rows, cols] = new.astype(BF16)

    def second_step(c):
        @pl.when(jnp.logical_not(top))
        def _():
            relay2(c).wait_recv()

        rows = pl.ds(pl.multiple_of(c // SPLIT2 * CHUNK, CHUNK), CHUNK)
        b = coef[rows, :]
        for h in range(part2 // 128):
            cols = pl.ds(pl.multiple_of(lax.rem(c, SPLIT2) * part2 + h * 128, 128), 128)
            hcols = pl.ds(pl.multiple_of(span + lax.rem(c, SPLIT2) * part2 + h * 128, 128), 128)
            inc2[rows, cols] = (inc2[rows, cols].astype(F32) - b * hid[rows, hcols].astype(F32)).astype(BF16)

        @pl.when(jnp.logical_and(sec > 0, jnp.logical_not(mid)))
        def _():
            relay2(c).start()

        if detour:
            @pl.when(mid)
            def _():
                relay2(c, fwd, n_sec - 1).start()

    def a2a_copy(m, kind, j):
        return pltpu.make_async_remote_copy(
            src_ref=snd.at[m, j, kind], dst_ref=rcv.at[m, kind, my_rows, :], send_sem=a2a_send.at[m, kind, j],
            recv_sem=a2a_recv.at[m, kind, me], device_id=dp_dev(j), device_id_type=MESH,
        )

    def a2a_in(m, kind, j):
        at = pl.ds(pl.multiple_of(j * rows_m, rows_m), rows_m)
        return pltpu.make_async_remote_copy(
            src_ref=snd.at[m, j, kind], dst_ref=rcv.at[m, kind, at, :], send_sem=a2a_send.at[m, kind, j],
            recv_sem=a2a_recv.at[m, kind, j], device_id=dp_dev(j), device_id_type=MESH,
        )

    def a2a_own(m, kind):
        return pltpu.make_async_copy(snd.at[m, me, kind], rcv.at[m, kind, my_rows, :], loc_sem.at[m, kind])

    def owner_at(g, i):
        if n_y == 4 and OWNERS == 4:
            odd, high = lax.rem(g, 2), g // 2
            dy = (2 * g + 1, 15 - 2 * g, 2, 0)[i]
            dx = (0, 1, 1 - odd, 1 - high)[i]
            dc = (high, 1 - high, lax.rem(odd + high, 2), 1 - odd)[i]
            return lax.rem(y_at + dy, 4) * 4 + lax.rem(x_lo + dx, 2) * 2 + lax.rem(core + dc, 2)
        return lax.rem(me + 1 + OWNERS * g + i, n_dp)

    def project(m, kinds, g):
        owners = [owner_at(g, i) for i in range(OWNERS)]
        for kind in kinds:
            project_compute(m, kind, owners)
        for i, j in enumerate(owners):
            for kind in kinds:
                own = OWNERS * g + i == n_dp - 1

                @pl.when(jnp.logical_not(own))
                def _():
                    a2a_copy(m, kind, j).start()

                @pl.when(own)
                def _():
                    a2a_own(m, kind).start()

    def project_compute(m, kind, owners):
        rows = pl.ds(pl.multiple_of(m * block, block), block)
        outs = []
        for j in owners:
            for i in range(heads_d):
                cols = pl.ds(pl.multiple_of(j * cols_d + i * 128, 128), 128)
                if kind == 0:
                    out = dot_tn(gs[rows, cols], q[rows, cols]) * scale
                else:
                    out = dot_tn(p[rows, cols].astype(BF16), go[rows, cols])
                outs.append((j, i, out.astype(BF16)))
        for j, i, out in outs:
            snd[m, j, kind, :, pl.ds(i * 128, 128)] = out

    def a2a_wait(m, kind):
        a2a_own(m, kind).wait()

        @pl.loop(1, n_dp)
        def _(k):
            a2a_in(m, kind, lax.rem(me + k, n_dp)).wait_recv()

    def weight_grad(m, kind):
        tile = WG_ROWS

        @pl.loop(0, lat_w // tile)
        def _(t):
            at = pl.ds(pl.multiple_of(t * tile, tile), tile)
            part = dot_nn(lt_all[m, at, :], rcv[m, kind])
            if m == 0:
                grads[kind, at, :] = part
            else:
                grads[kind, at, :] += part

    def adam(i):
        @pl.loop(0, lat_w // ADAM_ROWS)
        def _(t):
            at = pl.ds(pl.multiple_of(t * ADAM_ROWS, ADAM_ROWS), ADAM_ROWS)
            g = grads[i, at, :]
            cur = wts[i, at, :]
            first = 0.9 * mf[i, at, :] + 0.1 * g
            second = 0.95 * ms[i, at, :] + 0.05 * g * g
            new = cur - 0.02 * (first / (jnp.sqrt(second) + 1e-08) + 0.1 * cur)
            wts[i, at, :] = new
            wlow[i, at, :] = new.astype(BF16)

    my_cols = pl.ds(pl.multiple_of(me * cols_d, cols_d), cols_d)

    def kv_copy(kind, j, source):
        cols = pl.ds(pl.multiple_of(source * cols_d, cols_d), cols_d)
        return pltpu.make_async_remote_copy(
            src_ref=kvs.at[kind, j], dst_ref=kv.at[kind, :, cols], send_sem=kv_send.at[kind, j],
            recv_sem=kv_recv.at[kind, source], device_id=dp_dev(j), device_id_type=MESH,
        )

    def kv_own(kind):
        return pltpu.make_async_copy(kvs.at[kind, me], kv.at[kind, :, my_cols], loc_sem.at[2, kind])

    def next_rows(kind, send):
        @pl.loop(0, n_dp // 2)
        def _(k):
            pair = lax.rem(me // 2 + 1 + k, n_dp // 2)
            at = pl.ds(pl.multiple_of(pair * 2 * block, 2 * block), 2 * block)
            out = dot_nn(nl_all[at, :], wlow[kind]).astype(BF16)
            for i in range(2):
                kvs[kind, 2 * pair + i] = out[i * block : (i + 1) * block, :]
            if send:
                send_rows(kind, k)

    def send_rows(kind, k):
        pair = lax.rem(me // 2 + 1 + k, n_dp // 2)

        @pl.when(k < n_dp // 2 - 1)
        def _():
            for i in range(2):
                kv_copy(kind, 2 * pair + i, me).start()

        @pl.when(k == n_dp // 2 - 1)
        def _():
            kv_copy(kind, core_peer, me).start()
            kv_own(kind).start()

    def update_kind(kind):
        a2a_wait(1, kind)
        weight_grad(1, kind)
        adam(kind)

    @pl.when(jnp.logical_not(top))
    def _():
        hid_loads[0].wait()
        key_loads[0].wait()
        prepare(0, 0, block)

    val_loads[0].wait()

    def wait_rest():
        for c in (hid_loads[1:], key_loads[1:], val_loads[1:]):
            for d in c:
                d.wait()

    @pl.when(jnp.logical_not(top))
    def _():
        wait_rest()
        prepare(1, 0, block)
        for m in range(micro):
            transpose_values(m)

    @pl.when(top)
    def _():
        cot_loads[0].wait()

    soon = sec < n_sec - 2

    @pl.when(soon)
    def _():
        gather_second()


    @pl.loop(0, n_chunks)
    def _(c):
        @pl.when(jnp.logical_and(c == per_micro // 2, jnp.logical_not(soon)))
        def _():
            gather_second()

        third_at = jnp.where(early, per_micro // 2, per_micro + per_micro // 4)

        @pl.when(jnp.logical_and(c == third_at, jnp.logical_not(top)))
        def _():
            gather_third()

        @pl.when(jnp.logical_and(c == per_micro + per_micro // 2, early))
        def _():
            gather_fourth()

        @pl.when(top)
        def _():
            @pl.when(c == per_micro)
            def _():
                wait_rest()
                for d in cot_loads[1:]:
                    d.wait()

            @pl.when(c == TOP_ROWS // CHUNK)
            def _():
                prepare(0, TOP_ROWS, block - TOP_ROWS)

            @pl.when(c == per_micro)
            def _():
                prepare(1, 0, block)

            chain_step(c, dot_nt)

        @pl.when(jnp.logical_not(top))
        def _():
            relay1(c).wait_recv()
            chain_step(c, dot_nn)

        @pl.when(sec > 0)
        def _():
            relay1(c).start()

        project_now = jnp.logical_and(c >= per_micro, c < per_micro + n_dp // OWNERS)

        @pl.when(jnp.logical_and(project_now, jnp.logical_not(mid)))
        def _():
            project(0, (1, 0), c - per_micro)

    @pl.when(mid)
    def _():
        @pl.loop(0, n_dp // OWNERS)
        def _(k):
            project(0, (1, 0), k)

    for kind in (1, 0):
        @pl.loop(0, n_dp // OWNERS)
        def _(k):
            project(1, (kind,), k)

    @pl.when(top)
    def _():
        for c in cot2_loads:
            c.wait()

    def second_steps(first, last):
        @pl.loop(first, last)
        def _(c):
            second_step(c)

    def forward_steps(first, last):
        if detour:
            @pl.loop(first, last)
            def _(c):
                relay2(c, fwd, mid_at).wait_recv()
                forward2(c).start()

    def part_grads(kind):
        a2a_wait(0, kind)
        weight_grad(0, kind)

    def gather_end():
        @pl.loop(0, n_dp // 2)
        def _(k):
            gather_wait_recv(2 * k + 1 - core)

        for c in (w_load, mf_load, ms_load):
            c.wait()

    @pl.when(top)
    def _():
        second_steps(0, n_chunks2)
        gather_third()
        quarter = n_chunks2 // 4
        forward_steps(0, quarter)
        gather_fourth()
        forward_steps(quarter, 2 * quarter)
        gather_end()
        pieces = [
            lambda: part_grads(1),
            lambda: part_grads(0),
            lambda: update_kind(1),
            lambda: next_rows(1, False),
            lambda: update_kind(0),
            lambda: next_rows(0, False),
        ]
        left = n_chunks2 - 2 * quarter
        for i, piece in enumerate(pieces):
            forward_steps(2 * quarter + i * left // len(pieces), 2 * quarter + (i + 1) * left // len(pieces))
            piece()
        for kind in (1, 0):
            @pl.loop(0, n_dp // 2)
            def _(k):
                send_rows(kind, k)

    @pl.when(jnp.logical_not(top))
    def _():
        def gather_rest():
            @pl.when(jnp.logical_not(early))
            def _():
                gather_fourth()

        pieces = [
            (gather_rest, 0, 10, 12),
            (gather_end, 0, 13, 15),
            (lambda: part_grads(1), 0, 13, 15),
            (lambda: part_grads(0), 0, 14, 16),
            (lambda: update_kind(1), jnp.where(sec > 0, 3 + sec, 0), 16, 16),
            (lambda: next_rows(1, True), jnp.where(sec > 0, 4 + sec, 0), 16, 16),
            (lambda: update_kind(0), jnp.where(sec > 0, 7 + 2 * sec, 0), 16, 16),
            (lambda: next_rows(0, True), jnp.where(sec > 0, 8 + 2 * sec, 0), 16, 16),
        ]
        done = 0
        for piece, low, at_mid, high in pieces:
            until = jnp.where(early, low, jnp.where(mid, at_mid, high)) * n_chunks2 // 16
            second_steps(done, until)
            done = until
            piece()
        second_steps(done, n_chunks2)

    @pl.when(sec > 0)
    def _():
        @pl.loop(0, n_chunks)
        def _(c):
            relay1(c).wait_send()

        @pl.loop(0, n_chunks2)
        def _(c):
            relay2(c).wait_send()

    @pl.loop(0, 2 * n_y - 1 + n_dp // 2)
    def _(k):
        gather_wait_send(k)

    if detour:
        @pl.when(top)
        def _():
            @pl.loop(0, n_chunks2)
            def _(c):
                forward2(c).wait_send()

    @pl.loop(1, n_dp)
    def _(k):
        j = lax.rem(me + k, n_dp)
        for kind in range(2):
            for m in range(micro):
                a2a_copy(m, kind, j).wait_send()
            kv_copy(kind, j, me).wait_send()
            kv_copy(kind, j, j).wait_recv()

    for kind in range(2):
        kv_own(kind).wait()


def store(inc, inc2, wts, kv, ig_hbm, nw_hbm, kv_hbm, sem):
    _, micro, block, width = ig_hbm.shape
    span = inc.shape[1]
    pairs = [(wts, nw_hbm.at[0]), (kv, kv_hbm.at[0])]
    for m in range(micro):
        rows = pl.ds(m * block, block)
        pairs.append((inc.at[rows, :], ig_hbm.at[0, m, :, pl.ds(0, span)]))
        pairs.append((inc2.at[rows, :], ig_hbm.at[0, m, :, pl.ds(span, width - span)]))
    copies = [pltpu.make_async_copy(src, dst, sem.at[i]) for i, (src, dst) in enumerate(pairs)]
    for c in copies:
        c.start()
    for c in copies:
        c.wait()


def body(
    hidden_states, key_rows, value_rows, latents, next_latents, media_index, cotangent, gate_alpha,
    weights, moment_first, moment_second,
):
    n_sec, n_dp = lax.axis_size("section"), lax.axis_size("dp")
    _, micro, block, width = hidden_states.shape
    span, rows_m = key_rows.shape[3], key_rows.shape[2]
    lat_w, cols_d = weights.shape[2], weights.shape[3]
    tokens = micro * block
    n_y = n_dp // 4
    n_chunks = tokens // CHUNK
    n_chunks2 = n_chunks * SPLIT2
    any_spec = pl.BlockSpec(memory_space=pl.ANY)
    vmem_spec = pl.BlockSpec(memory_space=pltpu.VMEM)
    dma = pltpu.SemaphoreType.DMA
    vmem = pltpu.VMEM
    held = pl.pallas_call(
        functools.partial(kernel, n_sec, n_dp),
        out_shape=(
            vmem((tokens, span), BF16),
            vmem((tokens, width - span), BF16),
            vmem((2, lat_w, cols_d), F32),
            vmem((2, rows_m, span), BF16),
        ),
        in_specs=[any_spec] * 5 + [vmem_spec, any_spec, vmem_spec] + [any_spec] * 3,
        out_specs=(vmem_spec,) * 4,
        scratch_shapes=[
            vmem((tokens, width), BF16),
            vmem((micro, rows_m, span), BF16),
            vmem((micro, rows_m, span), BF16),
            vmem((micro, rows_m, lat_w), BF16),
            vmem((tokens, span), BF16),
            vmem((tokens, span), F32),
            vmem((tokens, span), BF16),
            vmem((tokens, span), BF16),
            vmem((block, GROUP * 128), F32),
            vmem((CHUNK, span), F32),
            vmem((CHUNK, span), F32),
            vmem((tokens, 128), F32),
            vmem((tokens, 128), F32),
            vmem((micro, block, rows_m), F32),
            vmem((micro, lat_w, n_dp * rows_m), BF16),
            vmem((n_dp * block, lat_w), BF16),
            vmem((micro, n_dp, 2, rows_m, cols_d), BF16),
            vmem((micro, 2, n_dp * rows_m, cols_d), BF16),
            vmem((2, lat_w, cols_d), F32),
            vmem((2, lat_w, cols_d), F32),
            vmem((2, lat_w, cols_d), F32),
            vmem((2, lat_w, cols_d), BF16),
            vmem((2, n_dp, block, cols_d), BF16),
            vmem((tokens, width - span), BF16),
            dma((15,)),
            dma((n_chunks,)),
            dma((n_chunks,)),
            dma((n_chunks2,)),
            dma((n_chunks2,)),
            dma((n_chunks2,)),
            dma((2, 2 * n_y - 1 + n_dp // 2)),
            dma((2, n_dp)),
            dma((micro, 2, n_dp)),
            dma((micro, 2, n_dp)),
            dma((2, n_dp)),
            dma((2, n_dp)),
            dma((3, 2)),
        ],
        compiler_params=pltpu.CompilerParams(
            collective_id=0, has_side_effects=True, vmem_limit_bytes=LIMIT
        ),
    )(
        hidden_states[0], key_rows[0], value_rows[0], latents, next_latents, media_index, cotangent,
        gate_alpha.reshape(1, 1), weights[0], moment_first[0], moment_second[0],
    )
    grad_in, new_w, kv = pl.pallas_call(
        store,
        out_shape=(
            jax.ShapeDtypeStruct((1, micro, block, width), BF16),
            jax.ShapeDtypeStruct((1, 2, lat_w, cols_d), F32),
            jax.ShapeDtypeStruct((1, 2, rows_m, span), BF16),
        ),
        in_specs=[vmem_spec] * 4,
        out_specs=(any_spec, any_spec, any_spec),
        scratch_shapes=[dma((2 + 2 * micro,))],
        compiler_params=pltpu.CompilerParams(vmem_limit_bytes=1024 * 1024),
    )(*held)
    return grad_in, new_w, kv


def solution(mesh):
    in_specs = (
        P("section", None, "dp", None),
        P("section", None, "dp", None),
        P("section", None, "dp", None),
        P(None, "dp", None),
        P("dp", None),
        P(None, "dp"),
        P(None, "dp", None),
        P("section"),
        P("section", None, None, "dp"),
        P("section", None, None, "dp"),
        P("section", None, None, "dp"),
    )
    out_specs = (
        P("section", None, "dp", None),
        P("section", None, None, "dp"),
        P("section", None, "dp", None),
    )
    return jax.shard_map(body, mesh=mesh, in_specs=in_specs, out_specs=out_specs, check_vma=False)
```

```python
import functools
import math

import jax
import jax.numpy as jnp
from jax import lax
from jax.experimental import pallas as pl
from jax.experimental.pallas import tpu as pltpu
from jax.sharding import PartitionSpec as P

HEAD_DIM = 128
LATENTS = 64
CHUNK = 16
DIRECT2 = 2
SPLIT2 = 2
NORM_ROWS = 16
TOP_ROWS = 32
OWNERS = 4
GROUP = 8
ADAM_ROWS = 64
WG_ROWS = 256
LIMIT = 54 * 1024 * 1024
F32 = jnp.float32
BF16 = jnp.bfloat16
MESH = pl.DeviceIdType.MESH


def dot_nt(a, b):
    return lax.dot_general(a, b, (((1,), (1,)), ((), ())), preferred_element_type=F32)


def dot_tn(a, b):
    return lax.dot_general(a, b, (((0,), (0,)), ((), ())), preferred_element_type=F32)


def dot_nn(a, b):
    return jnp.dot(a, b, preferred_element_type=F32)


def kernel(
    n_sec, n_dp,
    hid_hbm, key_hbm, val_hbm, lat_hbm, nl_hbm, media_ref, cot_hbm, gate_ref, w_hbm, mf_hbm, ms_hbm,
    inc, inc2, wts, kv,
    hid, keys, vals, lat, q, p, go, gs, sbuf, gpbuf, gbuf, rinv, coef, maskf,
    lt_all, nl_all, snd, rcv, mf, ms, grads, wlow, kvs, fwd,
    in_sem, r1_send, r1_recv, r2_send, r2_recv,
    f_send, gat_send, gat_recv, a2a_send, a2a_recv, kv_send, kv_recv, loc_sem,
):
    sec, me = lax.axis_index("section"), lax.axis_index("dp")
    micro, block, width = hid_hbm.shape
    span = key_hbm.shape[2]
    rows_m = key_hbm.shape[1]
    lat_w = lat_hbm.shape[2]
    cols_d = w_hbm.shape[2]
    heads = span // HEAD_DIM
    heads_d = cols_d // HEAD_DIM
    tokens = micro * block
    n_chunks = tokens // CHUNK
    per_micro = n_chunks // micro
    n_chunks2 = n_chunks * SPLIT2
    n_y = n_dp // 4
    scale = 1.0 / math.sqrt(HEAD_DIM)
    core = lax.rem(me, 2)
    x_lo = lax.rem(me // 2, 2)
    y_at = me // 4
    top = sec == n_sec - 1
    mid_at = n_sec // 2
    early = sec < mid_at
    detour = mid_at < n_sec - 1
    mid = jnp.logical_and(sec == mid_at, detour)

    def dp_dev(j):
        return (sec, j)

    barrier = pltpu.get_barrier_semaphore()

    @pl.loop(1, n_dp)
    def _(k):
        pl.semaphore_signal(barrier, inc=1, device_id=dp_dev(lax.rem(me + k, n_dp)), device_id_type=MESH)

    @pl.when(sec > 0)
    def _():
        pl.semaphore_signal(barrier, inc=1, device_id=(sec - 1, me), device_id_type=MESH)

    @pl.when(sec < n_sec - 1)
    def _():
        pl.semaphore_signal(barrier, inc=1, device_id=(sec + 1, me), device_id_type=MESH)

    def ring_pairs(do):
        if detour:
            for one, two in ((mid_at, n_sec - 1), (n_sec - 1, mid_at - 1)):
                if one - two != 1 and two - one != 1:
                    for a, b in ((one, two), (two, one)):
                        do(a, b)

    def greet(a, b):
        @pl.when(sec == a)
        def _():
            pl.semaphore_signal(barrier, inc=1, device_id=(b, me), device_id_type=MESH)

    ring_pairs(greet)

    def load(i, src, dst):
        return pltpu.make_async_copy(src, dst, in_sem.at[i])

    hid_loads = [load(m, hid_hbm.at[m], hid.at[pl.ds(m * block, block), :]) for m in range(micro)]
    key_loads = [load(2 + m, key_hbm.at[m], keys.at[m]) for m in range(micro)]
    val_loads = [load(4 + m, val_hbm.at[m], vals.at[m]) for m in range(micro)]
    lat_load = load(6, lat_hbm, lat)
    nl_load = load(7, nl_hbm, nl_all.at[pl.ds(me * block, block), :])
    w_load, mf_load, ms_load = load(8, w_hbm, wts), load(9, mf_hbm, mf), load(10, ms_hbm, ms)
    cot_loads = [load(11 + m, cot_hbm.at[m, :, pl.ds(0, span)], inc.at[pl.ds(m * block, block), :]) for m in range(micro)]
    cot2_loads = [
        load(13 + m, cot_hbm.at[m, :, pl.ds(span, width - span)], inc2.at[pl.ds(m * block, block), :])
        for m in range(micro)
    ]
    lat_load.start()
    nl_load.start()
    hid_loads[0].start()
    key_loads[0].start()

    @pl.when(top)
    def _():
        for c in cot_loads:
            c.start()

    val_loads[0].start()
    for c in (hid_loads[1], key_loads[1], val_loads[1], w_load, mf_load, ms_load):
        c.start()

    @pl.when(top)
    def _():
        for c in cot2_loads:
            c.start()

    for m in range(micro):
        row = media_ref[pl.ds(m, 1), :].astype(F32)
        maskf[m] = jnp.transpose(jnp.broadcast_to(row, (block, block)))
    lat_load.wait()
    nl_load.wait()
    my_rows = pl.ds(pl.multiple_of(me * rows_m, rows_m), rows_m)
    for m in range(micro):
        lt_all[m, :, my_rows] = jnp.transpose(lat[m].astype(F32)).astype(BF16)

    def prepare(m, start, count):
        @pl.loop(0, count // NORM_ROWS)
        def _(t):
            rows = pl.ds(pl.multiple_of(m * block + start + t * NORM_ROWS, NORM_ROWS), NORM_ROWS)
            total = jnp.zeros((NORM_ROWS, 128), F32)
            for c in range(width // 128):
                h = hid[rows, pl.ds(c * 128, 128)].astype(F32)
                total = total + h * h
            mean = jnp.sum(total, axis=1, keepdims=True) * (1.0 / width)
            r = jnp.broadcast_to(1.0 / jnp.sqrt(mean + 1e-06), (NORM_ROWS, 128))
            rinv[rows, :] = r
            for c in range(heads):
                cols = pl.ds(c * 128, 128)
                q[rows, cols] = (hid[rows, cols].astype(F32) * r).astype(BF16)

        rows = pl.ds(m * block + start, count)
        half = lax.broadcasted_iota(jnp.int32, (count, rows_m), 1) // LATENTS
        allowed = half.astype(F32) == maskf[m, pl.ds(start, count), :]

        @pl.loop(0, heads // GROUP)
        def _(hg):
            for j in range(GROUP):
                cols = pl.ds(pl.multiple_of((hg * GROUP + j) * 128, 128), 128)
                sbuf[pl.ds(0, count), pl.ds(j * 128, 128)] = dot_nt(q[rows, cols], keys[m, :, cols])
            for j in range(GROUP):
                cols = pl.ds(pl.multiple_of((hg * GROUP + j) * 128, 128), 128)
                s = jnp.where(allowed, sbuf[pl.ds(0, count), pl.ds(j * 128, 128)] * scale, -1e30)
                e = jnp.exp(s - jnp.max(s, axis=1, keepdims=True))
                p[rows, cols] = e / jnp.sum(e, axis=1, keepdims=True)

    @pl.when(top)
    def _():
        hid_loads[0].wait()
        key_loads[0].wait()
        prepare(0, 0, TOP_ROWS)

    others = jnp.where(sec > 0, 1, 0) + jnp.where(sec < n_sec - 1, 1, 0) + n_dp - 1
    extra = [others]

    def expect(a, b):
        extra[0] = extra[0] + jnp.where(sec == a, 1, 0)

    ring_pairs(expect)
    pl.semaphore_wait(barrier, extra[0])

    def gather_copy(slot, owner, target):
        at = pl.ds(pl.multiple_of(owner * rows_m, rows_m), rows_m)
        ref_l = lt_all.at[:, :, at]
        ref_n = nl_all.at[at, :]
        return [
            pltpu.make_async_remote_copy(
                src_ref=ref, dst_ref=ref, send_sem=gat_send.at[i, slot], recv_sem=gat_recv.at[i, owner],
                device_id=dp_dev(target), device_id_type=MESH,
            )
            for i, ref in enumerate((ref_l, ref_n))
        ]

    def gather_start(slot, owner, target):
        for c in gather_copy(slot, owner, target):
            c.start()

    def gather_wait_recv(owner):
        for c in gather_copy(0, owner, me):
            c.wait_recv()

    def gather_wait_send(slot):
        for c in gather_copy(slot, me, me):
            c.wait_send()

    x_peer = me + 2 - 4 * x_lo
    core_peer = me + 1 - 2 * core

    def y_peer(dy):
        return lax.rem(y_at + dy, n_y) * 4 + x_lo * 2 + core

    def beside(j):
        return j + 2 - 4 * x_lo

    near = sorted({1, n_y - 1} - {0})
    far = [2] if n_y == 4 else []

    gather_start(0, me, x_peer)
    for dy in near:
        gather_start(dy, me, y_peer(dy))

    def gather_second():
        gather_wait_recv(x_peer)
        for dy in near:
            gather_start(n_y - 1 + dy, x_peer, y_peer(dy))

    def gather_core(owner):
        gather_start(2 * n_y - 1 + owner // 2, owner, core_peer)

    def gather_third():
        for dy in near:
            gather_wait_recv(y_peer(dy))
            gather_wait_recv(beside(y_peer(dy)))
        for dy in far:
            gather_start(dy, y_peer(n_y - 1), y_peer(1))
            gather_start(n_y - 1 + dy, beside(y_peer(1)), y_peer(n_y - 1))
        for owner in [me, x_peer] + [y_peer(dy) for dy in near] + [beside(y_peer(dy)) for dy in near]:
            gather_core(owner)

    def gather_fourth():
        for dy in far:
            for owner in (y_peer(dy), beside(y_peer(dy))):
                gather_wait_recv(owner)
                gather_core(owner)

    def transpose_values(m):
        @pl.loop(0, heads // 4)
        def _(hg):
            for j in range(4):
                cols = pl.ds(pl.multiple_of((hg * 4 + j) * 128, 128), 128)
                vals[m, :, cols] = jnp.transpose(vals[m, :, cols])

    def relay1(c):
        rows = pl.ds(pl.multiple_of(c * CHUNK, CHUNK), CHUNK)
        return pltpu.make_async_remote_copy(
            src_ref=inc.at[rows, :], dst_ref=inc.at[rows, :], send_sem=r1_send.at[c], recv_sem=r1_recv.at[c],
            device_id=(jnp.maximum(sec - 1, 0), me), device_id_type=MESH,
        )

    part2 = (width - span) // SPLIT2

    def at2(ref, c):
        return ref.at[
            pl.ds(pl.multiple_of(c // SPLIT2 * CHUNK, CHUNK), CHUNK),
            pl.ds(pl.multiple_of(lax.rem(c, SPLIT2) * part2, 128), part2),
        ]

    def relay2(c, dst=inc2, to=None):
        return pltpu.make_async_remote_copy(
            src_ref=at2(inc2, c), dst_ref=at2(dst, c), send_sem=r2_send.at[c], recv_sem=r2_recv.at[c],
            device_id=(jnp.maximum(sec - 1, 0) if to is None else to, me), device_id_type=MESH,
        )

    def forward2(c):
        return pltpu.make_async_remote_copy(
            src_ref=at2(fwd, c), dst_ref=at2(inc2, c), send_sem=f_send.at[c], recv_sem=r2_recv.at[c],
            device_id=(mid_at - 1, me), device_id_type=MESH,
        )

    gate_tanh = jnp.tanh(jnp.full((CHUNK, 128), gate_ref[0], F32))

    def chain_step(c, dot_values):
        m = c // per_micro
        rows = pl.ds(pl.multiple_of(c * CHUNK, CHUNK), CHUNK)
        for h in range(heads):
            cols = pl.ds(h * 128, 128)
            g = (gate_tanh * inc[rows, cols].astype(F32)).astype(BF16)
            go[rows, cols] = g
            gpbuf[:, cols] = dot_values(g, vals[m, :, cols])
        for h in range(heads):
            cols = pl.ds(h * 128, 128)
            pr, gp = p[rows, cols], gpbuf[:, cols]
            weighted = jnp.sum(pr * gp, axis=1, keepdims=True)
            gs[rows, cols] = (pr * (gp - weighted)).astype(BF16)
        acc = jnp.zeros((CHUNK, 128), F32)
        for h in range(heads):
            cols = pl.ds(h * 128, 128)
            gk = dot_nn(gs[rows, cols], keys[m, :, cols])
            gbuf[:, cols] = gk
            acc = acc + gk * hid[rows, cols].astype(F32)
        r = rinv[rows, :]
        dots = jnp.sum(acc, axis=1, keepdims=True)
        a = r * scale
        b = r * r * r * (dots * (scale / width))
        coef[rows, :] = b
        for h in range(heads):
            cols = pl.ds(h * 128, 128)
            new = inc[rows, cols].astype(F32) + (a * gbuf[:, cols] - b * hid[rows, cols].astype(F32))
            inc[rows, cols] = new.astype(BF16)

    def second_step(c):
        @pl.when(jnp.logical_not(top))
        def _():
            relay2(c).wait_recv()

        rows = pl.ds(pl.multiple_of(c // SPLIT2 * CHUNK, CHUNK), CHUNK)
        b = coef[rows, :]
        for h in range(part2 // 128):
            cols = pl.ds(pl.multiple_of(lax.rem(c, SPLIT2) * part2 + h * 128, 128), 128)
            hcols = pl.ds(pl.multiple_of(span + lax.rem(c, SPLIT2) * part2 + h * 128, 128), 128)
            inc2[rows, cols] = (inc2[rows, cols].astype(F32) - b * hid[rows, hcols].astype(F32)).astype(BF16)

        around = jnp.logical_and(mid, c < n_chunks2 - DIRECT2)

        @pl.when(jnp.logical_and(sec > 0, jnp.logical_not(around)))
        def _():
            relay2(c).start()

        if detour:
            @pl.when(around)
            def _():
                relay2(c, fwd, n_sec - 1).start()

    def a2a_copy(m, kind, j):
        return pltpu.make_async_remote_copy(
            src_ref=snd.at[m, j, kind], dst_ref=rcv.at[m, kind, my_rows, :], send_sem=a2a_send.at[m, kind, j],
            recv_sem=a2a_recv.at[m, kind, me], device_id=dp_dev(j), device_id_type=MESH,
        )

    def a2a_in(m, kind, j):
        at = pl.ds(pl.multiple_of(j * rows_m, rows_m), rows_m)
        return pltpu.make_async_remote_copy(
            src_ref=snd.at[m, j, kind], dst_ref=rcv.at[m, kind, at, :], send_sem=a2a_send.at[m, kind, j],
            recv_sem=a2a_recv.at[m, kind, j], device_id=dp_dev(j), device_id_type=MESH,
        )

    def a2a_own(m, kind):
        return pltpu.make_async_copy(snd.at[m, me, kind], rcv.at[m, kind, my_rows, :], loc_sem.at[m, kind])

    def owner_at(g, i):
        if n_y == 4 and OWNERS == 4:
            odd, high = lax.rem(g, 2), g // 2
            dy = (2 * g + 1, 15 - 2 * g, 2, 0)[i]
            dx = (0, 1, 1 - odd, 1 - high)[i]
            dc = (high, 1 - high, lax.rem(odd + high, 2), 1 - odd)[i]
            return lax.rem(y_at + dy, 4) * 4 + lax.rem(x_lo + dx, 2) * 2 + lax.rem(core + dc, 2)
        return lax.rem(me + 1 + OWNERS * g + i, n_dp)

    def project(m, kinds, g, held=False):
        owners = [owner_at(g, i) for i in range(OWNERS)]
        if not held:
            for kind in kinds:
                project_compute(m, kind, owners)
        for i, j in enumerate(owners):
            crosses = lax.rem(j // 2, 2) != x_lo
            own = OWNERS * g + i == n_dp - 1
            for kind in kinds:
                if held:
                    now = crosses
                elif m == 0:
                    now = jnp.logical_not(jnp.logical_or(own, jnp.logical_and(crosses, mid)))
                else:
                    now = jnp.logical_not(own)

                @pl.when(now)
                def _():
                    a2a_copy(m, kind, j).start()

                if not held:
                    @pl.when(own)
                    def _():
                        a2a_own(m, kind).start()

    def project_compute(m, kind, owners):
        rows = pl.ds(pl.multiple_of(m * block, block), block)
        outs = []
        for j in owners:
            for i in range(heads_d):
                cols = pl.ds(pl.multiple_of(j * cols_d + i * 128, 128), 128)
                if kind == 0:
                    out = dot_tn(gs[rows, cols], q[rows, cols]) * scale
                else:
                    out = dot_tn(p[rows, cols].astype(BF16), go[rows, cols])
                outs.append((j, i, out.astype(BF16)))
        for j, i, out in outs:
            snd[m, j, kind, :, pl.ds(i * 128, 128)] = out

    def a2a_wait(m, kind):
        a2a_own(m, kind).wait()

        @pl.loop(1, n_dp)
        def _(k):
            a2a_in(m, kind, lax.rem(me + k, n_dp)).wait_recv()

    def weight_grad(m, kind):
        tile = WG_ROWS

        @pl.loop(0, lat_w // tile)
        def _(t):
            at = pl.ds(pl.multiple_of(t * tile, tile), tile)
            part = dot_nn(lt_all[m, at, :], rcv[m, kind])
            if m == 0:
                grads[kind, at, :] = part
            else:
                grads[kind, at, :] += part

    def adam(i):
        @pl.loop(0, lat_w // ADAM_ROWS)
        def _(t):
            at = pl.ds(pl.multiple_of(t * ADAM_ROWS, ADAM_ROWS), ADAM_ROWS)
            g = grads[i, at, :]
            cur = wts[i, at, :]
            first = 0.9 * mf[i, at, :] + 0.1 * g
            second = 0.95 * ms[i, at, :] + 0.05 * g * g
            new = cur - 0.02 * (first / (jnp.sqrt(second) + 1e-08) + 0.1 * cur)
            wts[i, at, :] = new
            wlow[i, at, :] = new.astype(BF16)

    my_cols = pl.ds(pl.multiple_of(me * cols_d, cols_d), cols_d)

    def kv_copy(kind, j, source):
        cols = pl.ds(pl.multiple_of(source * cols_d, cols_d), cols_d)
        return pltpu.make_async_remote_copy(
            src_ref=kvs.at[kind, j], dst_ref=kv.at[kind, :, cols], send_sem=kv_send.at[kind, j],
            recv_sem=kv_recv.at[kind, source], device_id=dp_dev(j), device_id_type=MESH,
        )

    def kv_own(kind):
        return pltpu.make_async_copy(kvs.at[kind, me], kv.at[kind, :, my_cols], loc_sem.at[2, kind])

    chip_steps = ((1, 0), (3, 1), (2, 1), (0, 1), (3, 0), (1, 1), (2, 0), (0, 0))

    def chip_at(k):
        if n_y != 4:
            return lax.rem(me // 2 + 1 + k, n_dp // 2)
        dy, dx = (sum(jnp.where(k == i, step[axis], 0) for i, step in enumerate(chip_steps)) for axis in (0, 1))
        return lax.rem(y_at + dy, 4) * 2 + lax.rem(x_lo + dx, 2)

    def next_rows(kind, send):
        @pl.loop(0, n_dp // 2)
        def _(k):
            pair = chip_at(k)
            at = pl.ds(pl.multiple_of(pair * 2 * block, 2 * block), 2 * block)
            out = dot_nn(nl_all[at, :], wlow[kind]).astype(BF16)
            for i in range(2):
                kvs[kind, 2 * pair + i] = out[i * block : (i + 1) * block, :]
            if send:
                send_rows(kind, k)

    def send_rows(kind, k):
        pair = chip_at(k)

        @pl.when(k < n_dp // 2 - 1)
        def _():
            for i in range(2):
                kv_copy(kind, 2 * pair + i, me).start()

        @pl.when(k == n_dp // 2 - 1)
        def _():
            kv_copy(kind, core_peer, me).start()
            kv_own(kind).start()

    def update_kind(kind):
        a2a_wait(1, kind)
        weight_grad(1, kind)
        adam(kind)

    @pl.when(jnp.logical_not(top))
    def _():
        hid_loads[0].wait()
        key_loads[0].wait()
        prepare(0, 0, block)

    val_loads[0].wait()

    def wait_rest():
        for c in (hid_loads[1:], key_loads[1:], val_loads[1:]):
            for d in c:
                d.wait()

    @pl.when(jnp.logical_not(top))
    def _():
        wait_rest()
        prepare(1, 0, block)
        for m in range(micro):
            transpose_values(m)

    @pl.when(top)
    def _():
        cot_loads[0].wait()

    soon = sec < n_sec - 2

    @pl.when(soon)
    def _():
        gather_second()


    @pl.loop(0, n_chunks)
    def _(c):
        @pl.when(jnp.logical_and(c == per_micro // 2, jnp.logical_not(soon)))
        def _():
            gather_second()

        third_at = jnp.where(early, per_micro // 2, per_micro + per_micro // 4)

        @pl.when(jnp.logical_and(c == third_at, jnp.logical_not(top)))
        def _():
            gather_third()

        @pl.when(jnp.logical_and(c == per_micro + per_micro // 2, early))
        def _():
            gather_fourth()

        @pl.when(top)
        def _():
            @pl.when(c == per_micro)
            def _():
                wait_rest()
                for d in cot_loads[1:]:
                    d.wait()

            @pl.when(c == TOP_ROWS // CHUNK)
            def _():
                prepare(0, TOP_ROWS, block - TOP_ROWS)

            @pl.when(c == per_micro)
            def _():
                prepare(1, 0, block)

            chain_step(c, dot_nt)

        @pl.when(jnp.logical_not(top))
        def _():
            relay1(c).wait_recv()
            chain_step(c, dot_nn)

        @pl.when(sec > 0)
        def _():
            relay1(c).start()

        project_now = jnp.logical_and(c >= per_micro, c < per_micro + n_dp // OWNERS)

        @pl.when(project_now)
        def _():
            project(0, (1, 0), c - per_micro)

    @pl.when(mid)
    def _():
        @pl.loop(0, n_dp // OWNERS)
        def _(k):
            project(0, (1, 0), k, True)

    for kind in (1, 0):
        @pl.loop(0, n_dp // OWNERS)
        def _(k):
            project(1, (kind,), k)

    @pl.when(top)
    def _():
        for c in cot2_loads:
            c.wait()

    def second_steps(first, last):
        @pl.loop(first, last)
        def _(c):
            second_step(c)

    def forward_steps(first, last):
        if detour:
            @pl.loop(first, last)
            def _(c):
                relay2(c, fwd, mid_at).wait_recv()
                forward2(c).start()

    def part_grads(kind):
        a2a_wait(0, kind)
        weight_grad(0, kind)

    def gather_end():
        @pl.loop(0, n_dp // 2)
        def _(k):
            gather_wait_recv(2 * k + 1 - core)

        for c in (w_load, mf_load, ms_load):
            c.wait()

    @pl.when(top)
    def _():
        second_steps(0, n_chunks2)
        gather_third()
        straight = [k for k, step in enumerate(chip_steps) if step[1] == 0] if n_y == 4 else []

        def rows_beside(kind):
            next_rows(kind, False)
            for k in straight:
                send_rows(kind, k)

        quarter = n_chunks2 // 4
        forward_steps(0, quarter)
        gather_fourth()
        forward_steps(quarter, 2 * quarter)
        gather_end()
        pieces = [
            lambda: part_grads(1),
            lambda: part_grads(0),
            lambda: update_kind(1),
            lambda: rows_beside(1),
            lambda: update_kind(0),
            lambda: rows_beside(0),
        ]
        left, groups = n_chunks2 - DIRECT2 - 2 * quarter, len(pieces) + 1
        for i, piece in enumerate(pieces):
            forward_steps(2 * quarter + i * left // groups, 2 * quarter + (i + 1) * left // groups)
            piece()
        forward_steps(2 * quarter + len(pieces) * left // groups, n_chunks2 - DIRECT2)
        for k in range(n_dp // 2):
            if k not in straight:
                for kind in (1, 0):
                    send_rows(kind, k)

    @pl.when(jnp.logical_not(top))
    def _():
        def gather_rest():
            @pl.when(jnp.logical_not(early))
            def _():
                gather_fourth()

        pieces = [
            (gather_rest, 0, 10, 12),
            (gather_end, 0, 13, 15),
            (lambda: part_grads(1), 0, 13, 15),
            (lambda: part_grads(0), 0, 14, 16),
            (lambda: update_kind(1), jnp.where(sec > 0, 3 + sec, 0), 15, 16),
            (lambda: next_rows(1, True), jnp.where(sec > 0, 4 + sec, 0), 16, 16),
            (lambda: update_kind(0), jnp.where(sec > 0, 7 + 2 * sec, 0), 16, 16),
            (lambda: next_rows(0, True), jnp.where(sec > 0, 8 + 2 * sec, 0), 16, 16),
        ]
        done = 0
        for piece, low, at_mid, high in pieces:
            until = jnp.where(early, low, jnp.where(mid, at_mid, high)) * n_chunks2 // 16
            second_steps(done, until)
            done = until
            piece()
        second_steps(done, n_chunks2)

    @pl.when(sec > 0)
    def _():
        @pl.loop(0, n_chunks)
        def _(c):
            relay1(c).wait_send()

        @pl.loop(0, n_chunks2)
        def _(c):
            relay2(c).wait_send()

    @pl.loop(0, 2 * n_y - 1 + n_dp // 2)
    def _(k):
        gather_wait_send(k)

    if detour:
        @pl.when(top)
        def _():
            @pl.loop(0, n_chunks2 - DIRECT2)
            def _(c):
                forward2(c).wait_send()

    @pl.loop(1, n_dp)
    def _(k):
        j = lax.rem(me + k, n_dp)
        for kind in range(2):
            for m in range(micro):
                a2a_copy(m, kind, j).wait_send()
            kv_copy(kind, j, me).wait_send()
            kv_copy(kind, j, j).wait_recv()

    for kind in range(2):
        kv_own(kind).wait()


def store(inc, inc2, wts, kv, ig_hbm, nw_hbm, kv_hbm, sem):
    _, micro, block, width = ig_hbm.shape
    span = inc.shape[1]
    pairs = [(wts, nw_hbm.at[0]), (kv, kv_hbm.at[0])]
    for m in range(micro):
        rows = pl.ds(m * block, block)
        pairs.append((inc.at[rows, :], ig_hbm.at[0, m, :, pl.ds(0, span)]))
        pairs.append((inc2.at[rows, :], ig_hbm.at[0, m, :, pl.ds(span, width - span)]))
    copies = [pltpu.make_async_copy(src, dst, sem.at[i]) for i, (src, dst) in enumerate(pairs)]
    for c in copies:
        c.start()
    for c in copies:
        c.wait()


def body(
    hidden_states, key_rows, value_rows, latents, next_latents, media_index, cotangent, gate_alpha,
    weights, moment_first, moment_second,
):
    n_sec, n_dp = lax.axis_size("section"), lax.axis_size("dp")
    _, micro, block, width = hidden_states.shape
    span, rows_m = key_rows.shape[3], key_rows.shape[2]
    lat_w, cols_d = weights.shape[2], weights.shape[3]
    tokens = micro * block
    n_y = n_dp // 4
    n_chunks = tokens // CHUNK
    n_chunks2 = n_chunks * SPLIT2
    any_spec = pl.BlockSpec(memory_space=pl.ANY)
    vmem_spec = pl.BlockSpec(memory_space=pltpu.VMEM)
    dma = pltpu.SemaphoreType.DMA
    vmem = pltpu.VMEM
    held = pl.pallas_call(
        functools.partial(kernel, n_sec, n_dp),
        out_shape=(
            vmem((tokens, span), BF16),
            vmem((tokens, width - span), BF16),
            vmem((2, lat_w, cols_d), F32),
            vmem((2, rows_m, span), BF16),
        ),
        in_specs=[any_spec] * 5 + [vmem_spec, any_spec, pl.BlockSpec(memory_space=pltpu.SMEM)] + [any_spec] * 3,
        out_specs=(vmem_spec,) * 4,
        scratch_shapes=[
            vmem((tokens, width), BF16),
            vmem((micro, rows_m, span), BF16),
            vmem((micro, rows_m, span), BF16),
            vmem((micro, rows_m, lat_w), BF16),
            vmem((tokens, span), BF16),
            vmem((tokens, span), F32),
            vmem((tokens, span), BF16),
            vmem((tokens, span), BF16),
            vmem((block, GROUP * 128), F32),
            vmem((CHUNK, span), F32),
            vmem((CHUNK, span), F32),
            vmem((tokens, 128), F32),
            vmem((tokens, 128), F32),
            vmem((micro, block, rows_m), F32),
            vmem((micro, lat_w, n_dp * rows_m), BF16),
            vmem((n_dp * block, lat_w), BF16),
            vmem((micro, n_dp, 2, rows_m, cols_d), BF16),
            vmem((micro, 2, n_dp * rows_m, cols_d), BF16),
            vmem((2, lat_w, cols_d), F32),
            vmem((2, lat_w, cols_d), F32),
            vmem((2, lat_w, cols_d), F32),
            vmem((2, lat_w, cols_d), BF16),
            vmem((2, n_dp, block, cols_d), BF16),
            vmem((tokens, width - span), BF16),
            dma((15,)),
            dma((n_chunks,)),
            dma((n_chunks,)),
            dma((n_chunks2,)),
            dma((n_chunks2,)),
            dma((n_chunks2,)),
            dma((2, 2 * n_y - 1 + n_dp // 2)),
            dma((2, n_dp)),
            dma((micro, 2, n_dp)),
            dma((micro, 2, n_dp)),
            dma((2, n_dp)),
            dma((2, n_dp)),
            dma((3, 2)),
        ],
        compiler_params=pltpu.CompilerParams(
            collective_id=0, has_side_effects=True, vmem_limit_bytes=LIMIT
        ),
    )(
        hidden_states[0], key_rows[0], value_rows[0], latents, next_latents, media_index, cotangent,
        gate_alpha, weights[0], moment_first[0], moment_second[0],
    )
    grad_in, new_w, kv = pl.pallas_call(
        store,
        out_shape=(
            jax.ShapeDtypeStruct((1, micro, block, width), BF16),
            jax.ShapeDtypeStruct((1, 2, lat_w, cols_d), F32),
            jax.ShapeDtypeStruct((1, 2, rows_m, span), BF16),
        ),
        in_specs=[vmem_spec] * 4,
        out_specs=(any_spec, any_spec, any_spec),
        scratch_shapes=[dma((2 + 2 * micro,))],
        compiler_params=pltpu.CompilerParams(vmem_limit_bytes=1024 * 1024),
    )(*held)
    return grad_in, new_w, kv


def solution(mesh):
    in_specs = (
        P("section", None, "dp", None),
        P("section", None, "dp", None),
        P("section", None, "dp", None),
        P(None, "dp", None),
        P("dp", None),
        P(None, "dp"),
        P(None, "dp", None),
        P("section"),
        P("section", None, None, "dp"),
        P("section", None, None, "dp"),
        P("section", None, None, "dp"),
    )
    out_specs = (
        P("section", None, "dp", None),
        P("section", None, None, "dp"),
        P("section", None, "dp", None),
    )
    return jax.shard_map(body, mesh=mesh, in_specs=in_specs, out_specs=out_specs, check_vma=False)
```

```python
import functools
import math

import jax
import jax.numpy as jnp
from jax import lax
from jax.experimental import pallas as pl
from jax.experimental.pallas import tpu as pltpu
from jax.sharding import PartitionSpec as P

HEAD_DIM = 128
LATENTS = 64
CHUNK = 16
DIRECT2 = 2
SPLIT2 = 2
NORM_ROWS = 16
TOP_ROWS = 16
OWNERS = 4
GROUP = 8
ADAM_ROWS = 64
WG_ROWS = 256
LIMIT = 54 * 1024 * 1024
F32 = jnp.float32
BF16 = jnp.bfloat16
MESH = pl.DeviceIdType.MESH


def dot_nt(a, b):
    return lax.dot_general(a, b, (((1,), (1,)), ((), ())), preferred_element_type=F32)


def dot_tn(a, b):
    return lax.dot_general(a, b, (((0,), (0,)), ((), ())), preferred_element_type=F32)


def dot_nn(a, b):
    return jnp.dot(a, b, preferred_element_type=F32)


def kernel(
    n_sec, n_dp,
    hid_hbm, key_hbm, val_hbm, lat_hbm, nl_hbm, media_ref, cot_hbm, gate_ref, w_hbm, mf_hbm, ms_hbm,
    inc, inc2, wts, kv,
    hid, keys, vals, lat, q, p, go, gs, sbuf, gpbuf, gbuf, rinv, coef, maskf,
    lt_all, nl_all, snd, rcv, mf, ms, grads, wlow, kvs, fwd,
    in_sem, r1_send, r1_recv, r2_send, r2_recv,
    f_send, gat_send, gat_recv, a2a_send, a2a_recv, kv_send, kv_recv, loc_sem,
):
    sec, me = lax.axis_index("section"), lax.axis_index("dp")
    micro, block, width = hid_hbm.shape
    span = key_hbm.shape[2]
    rows_m = key_hbm.shape[1]
    lat_w = lat_hbm.shape[2]
    cols_d = w_hbm.shape[2]
    heads = span // HEAD_DIM
    heads_d = cols_d // HEAD_DIM
    tokens = micro * block
    n_chunks = tokens // CHUNK
    per_micro = n_chunks // micro
    n_chunks2 = n_chunks * SPLIT2
    n_y = n_dp // 4
    scale = 1.0 / math.sqrt(HEAD_DIM)
    core = lax.rem(me, 2)
    x_lo = lax.rem(me // 2, 2)
    y_at = me // 4
    top = sec == n_sec - 1
    mid_at = n_sec // 2
    early = sec < mid_at
    detour = mid_at < n_sec - 1
    mid = jnp.logical_and(sec == mid_at, detour)

    def dp_dev(j):
        return (sec, j)

    barrier = pltpu.get_barrier_semaphore()

    @pl.loop(1, n_dp)
    def _(k):
        pl.semaphore_signal(barrier, inc=1, device_id=dp_dev(lax.rem(me + k, n_dp)), device_id_type=MESH)

    @pl.when(sec > 0)
    def _():
        pl.semaphore_signal(barrier, inc=1, device_id=(sec - 1, me), device_id_type=MESH)

    @pl.when(sec < n_sec - 1)
    def _():
        pl.semaphore_signal(barrier, inc=1, device_id=(sec + 1, me), device_id_type=MESH)

    def ring_pairs(do):
        if detour:
            for one, two in ((mid_at, n_sec - 1), (n_sec - 1, mid_at - 1)):
                if one - two != 1 and two - one != 1:
                    for a, b in ((one, two), (two, one)):
                        do(a, b)

    def greet(a, b):
        @pl.when(sec == a)
        def _():
            pl.semaphore_signal(barrier, inc=1, device_id=(b, me), device_id_type=MESH)

    ring_pairs(greet)

    def load(i, src, dst):
        return pltpu.make_async_copy(src, dst, in_sem.at[i])

    hid_loads = [load(m, hid_hbm.at[m], hid.at[pl.ds(m * block, block), :]) for m in range(micro)]
    key_loads = [load(2 + m, key_hbm.at[m], keys.at[m]) for m in range(micro)]
    val_loads = [load(4 + m, val_hbm.at[m], vals.at[m]) for m in range(micro)]
    lat_load = load(6, lat_hbm, lat)
    nl_load = load(7, nl_hbm, nl_all.at[pl.ds(me * block, block), :])
    w_load, mf_load, ms_load = load(8, w_hbm, wts), load(9, mf_hbm, mf), load(10, ms_hbm, ms)
    cot_loads = [load(11 + m, cot_hbm.at[m, :, pl.ds(0, span)], inc.at[pl.ds(m * block, block), :]) for m in range(micro)]
    cot2_loads = [
        load(13 + m, cot_hbm.at[m, :, pl.ds(span, width - span)], inc2.at[pl.ds(m * block, block), :])
        for m in range(micro)
    ]
    lat_load.start()
    nl_load.start()
    hid_loads[0].start()
    key_loads[0].start()

    @pl.when(top)
    def _():
        for c in cot_loads:
            c.start()

    val_loads[0].start()
    for c in (hid_loads[1], key_loads[1], val_loads[1], w_load, mf_load, ms_load):
        c.start()

    @pl.when(top)
    def _():
        for c in cot2_loads:
            c.start()

    for m in range(micro):
        row = media_ref[pl.ds(m, 1), :].astype(F32)
        maskf[m] = jnp.transpose(jnp.broadcast_to(row, (block, block)))
    lat_load.wait()
    nl_load.wait()
    my_rows = pl.ds(pl.multiple_of(me * rows_m, rows_m), rows_m)
    for m in range(micro):
        lt_all[m, :, my_rows] = jnp.transpose(lat[m].astype(F32)).astype(BF16)

    def prepare(m, start, count):
        @pl.loop(0, count // NORM_ROWS)
        def _(t):
            rows = pl.ds(pl.multiple_of(m * block + start + t * NORM_ROWS, NORM_ROWS), NORM_ROWS)
            total = jnp.zeros((NORM_ROWS, 128), F32)
            for c in range(width // 128):
                h = hid[rows, pl.ds(c * 128, 128)].astype(F32)
                total = total + h * h
            mean = jnp.sum(total, axis=1, keepdims=True) * (1.0 / width)
            r = jnp.broadcast_to(1.0 / jnp.sqrt(mean + 1e-06), (NORM_ROWS, 128))
            rinv[rows, :] = r
            for c in range(heads):
                cols = pl.ds(c * 128, 128)
                q[rows, cols] = (hid[rows, cols].astype(F32) * r).astype(BF16)

        rows = pl.ds(m * block + start, count)
        half = lax.broadcasted_iota(jnp.int32, (count, rows_m), 1) // LATENTS
        allowed = half.astype(F32) == maskf[m, pl.ds(start, count), :]

        @pl.loop(0, heads // GROUP)
        def _(hg):
            for j in range(GROUP):
                cols = pl.ds(pl.multiple_of((hg * GROUP + j) * 128, 128), 128)
                sbuf[pl.ds(0, count), pl.ds(j * 128, 128)] = dot_nt(q[rows, cols], keys[m, :, cols])
            for j in range(GROUP):
                cols = pl.ds(pl.multiple_of((hg * GROUP + j) * 128, 128), 128)
                s = jnp.where(allowed, sbuf[pl.ds(0, count), pl.ds(j * 128, 128)] * scale, -1e30)
                e = jnp.exp(s - jnp.max(s, axis=1, keepdims=True))
                p[rows, cols] = e / jnp.sum(e, axis=1, keepdims=True)

    @pl.when(top)
    def _():
        hid_loads[0].wait()
        key_loads[0].wait()
        prepare(0, 0, TOP_ROWS)

    others = jnp.where(sec > 0, 1, 0) + jnp.where(sec < n_sec - 1, 1, 0) + n_dp - 1
    extra = [others]

    def expect(a, b):
        extra[0] = extra[0] + jnp.where(sec == a, 1, 0)

    ring_pairs(expect)
    pl.semaphore_wait(barrier, extra[0])

    def gather_copy(slot, owner, target):
        at = pl.ds(pl.multiple_of(owner * rows_m, rows_m), rows_m)
        ref_l = lt_all.at[:, :, at]
        ref_n = nl_all.at[at, :]
        return [
            pltpu.make_async_remote_copy(
                src_ref=ref, dst_ref=ref, send_sem=gat_send.at[i, slot], recv_sem=gat_recv.at[i, owner],
                device_id=dp_dev(target), device_id_type=MESH,
            )
            for i, ref in enumerate((ref_l, ref_n))
        ]

    def gather_start(slot, owner, target):
        for c in gather_copy(slot, owner, target):
            c.start()

    def gather_wait_recv(owner):
        for c in gather_copy(0, owner, me):
            c.wait_recv()

    def gather_wait_send(slot):
        for c in gather_copy(slot, me, me):
            c.wait_send()

    x_peer = me + 2 - 4 * x_lo
    core_peer = me + 1 - 2 * core

    def y_peer(dy):
        return lax.rem(y_at + dy, n_y) * 4 + x_lo * 2 + core

    def beside(j):
        return j + 2 - 4 * x_lo

    near = sorted({1, n_y - 1} - {0})
    far = [2] if n_y == 4 else []

    gather_start(0, me, x_peer)
    for dy in near:
        gather_start(dy, me, y_peer(dy))

    def gather_second():
        gather_wait_recv(x_peer)
        for dy in near:
            gather_start(n_y - 1 + dy, x_peer, y_peer(dy))

    def gather_core(owner):
        gather_start(2 * n_y - 1 + owner // 2, owner, core_peer)

    def gather_third():
        for dy in near:
            gather_wait_recv(y_peer(dy))
            gather_wait_recv(beside(y_peer(dy)))
        for dy in far:
            gather_start(dy, y_peer(n_y - 1), y_peer(1))
            gather_start(n_y - 1 + dy, beside(y_peer(1)), y_peer(n_y - 1))
        for owner in [me, x_peer] + [y_peer(dy) for dy in near] + [beside(y_peer(dy)) for dy in near]:
            gather_core(owner)

    def gather_fourth():
        for dy in far:
            for owner in (y_peer(dy), beside(y_peer(dy))):
                gather_wait_recv(owner)
                gather_core(owner)

    def transpose_values(m):
        @pl.loop(0, heads // 4)
        def _(hg):
            for j in range(4):
                cols = pl.ds(pl.multiple_of((hg * 4 + j) * 128, 128), 128)
                vals[m, :, cols] = jnp.transpose(vals[m, :, cols])

    def relay1(c):
        rows = pl.ds(pl.multiple_of(c * CHUNK, CHUNK), CHUNK)
        return pltpu.make_async_remote_copy(
            src_ref=inc.at[rows, :], dst_ref=inc.at[rows, :], send_sem=r1_send.at[c], recv_sem=r1_recv.at[c],
            device_id=(jnp.maximum(sec - 1, 0), me), device_id_type=MESH,
        )

    part2 = (width - span) // SPLIT2

    def at2(ref, c):
        return ref.at[
            pl.ds(pl.multiple_of(c // SPLIT2 * CHUNK, CHUNK), CHUNK),
            pl.ds(pl.multiple_of(lax.rem(c, SPLIT2) * part2, 128), part2),
        ]

    def relay2(c, dst=inc2, to=None):
        return pltpu.make_async_remote_copy(
            src_ref=at2(inc2, c), dst_ref=at2(dst, c), send_sem=r2_send.at[c], recv_sem=r2_recv.at[c],
            device_id=(jnp.maximum(sec - 1, 0) if to is None else to, me), device_id_type=MESH,
        )

    def forward2(c):
        return pltpu.make_async_remote_copy(
            src_ref=at2(fwd, c), dst_ref=at2(inc2, c), send_sem=f_send.at[c], recv_sem=r2_recv.at[c],
            device_id=(mid_at - 1, me), device_id_type=MESH,
        )

    gate_tanh = jnp.tanh(jnp.full((CHUNK, 128), gate_ref[0], F32))

    def chain_step(c, dot_values):
        m = c // per_micro
        rows = pl.ds(pl.multiple_of(c * CHUNK, CHUNK), CHUNK)
        for h in range(heads):
            cols = pl.ds(h * 128, 128)
            g = (gate_tanh * inc[rows, cols].astype(F32)).astype(BF16)
            go[rows, cols] = g
            gpbuf[:, cols] = dot_values(g, vals[m, :, cols])
        for h in range(heads):
            cols = pl.ds(h * 128, 128)
            pr, gp = p[rows, cols], gpbuf[:, cols]
            weighted = jnp.sum(pr * gp, axis=1, keepdims=True)
            gs[rows, cols] = (pr * (gp - weighted)).astype(BF16)
        acc = jnp.zeros((CHUNK, 128), F32)
        for h in range(heads):
            cols = pl.ds(h * 128, 128)
            gk = dot_nn(gs[rows, cols], keys[m, :, cols])
            gbuf[:, cols] = gk
            acc = acc + gk * hid[rows, cols].astype(F32)
        r = rinv[rows, :]
        dots = jnp.sum(acc, axis=1, keepdims=True)
        a = r * scale
        b = r * r * r * (dots * (scale / width))
        coef[rows, :] = b
        for h in range(heads):
            cols = pl.ds(h * 128, 128)
            new = inc[rows, cols].astype(F32) + (a * gbuf[:, cols] - b * hid[rows, cols].astype(F32))
            inc[rows, cols] = new.astype(BF16)

    def second_step(c):
        @pl.when(jnp.logical_not(top))
        def _():
            relay2(c).wait_recv()

        rows = pl.ds(pl.multiple_of(c // SPLIT2 * CHUNK, CHUNK), CHUNK)
        b = coef[rows, :]
        for h in range(part2 // 128):
            cols = pl.ds(pl.multiple_of(lax.rem(c, SPLIT2) * part2 + h * 128, 128), 128)
            hcols = pl.ds(pl.multiple_of(span + lax.rem(c, SPLIT2) * part2 + h * 128, 128), 128)
            inc2[rows, cols] = (inc2[rows, cols].astype(F32) - b * hid[rows, hcols].astype(F32)).astype(BF16)

        around = jnp.logical_and(mid, c < n_chunks2 - DIRECT2)

        @pl.when(jnp.logical_and(sec > 0, jnp.logical_not(around)))
        def _():
            relay2(c).start()

        if detour:
            @pl.when(around)
            def _():
                relay2(c, fwd, n_sec - 1).start()

    def a2a_copy(m, kind, j):
        return pltpu.make_async_remote_copy(
            src_ref=snd.at[m, j, kind], dst_ref=rcv.at[m, kind, my_rows, :], send_sem=a2a_send.at[m, kind, j],
            recv_sem=a2a_recv.at[m, kind, me], device_id=dp_dev(j), device_id_type=MESH,
        )

    def a2a_in(m, kind, j):
        at = pl.ds(pl.multiple_of(j * rows_m, rows_m), rows_m)
        return pltpu.make_async_remote_copy(
            src_ref=snd.at[m, j, kind], dst_ref=rcv.at[m, kind, at, :], send_sem=a2a_send.at[m, kind, j],
            recv_sem=a2a_recv.at[m, kind, j], device_id=dp_dev(j), device_id_type=MESH,
        )

    def a2a_own(m, kind):
        return pltpu.make_async_copy(snd.at[m, me, kind], rcv.at[m, kind, my_rows, :], loc_sem.at[m, kind])

    def owner_at(g, i):
        if n_y == 4 and OWNERS == 4:
            odd, high = lax.rem(g, 2), g // 2
            dy = (2 * g + 1, 15 - 2 * g, 2, 0)[i]
            dx = (0, 1, 1 - odd, 1 - high)[i]
            dc = (high, 1 - high, lax.rem(odd + high, 2), 1 - odd)[i]
            return lax.rem(y_at + dy, 4) * 4 + lax.rem(x_lo + dx, 2) * 2 + lax.rem(core + dc, 2)
        return lax.rem(me + 1 + OWNERS * g + i, n_dp)

    def project(m, kinds, g, held=False):
        owners = [owner_at(g, i) for i in range(OWNERS)]
        if not held:
            for kind in kinds:
                project_compute(m, kind, owners)
        for i, j in enumerate(owners):
            crosses = lax.rem(j // 2, 2) != x_lo
            own = OWNERS * g + i == n_dp - 1
            for kind in kinds:
                if held:
                    now = crosses
                elif m == 0:
                    now = jnp.logical_not(jnp.logical_or(own, jnp.logical_and(crosses, mid)))
                else:
                    now = jnp.logical_not(own)

                @pl.when(now)
                def _():
                    a2a_copy(m, kind, j).start()

                if not held:
                    @pl.when(own)
                    def _():
                        a2a_own(m, kind).start()

    def project_compute(m, kind, owners):
        rows = pl.ds(pl.multiple_of(m * block, block), block)
        outs = []
        for j in owners:
            for i in range(heads_d):
                cols = pl.ds(pl.multiple_of(j * cols_d + i * 128, 128), 128)
                if kind == 0:
                    out = dot_tn(gs[rows, cols], q[rows, cols]) * scale
                else:
                    out = dot_tn(p[rows, cols].astype(BF16), go[rows, cols])
                outs.append((j, i, out.astype(BF16)))
        for j, i, out in outs:
            snd[m, j, kind, :, pl.ds(i * 128, 128)] = out

    def a2a_wait(m, kind):
        a2a_own(m, kind).wait()

        @pl.loop(1, n_dp)
        def _(k):
            a2a_in(m, kind, lax.rem(me + k, n_dp)).wait_recv()

    def weight_grad(m, kind):
        tile = WG_ROWS

        @pl.loop(0, lat_w // tile)
        def _(t):
            at = pl.ds(pl.multiple_of(t * tile, tile), tile)
            part = dot_nn(lt_all[m, at, :], rcv[m, kind])
            if m == 0:
                grads[kind, at, :] = part
            else:
                grads[kind, at, :] += part

    def adam(i):
        @pl.loop(0, lat_w // ADAM_ROWS)
        def _(t):
            at = pl.ds(pl.multiple_of(t * ADAM_ROWS, ADAM_ROWS), ADAM_ROWS)
            g = grads[i, at, :]
            cur = wts[i, at, :]
            first = 0.9 * mf[i, at, :] + 0.1 * g
            second = 0.95 * ms[i, at, :] + 0.05 * g * g
            new = cur - 0.02 * (first / (jnp.sqrt(second) + 1e-08) + 0.1 * cur)
            wts[i, at, :] = new
            wlow[i, at, :] = new.astype(BF16)

    my_cols = pl.ds(pl.multiple_of(me * cols_d, cols_d), cols_d)

    def kv_copy(kind, j, source):
        cols = pl.ds(pl.multiple_of(source * cols_d, cols_d), cols_d)
        return pltpu.make_async_remote_copy(
            src_ref=kvs.at[kind, j], dst_ref=kv.at[kind, :, cols], send_sem=kv_send.at[kind, j],
            recv_sem=kv_recv.at[kind, source], device_id=dp_dev(j), device_id_type=MESH,
        )

    def kv_own(kind):
        return pltpu.make_async_copy(kvs.at[kind, me], kv.at[kind, :, my_cols], loc_sem.at[2, kind])

    chip_steps = ((1, 0), (3, 1), (2, 1), (0, 1), (3, 0), (1, 1), (2, 0), (0, 0))

    def chip_at(k):
        if n_y != 4:
            return lax.rem(me // 2 + 1 + k, n_dp // 2)
        dy, dx = (sum(jnp.where(k == i, step[axis], 0) for i, step in enumerate(chip_steps)) for axis in (0, 1))
        return lax.rem(y_at + dy, 4) * 2 + lax.rem(x_lo + dx, 2)

    def next_rows(kind, send):
        @pl.loop(0, n_dp // 2)
        def _(k):
            pair = chip_at(k)
            at = pl.ds(pl.multiple_of(pair * 2 * block, 2 * block), 2 * block)
            out = dot_nn(nl_all[at, :], wlow[kind]).astype(BF16)
            for i in range(2):
                kvs[kind, 2 * pair + i] = out[i * block : (i + 1) * block, :]
            if send:
                send_rows(kind, k)

    def send_rows(kind, k):
        pair = chip_at(k)

        @pl.when(k < n_dp // 2 - 1)
        def _():
            for i in range(2):
                kv_copy(kind, 2 * pair + i, me).start()

        @pl.when(k == n_dp // 2 - 1)
        def _():
            kv_copy(kind, core_peer, me).start()
            kv_own(kind).start()

    def update_kind(kind):
        a2a_wait(1, kind)
        weight_grad(1, kind)
        adam(kind)

    @pl.when(jnp.logical_not(top))
    def _():
        hid_loads[0].wait()
        key_loads[0].wait()
        prepare(0, 0, block)

    val_loads[0].wait()

    def wait_rest():
        for c in (hid_loads[1:], key_loads[1:], val_loads[1:]):
            for d in c:
                d.wait()

    @pl.when(jnp.logical_not(top))
    def _():
        wait_rest()
        prepare(1, 0, block)
        for m in range(micro):
            transpose_values(m)

    @pl.when(top)
    def _():
        cot_loads[0].wait()

    soon = sec < n_sec - 2

    @pl.when(soon)
    def _():
        gather_second()


    @pl.loop(0, n_chunks)
    def _(c):
        @pl.when(jnp.logical_and(c == per_micro // 2, jnp.logical_not(soon)))
        def _():
            gather_second()

        third_at = jnp.where(early, per_micro // 2, per_micro + per_micro // 4)

        @pl.when(jnp.logical_and(c == third_at, jnp.logical_not(top)))
        def _():
            gather_third()

        @pl.when(jnp.logical_and(c == per_micro + per_micro // 2, early))
        def _():
            gather_fourth()

        @pl.when(top)
        def _():
            @pl.when(c == per_micro)
            def _():
                wait_rest()
                for d in cot_loads[1:]:
                    d.wait()

            @pl.when(c == TOP_ROWS // CHUNK)
            def _():
                prepare(0, TOP_ROWS, block - TOP_ROWS)

            @pl.when(c == per_micro)
            def _():
                prepare(1, 0, block)

            chain_step(c, dot_nt)

        @pl.when(jnp.logical_not(top))
        def _():
            relay1(c).wait_recv()
            chain_step(c, dot_nn)

        @pl.when(sec > 0)
        def _():
            relay1(c).start()

        project_now = jnp.logical_and(c >= per_micro, c < per_micro + n_dp // OWNERS)

        @pl.when(project_now)
        def _():
            project(0, (1, 0), c - per_micro)

    @pl.when(mid)
    def _():
        @pl.loop(0, n_dp // OWNERS)
        def _(k):
            project(0, (1, 0), k, True)

    for kind in (1, 0):
        @pl.loop(0, n_dp // OWNERS)
        def _(k):
            project(1, (kind,), k)

    @pl.when(top)
    def _():
        for c in cot2_loads:
            c.wait()

    def second_steps(first, last):
        @pl.loop(first, last)
        def _(c):
            second_step(c)

    def forward_steps(first, last):
        if detour:
            @pl.loop(first, last)
            def _(c):
                relay2(c, fwd, mid_at).wait_recv()
                forward2(c).start()

    def part_grads(kind):
        a2a_wait(0, kind)
        weight_grad(0, kind)

    def gather_end():
        @pl.loop(0, n_dp // 2)
        def _(k):
            gather_wait_recv(2 * k + 1 - core)

        for c in (w_load, mf_load, ms_load):
            c.wait()

    @pl.when(top)
    def _():
        second_steps(0, n_chunks2)
        gather_third()
        straight = [k for k, step in enumerate(chip_steps) if step[1] == 0] if n_y == 4 else []

        def rows_beside(kind):
            next_rows(kind, False)
            for k in straight:
                send_rows(kind, k)

        quarter = n_chunks2 // 4
        forward_steps(0, quarter)
        gather_fourth()
        forward_steps(quarter, 2 * quarter)
        gather_end()
        pieces = [
            lambda: part_grads(1),
            lambda: part_grads(0),
            lambda: update_kind(1),
            lambda: rows_beside(1),
            lambda: update_kind(0),
            lambda: rows_beside(0),
        ]
        left, groups = n_chunks2 - DIRECT2 - 2 * quarter, len(pieces) + 1
        for i, piece in enumerate(pieces):
            forward_steps(2 * quarter + i * left // groups, 2 * quarter + (i + 1) * left // groups)
            piece()
        forward_steps(2 * quarter + len(pieces) * left // groups, n_chunks2 - DIRECT2)
        for k in range(n_dp // 2):
            if k not in straight:
                for kind in (1, 0):
                    send_rows(kind, k)

    @pl.when(jnp.logical_not(top))
    def _():
        def gather_rest():
            @pl.when(jnp.logical_not(early))
            def _():
                gather_fourth()

        pieces = [
            (gather_rest, 0, 10, 12),
            (gather_end, 0, 13, 15),
            (lambda: part_grads(1), 0, 13, 15),
            (lambda: part_grads(0), 0, 14, 16),
            (lambda: update_kind(1), jnp.where(sec > 0, 3 + sec, 0), 15, 16),
            (lambda: next_rows(1, True), jnp.where(sec > 0, 4 + sec, 0), 16, 16),
            (lambda: update_kind(0), jnp.where(sec > 0, 7 + 2 * sec, 0), 16, 16),
            (lambda: next_rows(0, True), jnp.where(sec > 0, 8 + 2 * sec, 0), 16, 16),
        ]
        done = 0
        for piece, low, at_mid, high in pieces:
            until = jnp.where(early, low, jnp.where(mid, at_mid, high)) * n_chunks2 // 16
            second_steps(done, until)
            done = until
            piece()
        second_steps(done, n_chunks2)

    @pl.when(sec > 0)
    def _():
        @pl.loop(0, n_chunks)
        def _(c):
            relay1(c).wait_send()

        @pl.loop(0, n_chunks2)
        def _(c):
            relay2(c).wait_send()

    @pl.loop(0, 2 * n_y - 1 + n_dp // 2)
    def _(k):
        gather_wait_send(k)

    if detour:
        @pl.when(top)
        def _():
            @pl.loop(0, n_chunks2 - DIRECT2)
            def _(c):
                forward2(c).wait_send()

    @pl.loop(1, n_dp)
    def _(k):
        j = lax.rem(me + k, n_dp)
        for kind in range(2):
            for m in range(micro):
                a2a_copy(m, kind, j).wait_send()
            kv_copy(kind, j, me).wait_send()
            kv_copy(kind, j, j).wait_recv()

    for kind in range(2):
        kv_own(kind).wait()


def store(inc, inc2, wts, kv, ig_hbm, nw_hbm, kv_hbm, sem):
    _, micro, block, width = ig_hbm.shape
    span = inc.shape[1]
    pairs = [(wts, nw_hbm.at[0]), (kv, kv_hbm.at[0])]
    for m in range(micro):
        rows = pl.ds(m * block, block)
        pairs.append((inc.at[rows, :], ig_hbm.at[0, m, :, pl.ds(0, span)]))
        pairs.append((inc2.at[rows, :], ig_hbm.at[0, m, :, pl.ds(span, width - span)]))
    copies = [pltpu.make_async_copy(src, dst, sem.at[i]) for i, (src, dst) in enumerate(pairs)]
    for c in copies:
        c.start()
    for c in copies:
        c.wait()


def body(
    hidden_states, key_rows, value_rows, latents, next_latents, media_index, cotangent, gate_alpha,
    weights, moment_first, moment_second,
):
    n_sec, n_dp = lax.axis_size("section"), lax.axis_size("dp")
    _, micro, block, width = hidden_states.shape
    span, rows_m = key_rows.shape[3], key_rows.shape[2]
    lat_w, cols_d = weights.shape[2], weights.shape[3]
    tokens = micro * block
    n_y = n_dp // 4
    n_chunks = tokens // CHUNK
    n_chunks2 = n_chunks * SPLIT2
    any_spec = pl.BlockSpec(memory_space=pl.ANY)
    vmem_spec = pl.BlockSpec(memory_space=pltpu.VMEM)
    dma = pltpu.SemaphoreType.DMA
    vmem = pltpu.VMEM
    held = pl.pallas_call(
        functools.partial(kernel, n_sec, n_dp),
        out_shape=(
            vmem((tokens, span), BF16),
            vmem((tokens, width - span), BF16),
            vmem((2, lat_w, cols_d), F32),
            vmem((2, rows_m, span), BF16),
        ),
        in_specs=[any_spec] * 5 + [vmem_spec, any_spec, pl.BlockSpec(memory_space=pltpu.SMEM)] + [any_spec] * 3,
        out_specs=(vmem_spec,) * 4,
        scratch_shapes=[
            vmem((tokens, width), BF16),
            vmem((micro, rows_m, span), BF16),
            vmem((micro, rows_m, span), BF16),
            vmem((micro, rows_m, lat_w), BF16),
            vmem((tokens, span), BF16),
            vmem((tokens, span), F32),
            vmem((tokens, span), BF16),
            vmem((tokens, span), BF16),
            vmem((block, GROUP * 128), F32),
            vmem((CHUNK, span), F32),
            vmem((CHUNK, span), F32),
            vmem((tokens, 128), F32),
            vmem((tokens, 128), F32),
            vmem((micro, block, rows_m), F32),
            vmem((micro, lat_w, n_dp * rows_m), BF16),
            vmem((n_dp * block, lat_w), BF16),
            vmem((micro, n_dp, 2, rows_m, cols_d), BF16),
            vmem((micro, 2, n_dp * rows_m, cols_d), BF16),
            vmem((2, lat_w, cols_d), F32),
            vmem((2, lat_w, cols_d), F32),
            vmem((2, lat_w, cols_d), F32),
            vmem((2, lat_w, cols_d), BF16),
            vmem((2, n_dp, block, cols_d), BF16),
            vmem((tokens, width - span), BF16),
            dma((15,)),
            dma((n_chunks,)),
            dma((n_chunks,)),
            dma((n_chunks2,)),
            dma((n_chunks2,)),
            dma((n_chunks2,)),
            dma((2, 2 * n_y - 1 + n_dp // 2)),
            dma((2, n_dp)),
            dma((micro, 2, n_dp)),
            dma((micro, 2, n_dp)),
            dma((2, n_dp)),
            dma((2, n_dp)),
            dma((3, 2)),
        ],
        compiler_params=pltpu.CompilerParams(
            collective_id=0, has_side_effects=True, vmem_limit_bytes=LIMIT
        ),
    )(
        hidden_states[0], key_rows[0], value_rows[0], latents, next_latents, media_index, cotangent,
        gate_alpha, weights[0], moment_first[0], moment_second[0],
    )
    grad_in, new_w, kv = pl.pallas_call(
        store,
        out_shape=(
            jax.ShapeDtypeStruct((1, micro, block, width), BF16),
            jax.ShapeDtypeStruct((1, 2, lat_w, cols_d), F32),
            jax.ShapeDtypeStruct((1, 2, rows_m, span), BF16),
        ),
        in_specs=[vmem_spec] * 4,
        out_specs=(any_spec, any_spec, any_spec),
        scratch_shapes=[dma((2 + 2 * micro,))],
        compiler_params=pltpu.CompilerParams(vmem_limit_bytes=1024 * 1024),
    )(*held)
    return grad_in, new_w, kv


def solution(mesh):
    in_specs = (
        P("section", None, "dp", None),
        P("section", None, "dp", None),
        P("section", None, "dp", None),
        P(None, "dp", None),
        P("dp", None),
        P(None, "dp"),
        P(None, "dp", None),
        P("section"),
        P("section", None, None, "dp"),
        P("section", None, None, "dp"),
        P("section", None, None, "dp"),
    )
    out_specs = (
        P("section", None, "dp", None),
        P("section", None, None, "dp"),
        P("section", None, "dp", None),
    )
    return jax.shard_map(body, mesh=mesh, in_specs=in_specs, out_specs=out_specs, check_vma=False)
```
